32 devices in a mesh: gx: 16 (over z, y, core), gy: 2 (over x).
Axes of the slice: x: 2, y: 2, z: 4, core: 2. Of those that a mesh axis runs over, the one named last changes fastest.
Arguments:
- child_state: float32 [5, 32, 256, 256], P(None, None, 'gx', 'gy'), may hold values from -6 to 6
- cotangent: float32 [5, 32, 256, 256], P(None, None, 'gx', 'gy'), may hold values from -6 to 6
- diffusivity: float32 [32, 256, 256], P(None, 'gx', 'gy'), may hold values from 0.01 to 0.16
- field_mix: float32 [5, 5], replicated, may hold values from -2.5 to 2.5
- parent_we: float32 [2, 5, 128, 256], P(None, None, 'gx', 'gy'), may hold values from -6 to 6
- parent_sn: float32 [2, 5, 128, 256], P(None, None, 'gy', 'gx'), may hold values from -6 to 6
- terrain_we: int32 [2, 256], P(None, 'gy'), may hold values from 0 to 96, as said below
- terrain_sn: int32 [2, 256], P(None, 'gx'), may hold values from 0 to 96, as said below
- relax_width: int32 [1], replicated, may hold values from 4 to 15
Outputs:
- child_final: float32 [5, 32, 256, 256], P(None, None, 'gx', 'gy')
- grad_state: float32 [5, 32, 256, 256], P(None, None, 'gx', 'gy')
- grad_we: float32 [2, 5, 128, 256], P(None, None, 'gx', 'gy')
- grad_sn: float32 [2, 5, 128, 256], P(None, None, 'gy', 'gx')
The draws below stay inside these ranges and needn't reach their ends.
Inputs may be any that keep to these rules, and one draw needn't show every extreme that they name: `terrain_we`: on each edge some column has the largest value 128 - 32. `terrain_sn`: on each edge some column has the largest value 128 - 32.
All inputs are finite; a program needn't handle non-finite values.
Results may differ from the reference program's by a relative error of at most 0.000084.
Values sent between devices are 32-bit elements; how exact they have to be, the bound alone decides.
No kernel may reach another device: no remote copies, remote signals or barrier semaphores. Data moves between devices by JAX's collectives and lax.ppermute only.
A program may use at most 128 MiB of HBM per device.

```python
import math
import jax
import jax.numpy as jnp
from jax import lax

F = 5
KC = 32
KP = 128
CX = 16
NX = 256
NY = 256


def terrain_columns(key, count):
    first_key, second_key = jax.random.split(key)
    heights = jax.random.randint(first_key, (2, count), 0, KP - KC + 1, dtype=jnp.int32)
    chosen = jax.random.randint(second_key, (2,), 0, count, dtype=jnp.int32)
    column = jnp.arange(count, dtype=jnp.int32)
    return jnp.where(column[None, :] == chosen[:, None], KP - KC, heights).astype(jnp.int32)


def draw_terrain_we(key, part):
    key = jax.random.fold_in(key, 11)
    return terrain_columns(key, NY)


def draw_terrain_sn(key, part):
    key = jax.random.fold_in(key, 23)
    return terrain_columns(key, NX)


def block_scale(rng, shape, shards, low, high):
    factor_of = 1.0
    for axis_at, shards_of in shards:
        steps = jax.random.uniform(jax.random.fold_in(jax.random.fold_in(rng, 6), axis_at), (shards_of,), jnp.float32, low / len(shards), high / len(shards))
        factor_of = factor_of * jnp.repeat(jnp.exp(steps), shape[axis_at] // shards_of).reshape((-1,) + (1,) * (len(shape) - 1 - axis_at))
    return factor_of


def centred(stream_key, shape, width, reach, cuts=(), held_as=jnp.bfloat16):
    factor_of = block_scale(stream_key, shape, cuts, -0.22, 0.18) if cuts else 1.0
    entries = jax.random.normal(stream_key, shape, jnp.float32) * width * factor_of
    return jnp.minimum(jnp.maximum(entries, -reach), reach).astype(held_as)


def setup_inputs(seed: int = 0) -> dict:
    streams_of = jax.random.split(jax.random.key(seed), 10)
    return {
        "child_state": centred(streams_of[0], (F, KC, NX, NY), 1.0, 6.0, ((2, 16), (3, 2)), jnp.float32),
        "cotangent": centred(streams_of[1], (F, KC, NX, NY), 1.0, 6.0, ((2, 16), (3, 2)), jnp.float32),
        "diffusivity": jnp.clip(jnp.exp(math.log(0.16) - 2.7725887 * jax.random.uniform(streams_of[2], (KC, NX, NY), jnp.float32) ** block_scale(streams_of[2], (KC, NX, NY), ((1, 16), (2, 2)), -0.2, 0.2)), 0.01, 0.16),
        "field_mix": centred(streams_of[3], (F, F), F ** -0.5, 2.5, (), jnp.float32),
        "parent_we": centred(streams_of[4], (2, F, KP, NY), 1.0, 6.0, ((2, 16), (3, 2)), jnp.float32),
        "parent_sn": centred(streams_of[5], (2, F, KP, NX), 1.0, 6.0, ((2, 2), (3, 16)), jnp.float32),
        "terrain_we": draw_terrain_we(jax.random.fold_in(streams_of[9], 71), 0),
        "terrain_sn": draw_terrain_sn(jax.random.fold_in(streams_of[9], 71), 0),
        "relax_width": jax.random.randint(streams_of[8], (1,), 4, CX).astype(jnp.int32),
    }


near_weight = 4.0 / 3.0
far_weight = -1.0 / 12.0
coupling = 0.25
highest = lax.Precision.HIGHEST


def laplace(padded):
    centre_cell = padded[..., 2:-2, 2:-2]
    summed = near_weight * (padded[..., 3:-1, 2:-2] + padded[..., 1:-3, 2:-2] + padded[..., 2:-2, 3:-1] + padded[..., 2:-2, 1:-3])
    summed = summed + far_weight * (padded[..., 4:, 2:-2] + padded[..., :-4, 2:-2] + padded[..., 2:-2, 4:] + padded[..., 2:-2, :-4])
    return summed - 5.0 * centre_cell


def zone_ramp(position, length, zone_width):
    distance = jnp.minimum(position, length - 1 - position)
    return jnp.maximum(zone_width - distance, 0).astype(jnp.float32) / (zone_width + 1).astype(jnp.float32)


def level_weights(terrain, first_level, level_count, child_count):
    child_level = jnp.arange(child_count, dtype=jnp.int32)
    base_level = terrain[:, None, :] + child_level[None, :, None]
    parent = first_level + jnp.arange(level_count, dtype=jnp.int32)
    return (parent[None, None, :, None] == base_level[:, :, None, :]).astype(jnp.float32)


def reference(child_state, cotangent, diffusivity, field_mix, parent_we, parent_sn, terrain_we, terrain_sn, relax_width):
    zone_width = relax_width[0]
    position_x = jnp.arange(NX, dtype=jnp.int32)
    position_y = jnp.arange(NY, dtype=jnp.int32)
    ramp_x = zone_ramp(position_x, NX, zone_width)[:, None]
    ramp_y = zone_ramp(position_y, NY, zone_width)[None, :]
    west_side = (position_x < NX // 2)[:, None]
    south_side = (position_y < NY // 2)[None, :]
    weights_we = level_weights(terrain_we, 0, KP, KC)
    weights_sn = level_weights(terrain_sn, 0, KP, KC)
    bound_we = jnp.einsum("eflc,eklc->efkc", parent_we, weights_we, precision=highest)
    bound_sn = jnp.einsum("eflc,eklc->efkc", parent_sn, weights_sn, precision=highest)

    def per_level(level_items):
        fields_now, adjoint, conduct, edge_we, edge_sn = level_items
        edge_x = jnp.where(west_side[None], edge_we[0][:, None, :], edge_we[1][:, None, :])
        edge_y = jnp.where(south_side[None], edge_sn[0][:, :, None], edge_sn[1][:, :, None])

        def advance(values):
            padded = jnp.pad(values, ((0, 0), (2, 2), (2, 2)))
            stepped = values + conduct * laplace(padded) + coupling * jnp.einsum("fg,gxy->fxy", field_mix, values, precision=highest)
            across = (1.0 - ramp_x) * stepped + ramp_x * edge_x
            return (1.0 - ramp_y) * across + ramp_y * edge_y

        def retreat(incoming):
            pulled = (1.0 - ramp_y) * (1.0 - ramp_x) * incoming
            padded = jnp.pad(conduct * pulled, ((0, 0), (2, 2), (2, 2)))
            return pulled + laplace(padded) + coupling * jnp.einsum("gf,gxy->fxy", field_mix, pulled, precision=highest)

        final_fields = advance(advance(fields_now))
        middle = retreat(adjoint)
        earliest = retreat(middle)
        carried = adjoint + middle
        push_x = (1.0 - ramp_y) * ramp_x * carried
        push_y = ramp_y * carried
        d_we = jnp.stack([jnp.sum(jnp.where(west_side, push_x, 0.0), axis=1), jnp.sum(jnp.where(west_side, 0.0, push_x), axis=1)])
        d_sn = jnp.stack([jnp.sum(jnp.where(south_side, push_y, 0.0), axis=2), jnp.sum(jnp.where(south_side, 0.0, push_y), axis=2)])
        return final_fields, earliest, d_we, d_sn

    mapped = lax.map(per_level, (child_state.transpose(1, 0, 2, 3), cotangent.transpose(1, 0, 2, 3), diffusivity, bound_we.transpose(2, 0, 1, 3), bound_sn.transpose(2, 0, 1, 3)))
    child_final = mapped[0].transpose(1, 0, 2, 3)
    grad_state = mapped[1].transpose(1, 0, 2, 3)
    d_we = mapped[2].transpose(1, 2, 0, 3)
    d_sn = mapped[3].transpose(1, 2, 0, 3)
    grad_we = jnp.einsum("efkc,eklc->eflc", d_we, weights_we, precision=highest)
    grad_sn = jnp.einsum("efkc,eklc->eflc", d_sn, weights_sn, precision=highest)
    return (child_final, grad_state, grad_we, grad_sn)
```

```python
import functools

import jax
import jax.numpy as jnp
from jax import lax
from jax.experimental import pallas as pl
from jax.experimental.pallas import tpu as pltpu
from jax.sharding import PartitionSpec as P

near = 4.0 / 3.0
far = -1.0 / 12.0
coupling = 0.25
highest = lax.Precision.HIGHEST
f32 = jnp.float32
places = {
    "v": pl.BlockSpec(memory_space=pltpu.VMEM),
    "s": pl.BlockSpec(memory_space=pltpu.SMEM),
    "h": pl.BlockSpec(memory_space=pltpu.HBM),
    "a": pl.BlockSpec(memory_space=pl.ANY),
}
widest_zone = 15


class Geometry:
    def __init__(self, child, nx, ny):
        self.F, self.K, self.X, self.Y = child
        self.nx, self.ny = nx, ny
        self.tiles = self.K // 8
        assert self.K % 8 == 0 and self.Y == 128 and 4 * self.X <= 64
        assert self.X > widest_zone and self.Y > widest_zone
        assert self.X == 16
        assert nx >= 4 and nx & (nx - 1) == 0 and ny % 2 == 0
        assert 4 * self.F <= 128
        self.pair = ny == 2
        self.tall = self.K + self.X + 8


def lanes():
    return lax.broadcasted_iota(jnp.int32, (8, 128), 1)


def turn(values, shift):
    return pltpu.roll(values, shift % 128, values.ndim - 1)


def ramp(position, length, width):
    distance = jnp.minimum(position, length - 1 - position)
    inside = (position >= 0) & (position < length)
    top = jnp.where(inside, jnp.maximum(width - distance, 0), 0)
    bottom = jnp.full((8, 128), width + 1, jnp.int32)
    return jnp.broadcast_to(top, (8, 128)).astype(f32) / bottom.astype(f32)


def ramp_y(g, width):
    return ramp(lax.axis_index("gy") * g.Y + lanes(), g.ny * g.Y, width)


def ramp_x(g, width, x):
    return ramp(lax.axis_index("gx") * g.X + x, g.nx * g.X, width)


def fill_ramp_x(g, width, ref):
    for x in range(g.X):
        ref[x] = ramp_x(g, width, x)


def lap_masks():
    lane = lanes()
    zero = jnp.zeros((8, 128), f32)
    return (
        (1, jnp.where(lane > 0, near, zero)),
        (-1, jnp.where(lane < 127, near, zero)),
        (2, jnp.where(lane > 1, far, zero)),
        (-2, jnp.where(lane < 126, far, zero)),
    )


def lap_inside(cells, x):
    beside = {
        1: [turn(cells[x], 1), turn(cells[x], -1)],
        2: [turn(cells[x], 2), turn(cells[x], -2)],
    }
    for step in (1, 2):
        beside[step] += [cells[x + i] for i in (-step, step) if 0 <= x + i < len(cells)]
    total = near * functools.reduce(jnp.add, beside[1]) - 5.0 * cells[x]
    return total + far * functools.reduce(jnp.add, beside[2])


def pack_lanes(x, base, values, packed):
    lane = lanes()
    start = base + 4 * x
    return jnp.where((lane >= start) & (lane < start + 4), turn(values, start + 2), packed)


def packed_message(packed):
    spot = lanes() % 4
    zero = jnp.zeros((8, 128), f32)
    low = far * turn(packed, -2) + jnp.where(spot == 1, near * turn(packed, -1), zero)
    high = far * turn(packed, 2) + jnp.where(spot == 2, near * turn(packed, 1), zero)
    return jnp.where(spot < 2, low, high)


def valid_lanes(g):
    at = lax.axis_index("gy")
    spot = lanes() % 4
    low = (at < g.ny - 1).astype(f32)
    high = (at > 0).astype(f32)
    return jnp.where(spot < 2, low, high)


def border():
    lane = lanes()
    return jnp.where((lane < 2) | (lane >= 126), 1.0, 0.0).astype(f32)


def unpack_lanes(x, base, packed, edge):
    return edge * turn(packed, -(base + 4 * x + 2))


def strided(ref, g, f, tile, x):
    start = (f * g.K + tile * 8) * g.X + x
    return ref.at[pl.ds(start, 8, stride=g.X), :]


def mix_table(mix, transposed):
    count = mix.shape[0]
    return [
        [
            (mix[h, f] if transposed else mix[f, h]) * coupling + (1.0 if f == h else 0.0)
            for h in range(count)
        ]
        for f in range(count)
    ]


def mixed(table, f, values):
    total = table[f][0] * values[0]
    for h in range(1, len(values)):
        total = total + table[f][h] * values[h]
    return total


def column_of(row):
    count = row.shape[1]
    wide = jnp.broadcast_to(row.astype(f32), (count, count))
    a = lax.broadcasted_iota(jnp.int32, (count, count), 0)
    b = lax.broadcasted_iota(jnp.int32, (count, count), 1)
    picked = jnp.sum(jnp.where(a == b, wide, 0.0), axis=1, keepdims=True)
    return jnp.broadcast_to(picked, (count, 128)).astype(jnp.int32)


def shift_levels(values, shift, sign):
    step = 1
    while step < 128:
        values = jnp.where((shift & step) != 0, turn(values, sign * step), values)
        step *= 2
    return values


def level_copies(g, pairs, sems, tile):
    levels = pl.ds(pl.multiple_of(tile * 8, 8), 8)
    copies = []
    for i, (source, target) in enumerate(pairs):
        at = (levels,) if len(source.shape) == 3 else (slice(None), levels)
        copies.append(pltpu.make_async_copy(source.at[at], target.at[at], sems.at[i, tile]))
    return copies


def rows_of(tile):
    return pl.ds(pl.multiple_of(tile * 8, 8), 8)


def odd_column():
    return lax.axis_index("gx") % 2 == 1


def send_ends(g, s, source, rows, ma, mb):
    odd = odd_column()
    for f in range(g.F):
        for j in range(2):
            low, high = source(f, j), source(f, g.X - 2 + j)
            ma[s, j, f, rows, :] = jnp.where(odd, low, high)
            mb[s, j, f, rows, :] = jnp.where(odd, high, low)


class Beyond:
    def __init__(self, g, s, fa, fb, fy, own):
        self.g, self.s, self.fa, self.fb, self.fy, self.own = g, s, fa, fb, fy, own
        self.edge = border()
        self.valid = valid_lanes(g)
        here = lax.axis_index("gx")
        self.odd = here % 2 == 1
        self.first, self.last = here == 0, here == g.nx - 1

    def left(self, j, f, rows):
        at = (self.s, j, f, rows, slice(None))
        value = jnp.where(self.odd, self.fa[at], self.fb[at])
        return jnp.where(self.first, jnp.zeros_like(value), value)

    def right(self, j, f, rows):
        at = (self.s, j, f, rows, slice(None))
        value = jnp.where(self.odd, self.fb[at], self.fa[at])
        return jnp.where(self.last, jnp.zeros_like(value), value)

    def lanes_of(self, f, rows):
        return self.fy[f, rows, :] * self.valid - self.own[f, rows, :]

    def add(self, f, x, rows, packed):
        s, last = self.s, self.g.X - 1
        total = unpack_lanes(x, 64 * s, packed, self.edge)
        if x == 0:
            total = total + near * self.left(1, f, rows) + far * self.left(0, f, rows)
        if x == 1:
            total = total + far * self.left(1, f, rows)
        if x == last - 1:
            total = total + far * self.right(0, f, rows)
        if x == last:
            total = total + near * self.right(0, f, rows) + far * self.right(1, f, rows)
        return total


def lane_sums(vectors):
    lane = lanes()
    step = 1
    while len(vectors) > 1:
        low = (lane & step) == 0
        merged = []
        for a, b in zip(vectors[::2], vectors[1::2]):
            merged.append(jnp.where(low, a, b) + turn(jnp.where(low, b, a), step))
        vectors = merged
        step *= 2
    total = vectors[0]
    while step < 128:
        total = total + turn(total, step)
        step *= 2
    return total


def pack_kernel(
    g, relax, child_far, cot_far, diff_far, sn_far, parent_far, terrain_far,
    ut, at, dt, qt, ma, mb, my, rx, child, cot, diff, sn, parent, terrain, sems, side_sems,
):
    width = relax[0]
    pairs = ((diff_far, diff), (child_far, child), (cot_far, cot))
    for tile in range(g.tiles):
        for copy in level_copies(g, pairs, sems, tile):
            copy.start()
    side_copies = [
        pltpu.make_async_copy(source, target, side_sems.at[i])
        for i, (source, target) in enumerate(
            ((sn_far, sn), (parent_far, parent), (terrain_far, terrain))
        )
    ]
    for copy in side_copies:
        copy.start()
    fill_ramp_x(g, width, rx)
    open_y = 1.0 - ramp_y(g, width)
    child2 = child.reshape(g.F * g.K * g.X, g.Y)
    cot2 = cot.reshape(g.F * g.K * g.X, g.Y)
    diff2 = diff.reshape(g.K * g.X, g.Y)

    def tile_step(tile, carry):
        for copy in level_copies(g, pairs, sems, tile):
            copy.wait()
        rows = rows_of(tile)
        packed = [jnp.zeros((8, 128), f32) for _ in range(g.F)]
        for x in range(g.X):
            d = strided(diff2, g, 0, tile, x)[...]
            dt[x, rows, :] = d
            open_xy = open_y * (1.0 - rx[x])
            for f in range(g.F):
                u = strided(child2, g, f, tile, x)[...]
                a = strided(cot2, g, f, tile, x)[...]
                q = d * (open_xy * a)
                ut[f, x, rows, :] = u
                at[f, x, rows, :] = a
                qt[f, x, rows, :] = q
                packed[f] = pack_lanes(x, 0, u, packed[f])
                packed[f] = pack_lanes(x, 64, q, packed[f])
        for f in range(g.F):
            my[f, rows, :] = packed_message(packed[f])
        for s, source in enumerate((ut, qt)):
            send_ends(g, s, lambda f, x: source[f, x, rows, :], rows, ma, mb)
        return carry

    lax.fori_loop(0, g.tiles, tile_step, 0)
    for copy in side_copies:
        copy.wait()
    for f in range(g.F):
        my[f, g.K :, :] = jnp.zeros((g.X + 8, 128), f32)
    if g.pair:
        other = 1 - lax.axis_index("gy")
        for f in range(g.F):
            my[f, g.K : g.K + g.X, : sn.shape[3]] = sn[other, f]
    span = parent.shape[2]
    lane = lax.broadcasted_iota(jnp.int32, (span, 128), 1)
    for f in range(g.F):
        total = jnp.zeros((span, 128), f32)
        for e in range(2):
            heights = jnp.broadcast_to(terrain[e : e + 1, :].astype(f32), (span, 128))
            for spot, values in ((e, parent[e, f]), (2 + e, heights)):
                here = (lane >= 4 * spot) & (lane < 4 * spot + 4)
                total = jnp.where(here, turn(values, 4 * spot + 2), total)
        my[f, g.K + g.X : g.K + g.X + span, :] = total


def adjoint_inside_kernel(g, scaled, relax, mix, ps, qs, gate, out, rx):
    width = relax[0]
    table = mix_table(mix, True)
    if scaled:
        fill_ramp_x(g, width, rx)
        open_y = 1.0 - ramp_y(g, width)

    def tile_step(tile, carry):
        rows = rows_of(tile)
        for x in range(g.X):
            p = [ps[f, x, rows, :] for f in range(g.F)]
            if scaled:
                open_xy = open_y * (1.0 - rx[x])
                p = [open_xy * value for value in p]
            for f in range(g.F):
                near_cells = Column(qs, f, rows, g.X)
                out[f, x, rows, :] = mixed(table, f, p) + lap_inside(near_cells, x)
        return carry

    lax.fori_loop(0, g.tiles, tile_step, 0)


class Column:
    def __init__(self, ref, f, rows, count):
        self.ref, self.f, self.rows, self.count = ref, f, rows, count

    def __len__(self):
        return self.count

    def __getitem__(self, x):
        return self.ref[self.f, x, self.rows, :]


def forward_inside_kernel(g, mix, ut, dt, gate, out):
    table = mix_table(mix, False)

    def tile_step(tile, carry):
        rows = rows_of(tile)
        for x in range(g.X):
            u = [ut[f, x, rows, :] for f in range(g.F)]
            d = dt[x, rows, :]
            for f in range(g.F):
                lap = lap_inside(Column(ut, f, rows, g.X), x)
                out[f, x, rows, :] = mixed(table, f, u) + d * lap
        return carry

    lax.fori_loop(0, g.tiles, tile_step, 0)


def adjoint_first_kernel(
    g, relax, inside, at, dt, fa, fb, fy, own, gate, p1, q1, ma, mb, my, dwe, dsn, rx
):
    width = relax[0]
    fill_ramp_x(g, width, rx)
    slope_y = ramp_y(g, width)
    open_y = 1.0 - slope_y
    beyond = Beyond(g, 1, fa, fb, fy, own)

    def tile_step(tile, carry):
        rows = rows_of(tile)
        for f in range(g.F):
            halo = beyond.lanes_of(f, rows)
            packed = jnp.zeros((8, 128), f32)
            share = jnp.zeros((8, 128), f32)
            pushes = []
            for x in range(g.X):
                slope_x = rx[x]
                open_xy = open_y * (1.0 - slope_x)
                middle = inside[f, x, rows, :] + beyond.add(f, x, rows, halo)
                carried = at[f, x, rows, :] + middle
                share = share + slope_x * carried
                pushes.append(slope_y * carried)
                pulled = open_xy * middle
                q = dt[x, rows, :] * pulled
                p1[f, x, rows, :] = pulled
                q1[f, x, rows, :] = q
                packed = pack_lanes(x, 64, q, packed)
            my[f, rows, :] = packed_message(packed)
            dsn[f, rows, :] = lane_sums(pushes)
            dwe[f, rows, :] = open_y * share
        send_ends(g, 1, lambda f, x: q1[f, x, rows, :], rows, ma, mb)
        return carry

    lax.fori_loop(0, g.tiles, tile_step, 0)
    for f in range(g.F):
        my[f, g.K :, :] = jnp.zeros((g.X + 8, 128), f32)


def forward_first_kernel(
    g, relax, inside, dt, fa, fb, fy, own, sides, gate, ma_in, mb_in, my_in, u1, ma, mb, my, rx
):
    width = relax[0]
    fill_ramp_x(g, width, rx)
    open_y = 1.0 - ramp_y(g, width)
    beyond = Beyond(g, 0, fa, fb, fy, own)
    lane = lanes()

    def tile_step(tile, carry):
        rows = rows_of(tile)
        for f in range(g.F):
            halo = beyond.lanes_of(f, rows)
            packed = jnp.zeros((8, 128), f32)
            for x in range(g.X):
                open_xy = open_y * (1.0 - rx[x])
                stepped = inside[f, x, rows, :] + dt[x, rows, :] * beyond.add(f, x, rows, halo)
                done = open_xy * stepped + sides[f, x, rows, :]
                u1[f, x, rows, :] = done
                packed = pack_lanes(x, 0, done, packed)
            my[f, rows, :] = jnp.where(lane < 64, packed_message(packed), my_in[f, rows, :])
        send_ends(g, 0, lambda f, x: u1[f, x, rows, :], rows, ma, mb)
        return carry

    lax.fori_loop(0, g.tiles, tile_step, 0)


def adjoint_last_kernel(g, inside, fa, fb, fy, own, gsn_own, gate, out, gsn):
    out2 = out.reshape(g.F * g.K * g.X, g.Y)
    beyond = Beyond(g, 1, fa, fb, fy, own)

    def tile_step(tile, carry):
        rows = rows_of(tile)
        for f in range(g.F):
            halo = beyond.lanes_of(f, rows)
            for x in range(g.X):
                value = inside[f, x, rows, :] + beyond.add(f, x, rows, halo)
                strided(out2, g, f, tile, x)[...] = value
        return carry

    lax.fori_loop(0, g.tiles, tile_step, 0)
    if g.pair:
        here = lax.axis_index("gy")
        span = gsn.shape[3]
        for f in range(g.F):
            gsn[here, f] = gsn_own[f, :, :span]
            gsn[1 - here, f] = fy[f, g.K : g.K + g.X, :span]
    else:
        gsn[...] = jnp.zeros(gsn.shape, f32)


def forward_last_kernel(
    g, relax, mix, inside, dt, fa, fb, fy, own, sides, kept, swapped, out, rx, lx
):
    width = relax[0]
    for x in range(-2, g.X + 2):
        rx[x + 2] = ramp_x(g, width, x)
    for x in range(g.X):
        lap_x = near * (rx[x + 1] + rx[x + 3]) + far * (rx[x] + rx[x + 4]) - 5.0 * rx[x + 2]
        lx[x] = lap_x
    open_y = 1.0 - ramp_y(g, width)
    masks = lap_masks()
    table = mix_table(mix, False)
    beyond = Beyond(g, 0, fa, fb, fy, own)
    out2 = out.reshape(g.F * g.K * g.X, g.Y)

    def tile_step(tile, carry):
        rows = rows_of(tile)
        bound = [
            open_y * (kept[g.F + f, rows, :] + swapped[g.F + f, rows, :]) for f in range(g.F)
        ]
        past = packed_message(kept[2 * g.F, rows, :] + swapped[2 * g.F, rows, :]) * beyond.valid
        for f in range(g.F):
            lap_y = unpack_lanes(f, 0, past, beyond.edge)
            for shift, mask in masks:
                lap_y = lap_y + mask * turn(bound[f], shift)
            mixed_bound = mixed(table, f, bound)
            halo = beyond.lanes_of(f, rows)
            for x in range(g.X):
                slope_x = rx[x + 2]
                open_xy = open_y * (1.0 - slope_x)
                lap = beyond.add(f, x, rows, halo) + slope_x * lap_y + lx[x] * bound[f]
                stepped = inside[f, x, rows, :] + slope_x * mixed_bound + dt[x, rows, :] * lap
                done = open_xy * stepped + slope_x * bound[f] + sides[f, x, rows, :]
                strided(out2, g, f, tile, x)[...] = done
        return carry

    lax.fori_loop(0, g.tiles, tile_step, 0)


def side_sums_kernel(g, dsn, tsn, my_in, gsn, my, wide):
    here = lax.axis_index("gy")
    shift = column_of(jnp.where(here == 0, tsn[0:1, :], tsn[1:2, :]))
    wide[...] = jnp.zeros(wide.shape, f32)
    for f in range(g.F):
        wide[f, : g.K, :] = dsn[f]
        whole = shift_levels(wide[f].T[: g.X], shift, 1)
        moved = turn(whole, 64)
        gsn[f] = jnp.where(here == 0, whole, moved)
        my[f, g.K : g.K + g.X, :] = jnp.where(here == 0, moved, whole)


def side_bounds_kernel(g, sn, fsn, tsn, gate, bsn, wide):
    here = lax.axis_index("gy")
    shift = column_of(jnp.where(here == 0, tsn[0:1, :], tsn[1:2, :]))
    span = sn.shape[3]
    wide[...] = jnp.zeros(wide.shape, f32)
    for f in range(g.F):
        wide[f, : g.X, :span] = sn[here, f]
        mine = wide[f, : g.X, :]
        theirs = fsn[f, g.K : g.K + g.X, :]
        whole = jnp.where(here == 0, mine, theirs) + turn(
            jnp.where(here == 0, theirs, mine), 64
        )
        wide[f, : g.X, :] = shift_levels(whole, shift, -1)
        bsn[f] = wide[f].T[: g.K]


def side_spread_kernel(g, relax, bsn, out):
    slope_y = ramp_y(g, relax[0])

    def tile_step(tile, carry):
        rows = rows_of(tile)
        for f in range(g.F):
            bounds = bsn[f, rows, :]
            for x in range(g.X):
                out[f, x, rows, :] = slope_y * jnp.broadcast_to(bounds[:, x : x + 1], (8, 128))
        return carry

    lax.fori_loop(0, g.tiles, tile_step, 0)


def fold_rows(values, base, first, count):
    level = lax.broadcasted_iota(jnp.int32, (count, 128), 0) + base - first
    total = jnp.zeros((count, 128), f32)
    for j in range(values.shape[0]):
        row = jnp.broadcast_to(values[j : j + 1, :], (count, 128))
        total = jnp.where(level == j, row, total)
    return total


def fold_kernel(g, parent, terrain, fy, keep, send):
    here = lax.axis_index("gx")
    odd = here >= g.nx // 2
    span = parent.shape[2]
    first = here * span
    lane = lax.broadcasted_iota(jnp.int32, (span, 128), 1)
    top = g.K + g.X
    parts = []
    for e in range(2):
        part = [fold_rows(parent[e, f], terrain[e : e + 1, :], first, g.K) for f in range(g.F)]
        values = jnp.zeros((span, 128), f32)
        heights = jnp.zeros((span, 128), f32)
        for f in range(g.F):
            spots = (lane >= 4 * f) & (lane < 4 * f + 4)
            rows = fy[f, top : top + span, :]
            values = jnp.where(spots, turn(rows, 4 * f - 4 * e), values)
            heights = jnp.where(spots, turn(rows, 4 * f - 8 - 4 * e), heights)
        part.append(fold_rows(values, heights[0:1, :].astype(jnp.int32), first, g.K))
        parts.append(part)
    for i in range(g.F + 1):
        keep[i] = jnp.where(odd, parts[1][i], parts[0][i])
        send[i] = jnp.where(odd, parts[0][i], parts[1][i])


def join_kernel(g, sums, bounds, more_bounds, out):
    for f in range(g.F):
        out[f] = sums[f]
    for f in range(g.F + 1):
        out[g.F + f] = bounds[f] + more_bounds[f]


def split_kernel(g, state, moved, out, sums):
    for f in range(2 * g.F + 1):
        total = state[f] + moved[f]
        out[f] = total
        if f < g.F:
            sums[f] = total


def finish_kernel(g, state, moved, out):
    for f in range(g.F):
        out[f] = state[f] + moved[f]
    for f in range(g.F, 2 * g.F + 1):
        out[f] = state[f]


def spread_kernel(g, kept, swapped, terrain, out):
    here = lax.axis_index("gx")
    odd = here % 2
    span = out.shape[2]
    for e in range(2):
        place = lax.broadcasted_iota(jnp.int32, (span, 128), 0) + here * span - terrain[e : e + 1, :]
        keep = [place == k for k in range(g.K)]
        for f in range(g.F):
            a, b = kept[f], swapped[f]
            chosen = jnp.where(odd == e, a, b)
            total = jnp.zeros((span, 128), f32)
            for k in range(g.K):
                row = jnp.broadcast_to(chosen[k : k + 1, :], (span, 128))
                total = jnp.where(keep[k], row, total)
            out[e, f] = total


def call(kernel, outs, scratch, ins, time, aliases=None):
    out_shape = [jax.ShapeDtypeStruct(s, f32) for s in outs]
    size = 4 * sum(functools.reduce(lambda a, b: a * b, s) for s in outs)
    return pl.pallas_call(
        kernel,
        out_shape=out_shape,
        in_specs=[places[where] for where, _ in ins],
        out_specs=[places["v"]] * len(outs),
        scratch_shapes=[pltpu.VMEM(s, f32) if isinstance(s, tuple) else s for s in scratch],
        input_output_aliases=aliases or {},
        compiler_params=pltpu.CompilerParams(vmem_limit_bytes=24 * 1024 * 1024),
        cost_estimate=pl.CostEstimate(flops=int(time * 1.1e9), bytes_accessed=2 * size, transcendentals=0),
    )(*[pltpu.with_memory_space_constraint(v, pltpu.HBM) if w == "h" else v for w, v in ins])


def body(
    child_state,
    cotangent,
    diffusivity,
    field_mix,
    parent_we,
    parent_sn,
    terrain_we,
    terrain_sn,
    relax_width,
):
    nx, ny = lax.axis_size("gx"), lax.axis_size("gy")
    g = Geometry(child_state.shape, nx, ny)
    F, K, X, Y = child_state.shape
    evens = [(i, i ^ 1) for i in range(nx)]
    odds = [(i, (((i + 1) ^ 1) - 1) % nx) for i in range(nx)]
    block = (F, X, K, 128)
    row_shape = (2, 2, F, K, 128)
    lane_shape = (F, g.tall, 128)
    edge_shape = (F, K, 128)
    ramps = (X, 8, 128)

    def bind(kernel, *args):
        return functools.partial(kernel, g, *args)

    def swapped(values, distance):
        return lax.ppermute(values, "gx", [(i, i ^ distance) for i in range(nx)])

    def to_y(message):
        if g.pair:
            return lax.ppermute(message, "gy", [(0, 1), (1, 0)])
        up = lax.ppermute(message, "gy", [(i, i + 1) for i in range(ny - 1)])
        down = lax.ppermute(message, "gy", [(i + 1, i) for i in range(ny - 1)])
        low = (jnp.arange(128, dtype=jnp.int32) % 4 < 2)[None, None, :]
        rows = (jnp.arange(g.tall, dtype=jnp.int32) < K)[None, :, None]
        return jnp.where(low == rows, down, up)

    sn_turned = jnp.swapaxes(parent_sn, 2, 3)
    ut, at, dt, qt, ma, mb, my = call(
        bind(pack_kernel),
        [block, block, (X, K, 128), block, row_shape, row_shape, lane_shape],
        [
            ramps,
            child_state.shape,
            child_state.shape,
            diffusivity.shape,
            sn_turned.shape,
            parent_we.shape,
            pltpu.VMEM(terrain_we.shape, jnp.int32),
            pltpu.SemaphoreType.DMA((3, g.tiles)),
            pltpu.SemaphoreType.DMA((3,)),
        ],
        [
            ("s", relax_width),
            ("h", child_state),
            ("h", cotangent),
            ("h", diffusivity),
            ("h", sn_turned),
            ("h", parent_we),
            ("h", terrain_we),
        ],
        3,
    )
    own = my
    fy = to_y(my)
    fa = lax.ppermute(ma, "gx", evens)
    fb = lax.ppermute(mb, "gx", odds)

    (inside_a,) = call(
        bind(adjoint_inside_kernel, True),
        [block],
        [ramps],
        [("s", relax_width), ("s", field_mix), ("v", at), ("v", qt), ("a", dt)],
        2.5,
    )
    (inside_u,) = call(
        bind(forward_inside_kernel),
        [block],
        [],
        [("s", field_mix), ("v", ut), ("v", dt), ("a", inside_a)],
        2.5,
    )
    keep, send = call(
        bind(fold_kernel),
        [(F + 1, K, 128)] * 2,
        [],
        [("v", parent_we), ("v", terrain_we), ("v", fy)],
        0.3,
    )
    first_bounds = swapped(send, nx // 2)
    p1, q1, ma, mb, my, dwe, dsn = call(
        bind(adjoint_first_kernel),
        [block, block, row_shape, row_shape, lane_shape, edge_shape, edge_shape],
        [ramps],
        [
            ("s", relax_width),
            ("v", inside_a),
            ("v", at),
            ("v", dt),
            ("v", fa),
            ("v", fb),
            ("v", fy),
            ("v", own),
            ("a", keep),
        ],
        3,
    )
    if g.pair:
        (bsn,) = call(
            bind(side_bounds_kernel),
            [edge_shape],
            [(F, 128, 128)],
            [("v", sn_turned), ("v", fy), ("v", terrain_sn), ("a", dwe)],
            0.7,
        )
    else:
        bsn = bound_sn_general(g, parent_sn, terrain_sn)
    (sides,) = call(
        bind(side_spread_kernel), [block], [], [("s", relax_width), ("v", bsn)], 0.7
    )
    state_shape = (2 * F + 1, K, 128)
    (state,) = call(
        bind(join_kernel),
        [state_shape],
        [],
        [("v", dwe), ("v", keep), ("v", first_bounds)],
        0.1,
    )
    gates = []
    distance = 2
    while distance < nx // 4:
        state = state + swapped(state, distance)
        gates.append(state)
        distance *= 2
    moved = swapped(state, distance) if distance < nx // 2 else jnp.zeros_like(state)
    state, sums = call(
        bind(split_kernel), [state_shape, edge_shape], [], [("v", state), ("v", moved)], 0.1
    )
    gates.append(state)
    (state,) = call(
        bind(finish_kernel), [state_shape], [], [("v", state), ("v", swapped(sums, nx // 2))], 0.1
    )
    other = swapped(state, 1)

    if g.pair:
        gsn_own, my = call(
            bind(side_sums_kernel),
            [(F, X, 128), lane_shape],
            [(F, 128, 128)],
            [("v", dsn), ("v", terrain_sn), ("v", my)],
            0.6,
            {2: 1},
        )
    else:
        gsn_own = dsn
    u1, ma, mb, my = call(
        bind(forward_first_kernel),
        [block, row_shape, row_shape, lane_shape],
        [ramps],
        [
            ("s", relax_width),
            ("v", inside_u),
            ("v", dt),
            ("v", fa),
            ("v", fb),
            ("v", fy),
            ("v", own),
            ("v", sides),
            ("a", gates[0]),
            ("v", ma),
            ("v", mb),
            ("v", my),
        ],
        2.5,
        {9: 1, 10: 2, 11: 3},
    )
    own = my
    fy = to_y(my)
    fa = lax.ppermute(ma, "gx", evens)
    fb = lax.ppermute(mb, "gx", odds)

    (inside_a,) = call(
        bind(adjoint_inside_kernel, False),
        [block],
        [ramps],
        [("s", relax_width), ("s", field_mix), ("v", p1), ("v", q1), ("a", gates[-1])],
        2.5,
    )
    (inside_u,) = call(
        bind(forward_inside_kernel),
        [block],
        [],
        [("s", field_mix), ("v", u1), ("v", dt), ("a", u1)],
        2.5,
    )
    grad_state, grad_sn = call(
        bind(adjoint_last_kernel),
        [child_state.shape, sn_turned.shape],
        [],
        [("v", inside_a), ("v", fa), ("v", fb), ("v", fy), ("v", own), ("v", gsn_own), ("a", state)],
        2.5,
    )
    (child_final,) = call(
        bind(forward_last_kernel),
        [child_state.shape],
        [(X + 4, 8, 128), ramps],
        [
            ("s", relax_width),
            ("s", field_mix),
            ("v", inside_u),
            ("v", dt),
            ("v", fa),
            ("v", fb),
            ("v", fy),
            ("v", own),
            ("v", sides),
            ("v", state),
            ("v", other),
        ],
        3,
    )
    (grad_we,) = call(
        bind(spread_kernel),
        [parent_we.shape],
        [],
        [("v", state), ("v", other), ("v", terrain_we)],
        0.7,
    )
    if g.pair:
        grad_sn = jnp.swapaxes(grad_sn, 2, 3)
    else:
        grad_sn = grad_sn_general(g, gsn_own, terrain_sn, parent_sn.shape[2])
    return (child_final, grad_state, grad_we, grad_sn)


def level_weights(g, terrain, span):
    first = lax.axis_index("gy") * span
    base = terrain[:, None, :] + jnp.arange(g.K, dtype=jnp.int32)[None, :, None]
    parent = first + jnp.arange(span, dtype=jnp.int32)
    return (parent[None, None, :, None] == base[:, :, None, :]).astype(f32)


def bound_sn_general(g, parent_sn, terrain_sn):
    weights = level_weights(g, terrain_sn, parent_sn.shape[2])
    bound = jnp.einsum("eflc,eklc->efkc", parent_sn, weights, precision=highest)
    bound = lax.psum(bound, "gy")
    mine = jnp.where(lax.axis_index("gy") < g.ny // 2, bound[0], bound[1])
    return jnp.pad(mine, ((0, 0), (0, 0), (0, 128 - g.X)))


def grad_sn_general(g, sums, terrain_sn, span):
    sums = sums[:, :, : g.X]
    south = lax.axis_index("gy") < g.ny // 2
    zero = jnp.zeros_like(sums)
    both = jnp.stack([jnp.where(south, sums, zero), jnp.where(south, zero, sums)])
    both = lax.psum(both, "gy")
    weights = level_weights(g, terrain_sn, span)
    return jnp.einsum("efkc,eklc->eflc", both, weights, precision=highest)


def solution(mesh):
    return jax.shard_map(
        body,
        mesh=mesh,
        in_specs=(
            P(None, None, "gx", "gy"),
            P(None, None, "gx", "gy"),
            P(None, "gx", "gy"),
            P(),
            P(None, None, "gx", "gy"),
            P(None, None, "gy", "gx"),
            P(None, "gy"),
            P(None, "gx"),
            P(),
        ),
        out_specs=(
            P(None, None, "gx", "gy"),
            P(None, None, "gx", "gy"),
            P(None, None, "gx", "gy"),
            P(None, None, "gy", "gx"),
        ),
        check_vma=False,
    )
```

```python
import functools

import jax
import jax.numpy as jnp
from jax import lax
from jax.experimental import pallas as pl
from jax.experimental.pallas import tpu as pltpu
from jax.sharding import PartitionSpec as P

near = 4.0 / 3.0
far = -1.0 / 12.0
coupling = 0.25
highest = lax.Precision.HIGHEST
f32 = jnp.float32
places = {
    "v": pl.BlockSpec(memory_space=pltpu.VMEM),
    "s": pl.BlockSpec(memory_space=pltpu.SMEM),
    "h": pl.BlockSpec(memory_space=pltpu.HBM),
    "a": pl.BlockSpec(memory_space=pl.ANY),
}
widest_zone = 15


class Geometry:
    def __init__(self, child, nx, ny):
        self.F, self.K, self.X, self.Y = child
        self.nx, self.ny = nx, ny
        self.tiles = self.K // 8
        assert self.K % 8 == 0 and self.Y == 128 and 4 * self.X <= 64
        assert self.X > widest_zone and self.Y > widest_zone
        assert self.X == 16
        assert nx >= 16 and nx & (nx - 1) == 0 and ny % 2 == 0
        assert 4 * self.F <= 128 and 128 % self.K == 0
        self.pair = ny == 2
        self.tall = self.K + self.X + 8


def lanes():
    return lax.broadcasted_iota(jnp.int32, (8, 128), 1)


def turn(values, shift):
    return pltpu.roll(values, shift % 128, values.ndim - 1)


def ramp(position, length, width):
    distance = jnp.minimum(position, length - 1 - position)
    inside = (position >= 0) & (position < length)
    top = jnp.where(inside, jnp.maximum(width - distance, 0), 0)
    bottom = jnp.full((8, 128), width + 1, jnp.int32)
    return jnp.broadcast_to(top, (8, 128)).astype(f32) / bottom.astype(f32)


def ramp_y(g, width):
    return ramp(lax.axis_index("gy") * g.Y + lanes(), g.ny * g.Y, width)


def ramp_x(g, width, x):
    return ramp(lax.axis_index("gx") * g.X + x, g.nx * g.X, width)


def fill_ramp_x(g, width, ref):
    for x in range(g.X):
        ref[x] = ramp_x(g, width, x)


def lap_masks():
    lane = lanes()
    zero = jnp.zeros((8, 128), f32)
    return (
        (1, jnp.where(lane > 0, near, zero)),
        (-1, jnp.where(lane < 127, near, zero)),
        (2, jnp.where(lane > 1, far, zero)),
        (-2, jnp.where(lane < 126, far, zero)),
    )


def fill_band(band):
    shape = (2 * 128, 128)
    row = lax.broadcasted_iota(jnp.int32, shape, 0) % 128
    gap = jnp.abs(row - lax.broadcasted_iota(jnp.int32, shape, 1))
    entry = jnp.where(gap == 0, -60.0, jnp.where(gap == 1, 16.0, jnp.where(gap == 2, -1.0, 0.0)))
    band[...] = entry.astype(jnp.bfloat16)


def along_lanes(values, band):
    high = values.astype(jnp.bfloat16)
    low = (values - high.astype(f32)).astype(jnp.bfloat16)
    return jnp.dot(
        jnp.concatenate([high, low], axis=1), band[...], preferred_element_type=f32
    )


def lap_inside(cells, lane_part, x):
    count = len(cells)
    ones = [cells[x + i] for i in (-1, 1) if 0 <= x + i < count]
    twos = [cells[x + i] for i in (-2, 2) if 0 <= x + i < count]
    total = lane_part + 16.0 * functools.reduce(jnp.add, ones) - functools.reduce(jnp.add, twos)
    return total * (1.0 / 12.0)


def pack_lanes(x, base, values, packed):
    lane = lanes()
    start = base + 4 * x
    return jnp.where((lane >= start) & (lane < start + 4), turn(values, start + 2), packed)


def packed_message(packed):
    spot = lanes() % 4
    zero = jnp.zeros((8, 128), f32)
    low = far * turn(packed, -2) + jnp.where(spot == 1, near * turn(packed, -1), zero)
    high = far * turn(packed, 2) + jnp.where(spot == 2, near * turn(packed, 1), zero)
    return jnp.where(spot < 2, low, high)


def valid_lanes(g):
    at = lax.axis_index("gy")
    spot = lanes() % 4
    low = (at < g.ny - 1).astype(f32)
    high = (at > 0).astype(f32)
    return jnp.where(spot < 2, low, high)


def border():
    lane = lanes()
    return jnp.where((lane < 2) | (lane >= 126), 1.0, 0.0).astype(f32)


def unpack_lanes(x, base, packed, edge):
    return edge * turn(packed, -(base + 4 * x + 2))


def strided(ref, g, f, tile, x):
    start = (f * g.K + tile * 8) * g.X + x
    return ref.at[pl.ds(start, 8, stride=g.X), :]


def mix_table(mix, transposed):
    count = mix.shape[0]
    return [
        [
            (mix[h, f] if transposed else mix[f, h]) * coupling + (1.0 if f == h else 0.0)
            for h in range(count)
        ]
        for f in range(count)
    ]


def mixed(table, f, values):
    total = table[f][0] * values[0]
    for h in range(1, len(values)):
        total = total + table[f][h] * values[h]
    return total


def column_of(row):
    count = row.shape[1]
    wide = jnp.broadcast_to(row.astype(f32), (count, count))
    a = lax.broadcasted_iota(jnp.int32, (count, count), 0)
    b = lax.broadcasted_iota(jnp.int32, (count, count), 1)
    picked = jnp.sum(jnp.where(a == b, wide, 0.0), axis=1, keepdims=True)
    return jnp.broadcast_to(picked, (count, 128)).astype(jnp.int32)


def shift_levels(values, shift, sign):
    step = 1
    while step < 128:
        values = jnp.where((shift & step) != 0, turn(values, sign * step), values)
        step *= 2
    return values


def level_copies(g, pairs, sems, tile):
    levels = pl.ds(pl.multiple_of(tile * 8, 8), 8)
    copies = []
    for i, (source, target) in enumerate(pairs):
        at = (levels,) if len(source.shape) == 3 else (slice(None), levels)
        copies.append(pltpu.make_async_copy(source.at[at], target.at[at], sems.at[i, tile]))
    return copies


def rows_of(tile):
    return pl.ds(pl.multiple_of(tile * 8, 8), 8)


def odd_column():
    return lax.axis_index("gx") % 2 == 1


def send_ends(g, s, source, rows, ma, mb):
    odd = odd_column()
    for f in range(g.F):
        for j in range(2):
            low, high = source(f, j), source(f, g.X - 2 + j)
            ma[s, j, f, rows, :] = jnp.where(odd, low, high)
            mb[s, j, f, rows, :] = jnp.where(odd, high, low)


class Beyond:
    def __init__(self, g, s, fa, fb, fy):
        self.g, self.s, self.fa, self.fb, self.fy = g, s, fa, fb, fy
        self.edge = border()
        self.valid = valid_lanes(g)
        here = lax.axis_index("gx")
        self.odd = here % 2 == 1
        self.first, self.last = here == 0, here == g.nx - 1

    def left(self, j, f, rows):
        at = (self.s, j, f, rows, slice(None))
        value = jnp.where(self.odd, self.fa[at], self.fb[at])
        return jnp.where(self.first, jnp.zeros_like(value), value)

    def right(self, j, f, rows):
        at = (self.s, j, f, rows, slice(None))
        value = jnp.where(self.odd, self.fb[at], self.fa[at])
        return jnp.where(self.last, jnp.zeros_like(value), value)

    def lanes_of(self, f, rows):
        return self.fy[f, rows, :] * self.valid

    def add(self, f, x, rows, packed):
        s, last = self.s, self.g.X - 1
        total = unpack_lanes(x, 64 * s, packed, self.edge)
        if x == 0:
            total = total + near * self.left(1, f, rows) + far * self.left(0, f, rows)
        if x == 1:
            total = total + far * self.left(1, f, rows)
        if x == last - 1:
            total = total + far * self.right(0, f, rows)
        if x == last:
            total = total + near * self.right(0, f, rows) + far * self.right(1, f, rows)
        return total


def lane_sums(vectors):
    lane = lanes()
    step = 1
    while len(vectors) > 1:
        low = (lane & step) == 0
        merged = []
        for a, b in zip(vectors[::2], vectors[1::2]):
            merged.append(jnp.where(low, a, b) + turn(jnp.where(low, b, a), step))
        vectors = merged
        step *= 2
    total = vectors[0]
    while step < 128:
        total = total + turn(total, step)
        step *= 2
    return total


def pack_kernel(
    g, relax, child_far, cot_far, diff_far, sn_far, parent_far, terrain_far,
    ut, at, dt, qt, ma, mb, my, rx, child, cot, diff, sn, parent, terrain, sems, side_sems,
):
    width = relax[0]
    pairs = ((diff_far, diff), (child_far, child), (cot_far, cot))
    for tile in range(g.tiles):
        for copy in level_copies(g, pairs, sems, tile):
            copy.start()
    side_copies = [
        pltpu.make_async_copy(source, target, side_sems.at[i])
        for i, (source, target) in enumerate(
            ((sn_far, sn), (parent_far, parent), (terrain_far, terrain))
        )
    ]
    for copy in side_copies:
        copy.start()
    fill_ramp_x(g, width, rx)
    open_y = 1.0 - ramp_y(g, width)
    child2 = child.reshape(g.F * g.K * g.X, g.Y)
    cot2 = cot.reshape(g.F * g.K * g.X, g.Y)
    diff2 = diff.reshape(g.K * g.X, g.Y)

    def tile_step(tile, carry):
        for copy in level_copies(g, pairs, sems, tile):
            copy.wait()
        rows = rows_of(tile)
        packed = [jnp.zeros((8, 128), f32) for _ in range(g.F)]
        for x in range(g.X):
            d = strided(diff2, g, 0, tile, x)[...]
            dt[x, rows, :] = d
            open_xy = open_y * (1.0 - rx[x])
            for f in range(g.F):
                u = strided(child2, g, f, tile, x)[...]
                a = strided(cot2, g, f, tile, x)[...]
                q = d * (open_xy * a)
                ut[f, x, rows, :] = u
                at[f, x, rows, :] = a
                qt[f, x, rows, :] = q
                packed[f] = pack_lanes(x, 0, u, packed[f])
                packed[f] = pack_lanes(x, 64, q, packed[f])
        for f in range(g.F):
            my[f, rows, :] = packed_message(packed[f])
        for s, source in enumerate((ut, qt)):
            send_ends(g, s, lambda f, x: source[f, x, rows, :], rows, ma, mb)
        return carry

    lax.fori_loop(0, g.tiles, tile_step, 0)
    for copy in side_copies:
        copy.wait()
    for f in range(g.F):
        my[f, g.K :, :] = jnp.zeros((g.X + 8, 128), f32)
    if g.pair:
        other = 1 - lax.axis_index("gy")
        for f in range(g.F):
            my[f, g.K : g.K + g.X, : sn.shape[3]] = sn[other, f]
    span = parent.shape[2]
    lane = lax.broadcasted_iota(jnp.int32, (span, 128), 1)
    for f in range(g.F):
        total = jnp.zeros((span, 128), f32)
        for e in range(2):
            heights = jnp.broadcast_to(terrain[e : e + 1, :].astype(f32), (span, 128))
            for spot, values in ((e, parent[e, f]), (2 + e, heights)):
                here = (lane >= 4 * spot) & (lane < 4 * spot + 4)
                total = jnp.where(here, turn(values, 4 * spot + 2), total)
        my[f, g.K + g.X : g.K + g.X + span, :] = total


class Column:
    def __init__(self, ref, f, rows, count):
        self.ref, self.f, self.rows, self.count = ref, f, rows, count

    def __len__(self):
        return self.count

    def __getitem__(self, x):
        return self.ref[self.f, x, self.rows, :]


def lane_parts(g, source, rows, band, parts):
    for f in range(g.F):
        parts[f] = along_lanes(source[f, :, rows, :].reshape(8 * g.X, 128), band)


def adjoint_inside_kernel(g, scaled, relax, mix, ps, qs, out, rx, band, parts):
    width = relax[0]
    table = mix_table(mix, True)
    fill_band(band)
    if scaled:
        fill_ramp_x(g, width, rx)
        open_y = 1.0 - ramp_y(g, width)

    def tile_step(tile, carry):
        rows = rows_of(tile)
        lane_parts(g, qs, rows, band, parts)
        for x in range(g.X):
            p = [ps[f, x, rows, :] for f in range(g.F)]
            if scaled:
                open_xy = open_y * (1.0 - rx[x])
                p = [open_xy * value for value in p]
            for f in range(g.F):
                lap = lap_inside(Column(qs, f, rows, g.X), parts[f, 8 * x : 8 * x + 8, :], x)
                out[f, x, rows, :] = mixed(table, f, p) + lap
        return carry

    lax.fori_loop(0, g.tiles, tile_step, 0)


def forward_inside_kernel(g, mix, ut, dt, out, band, parts):
    table = mix_table(mix, False)
    fill_band(band)

    def tile_step(tile, carry):
        rows = rows_of(tile)
        lane_parts(g, ut, rows, band, parts)
        for x in range(g.X):
            u = [ut[f, x, rows, :] for f in range(g.F)]
            d = dt[x, rows, :]
            for f in range(g.F):
                lap = lap_inside(Column(ut, f, rows, g.X), parts[f, 8 * x : 8 * x + 8, :], x)
                out[f, x, rows, :] = mixed(table, f, u) + d * lap
        return carry

    lax.fori_loop(0, g.tiles, tile_step, 0)


def adjoint_first_kernel(
    g, relax, inside, at, dt, fa, fb, fy, p1, q1, ma, mb, my, dwe, dsn, rx
):
    width = relax[0]
    fill_ramp_x(g, width, rx)
    slope_y = ramp_y(g, width)
    open_y = 1.0 - slope_y
    beyond = Beyond(g, 1, fa, fb, fy)

    def tile_step(tile, carry):
        rows = rows_of(tile)
        for f in range(g.F):
            halo = beyond.lanes_of(f, rows)
            packed = jnp.zeros((8, 128), f32)
            share = jnp.zeros((8, 128), f32)
            pushes = []
            for x in range(g.X):
                slope_x = rx[x]
                open_xy = open_y * (1.0 - slope_x)
                middle = inside[f, x, rows, :] + beyond.add(f, x, rows, halo)
                carried = at[f, x, rows, :] + middle
                share = share + slope_x * carried
                pushes.append(slope_y * carried)
                pulled = open_xy * middle
                q = dt[x, rows, :] * pulled
                p1[f, x, rows, :] = pulled
                q1[f, x, rows, :] = q
                packed = pack_lanes(x, 64, q, packed)
            my[f, rows, :] = packed_message(packed)
            dsn[f, rows, :] = lane_sums(pushes)
            dwe[f, rows, :] = open_y * share
        send_ends(g, 1, lambda f, x: q1[f, x, rows, :], rows, ma, mb)
        return carry

    lax.fori_loop(0, g.tiles, tile_step, 0)
    for f in range(g.F):
        my[f, g.K :, :] = jnp.zeros((g.X + 8, 128), f32)


def forward_first_kernel(
    g, relax, inside, dt, fa, fb, fy, sides, ma_in, mb_in, my_in, u1, ma, mb, my, rx
):
    width = relax[0]
    fill_ramp_x(g, width, rx)
    open_y = 1.0 - ramp_y(g, width)
    beyond = Beyond(g, 0, fa, fb, fy)
    lane = lanes()

    def tile_step(tile, carry):
        rows = rows_of(tile)
        for f in range(g.F):
            halo = beyond.lanes_of(f, rows)
            packed = jnp.zeros((8, 128), f32)
            for x in range(g.X):
                open_xy = open_y * (1.0 - rx[x])
                stepped = inside[f, x, rows, :] + dt[x, rows, :] * beyond.add(f, x, rows, halo)
                done = open_xy * stepped + sides[f, x, rows, :]
                u1[f, x, rows, :] = done
                packed = pack_lanes(x, 0, done, packed)
            my[f, rows, :] = jnp.where(lane < 64, packed_message(packed), my_in[f, rows, :])
        send_ends(g, 0, lambda f, x: u1[f, x, rows, :], rows, ma, mb)
        return carry

    lax.fori_loop(0, g.tiles, tile_step, 0)


def adjoint_last_kernel(g, inside, fa, fb, fy, gsn_own, out, gsn):
    out2 = out.reshape(g.F * g.K * g.X, g.Y)
    beyond = Beyond(g, 1, fa, fb, fy)

    def tile_step(tile, carry):
        rows = rows_of(tile)
        for f in range(g.F):
            halo = beyond.lanes_of(f, rows)
            for x in range(g.X):
                value = inside[f, x, rows, :] + beyond.add(f, x, rows, halo)
                strided(out2, g, f, tile, x)[...] = value
        return carry

    lax.fori_loop(0, g.tiles, tile_step, 0)
    if g.pair:
        here = lax.axis_index("gy")
        span = gsn.shape[3]
        for f in range(g.F):
            gsn[here, f] = gsn_own[f, :, :span]
            gsn[1 - here, f] = fy[f, g.K : g.K + g.X, :span]
    else:
        gsn[...] = jnp.zeros(gsn.shape, f32)


def forward_last_kernel(
    g, relax, mix, inside, dt, fa, fb, fy, sides, kept, swapped, out, rx, lx
):
    width = relax[0]
    for x in range(-2, g.X + 2):
        rx[x + 2] = ramp_x(g, width, x)
    for x in range(g.X):
        lap_x = near * (rx[x + 1] + rx[x + 3]) + far * (rx[x] + rx[x + 4]) - 5.0 * rx[x + 2]
        lx[x] = lap_x
    open_y = 1.0 - ramp_y(g, width)
    masks = lap_masks()
    table = mix_table(mix, False)
    beyond = Beyond(g, 0, fa, fb, fy)
    out2 = out.reshape(g.F * g.K * g.X, g.Y)

    def tile_step(tile, carry):
        rows = rows_of(tile)
        bound = [
            open_y * (kept[f, rows, :] + swapped[f, rows, :]) for f in range(g.F)
        ]
        past = packed_message(kept[g.F, rows, :] + swapped[g.F, rows, :]) * beyond.valid
        for f in range(g.F):
            lap_y = unpack_lanes(f, 0, past, beyond.edge)
            for shift, mask in masks:
                lap_y = lap_y + mask * turn(bound[f], shift)
            mixed_bound = mixed(table, f, bound)
            halo = beyond.lanes_of(f, rows)
            for x in range(g.X):
                slope_x = rx[x + 2]
                open_xy = open_y * (1.0 - slope_x)
                lap = beyond.add(f, x, rows, halo) + slope_x * lap_y + lx[x] * bound[f]
                stepped = inside[f, x, rows, :] + slope_x * mixed_bound + dt[x, rows, :] * lap
                done = open_xy * stepped + slope_x * bound[f] + sides[f, x, rows, :]
                strided(out2, g, f, tile, x)[...] = done
        return carry

    lax.fori_loop(0, g.tiles, tile_step, 0)


def side_sums_kernel(g, dsn, tsn, my_in, gsn, my, wide):
    here = lax.axis_index("gy")
    shift = column_of(jnp.where(here == 0, tsn[0:1, :], tsn[1:2, :]))
    lane = lax.broadcasted_iota(jnp.int32, (g.X, 128), 1)
    batch = 128 // g.K
    for first in range(0, g.F, batch):
        some = range(first, min(first + batch, g.F))
        for f in some:
            wide[(f - first) * g.K : (f - first + 1) * g.K, :] = dsn[f]
        turned = wide[...].T[: g.X]
        for f in some:
            levels = jnp.where(lane < g.K, turn(turned, -(f - first) * g.K), 0.0)
            whole = shift_levels(levels, shift, 1)
            moved = turn(whole, 64)
            gsn[f] = jnp.where(here == 0, whole, moved)
            my[f, g.K : g.K + g.X, :] = jnp.where(here == 0, moved, whole)


def side_bounds_kernel(g, sn, fsn, tsn, bsn, wide):
    here = lax.axis_index("gy")
    shift = column_of(jnp.where(here == 0, tsn[0:1, :], tsn[1:2, :]))
    span = sn.shape[3]
    wide[...] = jnp.zeros(wide.shape, f32)
    for f in range(g.F):
        wide[f, : g.X, :span] = sn[here, f]
        mine = wide[f, : g.X, :]
        theirs = fsn[f, g.K : g.K + g.X, :]
        whole = jnp.where(here == 0, mine, theirs) + turn(
            jnp.where(here == 0, theirs, mine), 64
        )
        wide[f, : g.X, :] = shift_levels(whole, shift, -1)
        bsn[f] = wide[f].T[: g.K]


def side_spread_kernel(g, relax, bsn, out):
    slope_y = ramp_y(g, relax[0])

    def tile_step(tile, carry):
        rows = rows_of(tile)
        for f in range(g.F):
            bounds = bsn[f, rows, :]
            for x in range(g.X):
                out[f, x, rows, :] = slope_y * jnp.broadcast_to(bounds[:, x : x + 1], (8, 128))
        return carry

    lax.fori_loop(0, g.tiles, tile_step, 0)


def fold_rows(values, base, first, count):
    level = lax.broadcasted_iota(jnp.int32, (count, 128), 0) + base - first
    total = jnp.zeros((count, 128), f32)
    for j in range(values.shape[0]):
        row = jnp.broadcast_to(values[j : j + 1, :], (count, 128))
        total = jnp.where(level == j, row, total)
    return total


def fold_kernel(g, parent, terrain, fy, keep, send):
    here = lax.axis_index("gx")
    odd = here >= g.nx // 2
    span = parent.shape[2]
    first = here * span
    lane = lax.broadcasted_iota(jnp.int32, (span, 128), 1)
    top = g.K + g.X
    parts = []
    for e in range(2):
        part = [fold_rows(parent[e, f], terrain[e : e + 1, :], first, g.K) for f in range(g.F)]
        values = jnp.zeros((span, 128), f32)
        heights = jnp.zeros((span, 128), f32)
        for f in range(g.F):
            spots = (lane >= 4 * f) & (lane < 4 * f + 4)
            rows = fy[f, top : top + span, :]
            values = jnp.where(spots, turn(rows, 4 * f - 4 * e), values)
            heights = jnp.where(spots, turn(rows, 4 * f - 8 - 4 * e), heights)
        part.append(fold_rows(values, heights[0:1, :].astype(jnp.int32), first, g.K))
        parts.append(part)
    for i in range(g.F + 1):
        keep[i] = jnp.where(odd, parts[1][i], parts[0][i])
        send[i] = jnp.where(odd, parts[0][i], parts[1][i])


def add_kernel(g, first, second, out):
    out[...] = first[...] + second[...]


def spread_kernel(g, kept, swapped, terrain, out):
    here = lax.axis_index("gx")
    odd = here % 2
    span = out.shape[2]
    row = lax.broadcasted_iota(jnp.int32, (8, 128), 0)
    zero = jnp.zeros((8, 128), f32)
    for e in range(2):
        start = jnp.broadcast_to(here * span - terrain[e : e + 1, :], (8, 128)) + 8
        inside = (start > 0) & (start < g.K + 8)
        tile, rest = start >> 3, start & 7
        for f in range(g.F):
            chosen = jnp.where(odd == e, kept[f], swapped[f])
            tiles = [zero] + [chosen[8 * i : 8 * i + 8] for i in range(g.tiles)] + [zero]
            low, high = zero, zero
            for i in range(g.tiles + 1):
                low = jnp.where(tile == i, tiles[i], low)
                high = jnp.where(tile == i, tiles[i + 1], high)
            for step in (4, 2, 1):
                moves = (rest & step) != 0
                up_low = pltpu.roll(low, 8 - step, 0)
                up_high = pltpu.roll(high, 8 - step, 0)
                low = jnp.where(moves, jnp.where(row < 8 - step, up_low, up_high), low)
                high = jnp.where(moves, up_high, high)
            out[e, f] = jnp.where(inside, low, zero)[:span]


def call(kernel, outs, scratch, ins, time, aliases=None, after=()):
    count = len(ins)
    ins = ins + [("a", value) for value in after]

    def run(*refs):
        kernel(*refs[:count], *refs[len(ins) :])

    out_shape = [jax.ShapeDtypeStruct(s, f32) for s in outs]
    size = 4 * sum(functools.reduce(lambda a, b: a * b, s) for s in outs)
    return pl.pallas_call(
        run,
        out_shape=out_shape,
        in_specs=[places[where] for where, _ in ins],
        out_specs=[places["v"]] * len(outs),
        scratch_shapes=[pltpu.VMEM(s, f32) if isinstance(s, tuple) else s for s in scratch],
        input_output_aliases=aliases or {},
        compiler_params=pltpu.CompilerParams(vmem_limit_bytes=24 * 1024 * 1024),
        cost_estimate=pl.CostEstimate(flops=int(time * 1.1e9), bytes_accessed=2 * size, transcendentals=0),
    )(*[pltpu.with_memory_space_constraint(v, pltpu.HBM) if w == "h" else v for w, v in ins])


def body(
    child_state,
    cotangent,
    diffusivity,
    field_mix,
    parent_we,
    parent_sn,
    terrain_we,
    terrain_sn,
    relax_width,
):
    nx, ny = lax.axis_size("gx"), lax.axis_size("gy")
    g = Geometry(child_state.shape, nx, ny)
    F, K, X, Y = child_state.shape
    evens = [(i, i ^ 1) for i in range(nx)]
    odds = [(i, (((i + 1) ^ 1) - 1) % nx) for i in range(nx)]
    block = (F, X, K, 128)
    row_shape = (2, 2, F, K, 128)
    lane_shape = (F, g.tall, 128)
    edge_shape = (F, K, 128)
    ramps = (X, 8, 128)
    band = pltpu.VMEM((256, 128), jnp.bfloat16)
    parts = (F, 8 * X, 128)

    def bind(kernel, *args):
        return functools.partial(kernel, g, *args)

    def swapped(values, distance):
        return lax.ppermute(values, "gx", [(i, i ^ distance) for i in range(nx)])

    def to_y(message):
        if g.pair:
            return lax.ppermute(message, "gy", [(0, 1), (1, 0)])
        up = lax.ppermute(message, "gy", [(i, i + 1) for i in range(ny - 1)])
        down = lax.ppermute(message, "gy", [(i + 1, i) for i in range(ny - 1)])
        low = (jnp.arange(128, dtype=jnp.int32) % 4 < 2)[None, None, :]
        rows = (jnp.arange(g.tall, dtype=jnp.int32) < K)[None, :, None]
        return jnp.where(low == rows, down, up)

    def add(first, second, after):
        (total,) = call(
            bind(add_kernel), [first.shape], [], [("v", first), ("v", second)], 0.1, after=after
        )
        return total

    sn_turned = jnp.swapaxes(parent_sn, 2, 3)
    ut, at, dt, qt, ma, mb, my = call(
        bind(pack_kernel),
        [block, block, (X, K, 128), block, row_shape, row_shape, lane_shape],
        [
            ramps,
            child_state.shape,
            child_state.shape,
            diffusivity.shape,
            sn_turned.shape,
            parent_we.shape,
            pltpu.VMEM(terrain_we.shape, jnp.int32),
            pltpu.SemaphoreType.DMA((3, g.tiles)),
            pltpu.SemaphoreType.DMA((3,)),
        ],
        [
            ("s", relax_width),
            ("h", child_state),
            ("h", cotangent),
            ("h", diffusivity),
            ("h", sn_turned),
            ("h", parent_we),
            ("h", terrain_we),
        ],
        3,
    )
    fb = lax.ppermute(mb, "gx", odds)
    fa = lax.ppermute(ma, "gx", evens)
    fy = to_y(my)

    (inside_a,) = call(
        bind(adjoint_inside_kernel, True),
        [block],
        [ramps, band, parts],
        [("s", relax_width), ("s", field_mix), ("v", at), ("v", qt)],
        2.5,
    )
    (inside_u,) = call(
        bind(forward_inside_kernel),
        [block],
        [band, parts],
        [("s", field_mix), ("v", ut), ("v", dt)],
        2.5,
        after=[inside_a],
    )
    keep, send = call(
        bind(fold_kernel),
        [(F + 1, K, 128)] * 2,
        [],
        [("v", parent_we), ("v", terrain_we), ("v", fy)],
        0.3,
    )
    first_bounds = swapped(send, nx // 2)

    if g.pair:
        (bsn,) = call(
            bind(side_bounds_kernel),
            [edge_shape],
            [(F, 128, 128)],
            [("v", sn_turned), ("v", fy), ("v", terrain_sn)],
            0.7,
        )
    else:
        bsn = bound_sn_general(g, parent_sn, terrain_sn)
    (sides,) = call(
        bind(side_spread_kernel), [block], [], [("s", relax_width), ("v", bsn)], 0.7
    )

    p1, q1, ma, mb, my, dwe, dsn = call(
        bind(adjoint_first_kernel),
        [block, block, row_shape, row_shape, lane_shape, edge_shape, edge_shape],
        [ramps],
        [
            ("s", relax_width),
            ("v", inside_a),
            ("v", at),
            ("v", dt),
            ("v", fa),
            ("v", fb),
            ("v", fy),
        ],
        3,
        after=[keep, sides],
    )
    first_sums = swapped(dwe, 2)
    bounds = add(keep, first_bounds, [dwe])
    second_bounds = swapped(bounds, 2)
    u1, ma, mb, my = call(
        bind(forward_first_kernel),
        [block, row_shape, row_shape, lane_shape],
        [ramps],
        [
            ("s", relax_width),
            ("v", inside_u),
            ("v", dt),
            ("v", fa),
            ("v", fb),
            ("v", fy),
            ("v", sides),
            ("v", ma),
            ("v", mb),
            ("v", my),
        ],
        2.5,
        {7: 1, 8: 2, 9: 3},
        after=[bounds],
    )
    if g.pair:
        gsn_own, my = call(
            bind(side_sums_kernel),
            [(F, X, 128), lane_shape],
            [(128, 128)],
            [("v", dsn), ("v", terrain_sn), ("v", my)],
            0.6,
            {2: 1},
        )
    else:
        gsn_own = dsn
    fb = lax.ppermute(mb, "gx", odds)
    fa = lax.ppermute(ma, "gx", evens)
    fy = to_y(my)

    sums = add(dwe, first_sums, [gsn_own])
    second_sums = swapped(sums, 4)
    bounds = add(bounds, second_bounds, [gsn_own])
    third_bounds = swapped(bounds, 4)
    (inside_a,) = call(
        bind(adjoint_inside_kernel, False),
        [block],
        [ramps, band, parts],
        [("s", relax_width), ("s", field_mix), ("v", p1), ("v", q1)],
        2.5,
        after=[sums, bounds],
    )
    sums = add(sums, second_sums, [inside_a])
    third_sums = swapped(sums, 8)
    (inside_u,) = call(
        bind(forward_inside_kernel),
        [block],
        [band, parts],
        [("s", field_mix), ("v", u1), ("v", dt)],
        2.5,
        after=[sums],
    )
    bounds = add(bounds, third_bounds, [inside_u])
    distance = 8
    while distance < nx // 2:
        bounds = bounds + swapped(bounds, distance)
        distance *= 2
    other_bounds = swapped(bounds, 1)
    grad_state, grad_sn = call(
        bind(adjoint_last_kernel),
        [child_state.shape, sn_turned.shape],
        [],
        [("v", inside_a), ("v", fa), ("v", fb), ("v", fy), ("v", gsn_own)],
        2.5,
        after=[bounds],
    )
    sums = add(sums, third_sums, [grad_state])
    distance = 16
    while distance < nx:
        sums = sums + swapped(sums, distance)
        distance *= 2
    other_sums = swapped(sums, 1)
    (child_final,) = call(
        bind(forward_last_kernel),
        [child_state.shape],
        [(X + 4, 8, 128), ramps],
        [
            ("s", relax_width),
            ("s", field_mix),
            ("v", inside_u),
            ("v", dt),
            ("v", fa),
            ("v", fb),
            ("v", fy),
            ("v", sides),
            ("v", bounds),
            ("v", other_bounds),
        ],
        3,
    )
    (grad_we,) = call(
        bind(spread_kernel),
        [parent_we.shape],
        [],
        [("v", sums), ("v", other_sums), ("v", terrain_we)],
        0.7,
    )
    if g.pair:
        grad_sn = jnp.swapaxes(grad_sn, 2, 3)
    else:
        grad_sn = grad_sn_general(g, gsn_own, terrain_sn, parent_sn.shape[2])
    return (child_final, grad_state, grad_we, grad_sn)


def level_weights(g, terrain, span):
    first = lax.axis_index("gy") * span
    base = terrain[:, None, :] + jnp.arange(g.K, dtype=jnp.int32)[None, :, None]
    parent = first + jnp.arange(span, dtype=jnp.int32)
    return (parent[None, None, :, None] == base[:, :, None, :]).astype(f32)


def bound_sn_general(g, parent_sn, terrain_sn):
    weights = level_weights(g, terrain_sn, parent_sn.shape[2])
    bound = jnp.einsum("eflc,eklc->efkc", parent_sn, weights, precision=highest)
    bound = lax.psum(bound, "gy")
    mine = jnp.where(lax.axis_index("gy") < g.ny // 2, bound[0], bound[1])
    return jnp.pad(mine, ((0, 0), (0, 0), (0, 128 - g.X)))


def grad_sn_general(g, sums, terrain_sn, span):
    sums = sums[:, :, : g.X]
    south = lax.axis_index("gy") < g.ny // 2
    zero = jnp.zeros_like(sums)
    both = jnp.stack([jnp.where(south, sums, zero), jnp.where(south, zero, sums)])
    both = lax.psum(both, "gy")
    weights = level_weights(g, terrain_sn, span)
    return jnp.einsum("efkc,eklc->eflc", both, weights, precision=highest)


def solution(mesh):
    return jax.shard_map(
        body,
        mesh=mesh,
        in_specs=(
            P(None, None, "gx", "gy"),
            P(None, None, "gx", "gy"),
            P(None, "gx", "gy"),
            P(),
            P(None, None, "gx", "gy"),
            P(None, None, "gy", "gx"),
            P(None, "gy"),
            P(None, "gx"),
            P(),
        ),
        out_specs=(
            P(None, None, "gx", "gy"),
            P(None, None, "gx", "gy"),
            P(None, None, "gx", "gy"),
            P(None, None, "gy", "gx"),
        ),
        check_vma=False,
    )
```

```python
import functools

import jax
import jax.numpy as jnp
from jax import lax
from jax.experimental import pallas as pl
from jax.experimental.pallas import tpu as pltpu
from jax.sharding import PartitionSpec as P

near = 4.0 / 3.0
far = -1.0 / 12.0
coupling = 0.25
highest = lax.Precision.HIGHEST
f32 = jnp.float32
places = {
    "v": pl.BlockSpec(memory_space=pltpu.VMEM),
    "s": pl.BlockSpec(memory_space=pltpu.SMEM),
    "h": pl.BlockSpec(memory_space=pltpu.HBM),
    "a": pl.BlockSpec(memory_space=pl.ANY),
}
widest_zone = 15


class Geometry:
    def __init__(self, child, nx, ny):
        self.F, self.K, self.X, self.Y = child
        self.nx, self.ny = nx, ny
        self.tiles = self.K // 8
        assert self.K % 8 == 0 and self.Y == 128 and 4 * self.X <= 64
        assert self.X > widest_zone and self.Y > widest_zone
        assert self.X == 16
        assert nx >= 16 and nx & (nx - 1) == 0 and ny % 2 == 0
        assert 4 * self.F <= 128 and 128 % self.K == 0
        self.pair = ny == 2
        self.tall = self.K + self.X + 8


def lanes():
    return lax.broadcasted_iota(jnp.int32, (8, 128), 1)


def turn(values, shift):
    return pltpu.roll(values, shift % 128, values.ndim - 1)


def ramp(position, length, width):
    distance = jnp.minimum(position, length - 1 - position)
    inside = (position >= 0) & (position < length)
    top = jnp.where(inside, jnp.maximum(width - distance, 0), 0)
    bottom = jnp.full((8, 128), width + 1, jnp.int32)
    return jnp.broadcast_to(top, (8, 128)).astype(f32) / bottom.astype(f32)


def ramp_y(g, width):
    return ramp(lax.axis_index("gy") * g.Y + lanes(), g.ny * g.Y, width)


def ramp_x(g, width, x):
    return ramp(lax.axis_index("gx") * g.X + x, g.nx * g.X, width)


def fill_ramp_x(g, width, ref):
    for x in range(g.X):
        ref[x] = ramp_x(g, width, x)


def lap_masks():
    lane = lanes()
    zero = jnp.zeros((8, 128), f32)
    return (
        (1, jnp.where(lane > 0, near, zero)),
        (-1, jnp.where(lane < 127, near, zero)),
        (2, jnp.where(lane > 1, far, zero)),
        (-2, jnp.where(lane < 126, far, zero)),
    )


def fill_band(band):
    shape = (2 * 128, 128)
    row = lax.broadcasted_iota(jnp.int32, shape, 0) % 128
    gap = jnp.abs(row - lax.broadcasted_iota(jnp.int32, shape, 1))
    entry = jnp.where(gap == 0, -60.0, jnp.where(gap == 1, 16.0, jnp.where(gap == 2, -1.0, 0.0)))
    band[...] = entry.astype(jnp.bfloat16)


def along_lanes(values, band):
    high = values.astype(jnp.bfloat16)
    low = (values - high.astype(f32)).astype(jnp.bfloat16)
    return jnp.dot(
        jnp.concatenate([high, low], axis=1), band[...], preferred_element_type=f32
    )


def pack_lanes(x, base, values, packed):
    lane = lanes()
    start = base + 4 * x
    return jnp.where((lane >= start) & (lane < start + 4), turn(values, start + 2), packed)


def packed_message(packed):
    spot = lanes() % 4
    zero = jnp.zeros((8, 128), f32)
    low = far * turn(packed, -2) + jnp.where(spot == 1, near * turn(packed, -1), zero)
    high = far * turn(packed, 2) + jnp.where(spot == 2, near * turn(packed, 1), zero)
    return jnp.where(spot < 2, low, high)


def valid_lanes(g):
    at = lax.axis_index("gy")
    spot = lanes() % 4
    low = (at < g.ny - 1).astype(f32)
    high = (at > 0).astype(f32)
    return jnp.where(spot < 2, low, high)


def border():
    lane = lanes()
    return jnp.where((lane < 2) | (lane >= 126), 1.0, 0.0).astype(f32)


def unpack_lanes(x, base, packed, edge):
    return edge * turn(packed, -(base + 4 * x + 2))


def strided(ref, g, f, tile, x):
    start = (f * g.K + tile * 8) * g.X + x
    return ref.at[pl.ds(start, 8, stride=g.X), :]


def mix_table(mix, transposed):
    count = mix.shape[0]
    return [
        [
            (mix[h, f] if transposed else mix[f, h]) * coupling + (1.0 if f == h else 0.0)
            for h in range(count)
        ]
        for f in range(count)
    ]


def mixed(table, f, values):
    total = table[f][0] * values[0]
    for h in range(1, len(values)):
        total = total + table[f][h] * values[h]
    return total


def column_of(row):
    count = row.shape[1]
    wide = jnp.broadcast_to(row.astype(f32), (count, count))
    a = lax.broadcasted_iota(jnp.int32, (count, count), 0)
    b = lax.broadcasted_iota(jnp.int32, (count, count), 1)
    picked = jnp.sum(jnp.where(a == b, wide, 0.0), axis=1, keepdims=True)
    return jnp.broadcast_to(picked, (count, 128)).astype(jnp.int32)


def shift_levels(values, shift, sign):
    step = 1
    while step < 128:
        values = jnp.where((shift & step) != 0, turn(values, sign * step), values)
        step *= 2
    return values


def level_copies(g, pairs, sems, tile):
    levels = pl.ds(pl.multiple_of(tile * 8, 8), 8)
    copies = []
    for i, (source, target) in enumerate(pairs):
        at = (levels,) if len(source.shape) == 3 else (slice(None), levels)
        copies.append(pltpu.make_async_copy(source.at[at], target.at[at], sems.at[i, tile]))
    return copies


def rows_of(tile):
    return pl.ds(pl.multiple_of(tile * 8, 8), 8)


def odd_column():
    return lax.axis_index("gx") % 2 == 1


def send_ends(g, s, source, rows, ma, mb):
    odd = odd_column()
    for f in range(g.F):
        for j in range(2):
            low, high = source(f, j), source(f, g.X - 2 + j)
            ma[s, j, f, rows, :] = jnp.where(odd, low, high)
            mb[s, j, f, rows, :] = jnp.where(odd, high, low)


class Beyond:
    def __init__(self, g, s, fa, fb, fy):
        self.g, self.s, self.fa, self.fb, self.fy = g, s, fa, fb, fy
        self.edge = border()
        self.valid = valid_lanes(g)
        here = lax.axis_index("gx")
        self.odd = here % 2 == 1
        self.first, self.last = here == 0, here == g.nx - 1

    def left(self, j, f, rows):
        at = (self.s, j, f, rows, slice(None))
        value = jnp.where(self.odd, self.fa[at], self.fb[at])
        return jnp.where(self.first, jnp.zeros_like(value), value)

    def right(self, j, f, rows):
        at = (self.s, j, f, rows, slice(None))
        value = jnp.where(self.odd, self.fb[at], self.fa[at])
        return jnp.where(self.last, jnp.zeros_like(value), value)

    def lanes_of(self, f, rows):
        return self.fy[f, rows, :] * self.valid

    def add(self, f, x, rows, packed):
        s, last = self.s, self.g.X - 1
        total = unpack_lanes(x, 64 * s, packed, self.edge)
        if x == 0:
            total = total + near * self.left(1, f, rows) + far * self.left(0, f, rows)
        if x == 1:
            total = total + far * self.left(1, f, rows)
        if x == last - 1:
            total = total + far * self.right(0, f, rows)
        if x == last:
            total = total + near * self.right(0, f, rows) + far * self.right(1, f, rows)
        return total


def lane_sums(vectors):
    lane = lanes()
    step = 1
    while len(vectors) > 1:
        low = (lane & step) == 0
        merged = []
        for a, b in zip(vectors[::2], vectors[1::2]):
            merged.append(jnp.where(low, a, b) + turn(jnp.where(low, b, a), step))
        vectors = merged
        step *= 2
    total = vectors[0]
    while step < 128:
        total = total + turn(total, step)
        step *= 2
    return total


def pack_kernel(
    g, relax, child_far, cot_far, diff_far, sn_far, parent_far, terrain_far,
    ut, at, dt, qt, ma, mb, my, rx, child, cot, diff, sn, parent, terrain, sems, side_sems,
):
    width = relax[0]
    pairs = ((diff_far, diff), (child_far, child), (cot_far, cot))
    for tile in range(g.tiles):
        for copy in level_copies(g, pairs, sems, tile):
            copy.start()
    side_copies = [
        pltpu.make_async_copy(source, target, side_sems.at[i])
        for i, (source, target) in enumerate(
            ((sn_far, sn), (parent_far, parent), (terrain_far, terrain))
        )
    ]
    for copy in side_copies:
        copy.start()
    fill_ramp_x(g, width, rx)
    open_y = 1.0 - ramp_y(g, width)
    child2 = child.reshape(g.F * g.K * g.X, g.Y)
    cot2 = cot.reshape(g.F * g.K * g.X, g.Y)
    diff2 = diff.reshape(g.K * g.X, g.Y)

    def tile_step(tile, carry):
        for copy in level_copies(g, pairs, sems, tile):
            copy.wait()
        rows = rows_of(tile)
        packed = [jnp.zeros((8, 128), f32) for _ in range(g.F)]
        for x in range(g.X):
            d = strided(diff2, g, 0, tile, x)[...]
            dt[x, rows, :] = d
            open_xy = open_y * (1.0 - rx[x])
            for f in range(g.F):
                u = strided(child2, g, f, tile, x)[...]
                a = strided(cot2, g, f, tile, x)[...]
                q = d * (open_xy * a)
                ut[f, x, rows, :] = u
                at[f, x, rows, :] = a
                qt[f, x, rows, :] = q
                packed[f] = pack_lanes(x, 0, u, packed[f])
                packed[f] = pack_lanes(x, 64, q, packed[f])
        for f in range(g.F):
            my[f, rows, :] = packed_message(packed[f])
        for s, source in enumerate((ut, qt)):
            send_ends(g, s, lambda f, x: source[f, x, rows, :], rows, ma, mb)
        return carry

    lax.fori_loop(0, g.tiles, tile_step, 0)
    for copy in side_copies:
        copy.wait()
    for f in range(g.F):
        my[f, g.K :, :] = jnp.zeros((g.X + 8, 128), f32)
    if g.pair:
        other = 1 - lax.axis_index("gy")
        for f in range(g.F):
            my[f, g.K : g.K + g.X, : sn.shape[3]] = sn[other, f]
    span = parent.shape[2]
    lane = lax.broadcasted_iota(jnp.int32, (span, 128), 1)
    for f in range(g.F):
        total = jnp.zeros((span, 128), f32)
        for e in range(2):
            heights = jnp.broadcast_to(terrain[e : e + 1, :].astype(f32), (span, 128))
            for spot, values in ((e, parent[e, f]), (2 + e, heights)):
                here = (lane >= 4 * spot) & (lane < 4 * spot + 4)
                total = jnp.where(here, turn(values, 4 * spot + 2), total)
        my[f, g.K + g.X : g.K + g.X + span, :] = total


def fill_laps(g, source, rows, band, laps):
    for f in range(g.F):
        cells = source[f, :, rows, :]
        parts = along_lanes(cells.reshape(8 * g.X, 128), band)
        for x in range(g.X):
            ones = [cells[x + i] for i in (-1, 1) if 0 <= x + i < g.X]
            twos = [cells[x + i] for i in (-2, 2) if 0 <= x + i < g.X]
            total = parts[8 * x : 8 * x + 8] + 16.0 * functools.reduce(jnp.add, ones)
            total = total - functools.reduce(jnp.add, twos)
            laps[f, x] = total * (1.0 / 12.0)


def adjoint_inside_kernel(g, scaled, relax, mix, ps, qs, out, rx, band, laps):
    width = relax[0]
    table = mix_table(mix, True)
    fill_band(band)
    if scaled:
        fill_ramp_x(g, width, rx)
        open_y = 1.0 - ramp_y(g, width)

    def tile_step(tile, carry):
        rows = rows_of(tile)
        fill_laps(g, qs, rows, band, laps)
        for x in range(g.X):
            p = [ps[f, x, rows, :] for f in range(g.F)]
            if scaled:
                open_xy = open_y * (1.0 - rx[x])
                p = [open_xy * value for value in p]
            for f in range(g.F):
                out[f, x, rows, :] = mixed(table, f, p) + laps[f, x]
        return carry

    lax.fori_loop(0, g.tiles, tile_step, 0)


def forward_inside_kernel(g, mix, ut, dt, out, band, laps):
    table = mix_table(mix, False)
    fill_band(band)

    def tile_step(tile, carry):
        rows = rows_of(tile)
        fill_laps(g, ut, rows, band, laps)
        for x in range(g.X):
            u = [ut[f, x, rows, :] for f in range(g.F)]
            d = dt[x, rows, :]
            for f in range(g.F):
                out[f, x, rows, :] = mixed(table, f, u) + d * laps[f, x]
        return carry

    lax.fori_loop(0, g.tiles, tile_step, 0)


def adjoint_first_kernel(
    g, relax, inside, at, dt, fa, fb, fy, p1, q1, ma, mb, my, dwe, dsn, rx
):
    width = relax[0]
    fill_ramp_x(g, width, rx)
    slope_y = ramp_y(g, width)
    open_y = 1.0 - slope_y
    beyond = Beyond(g, 1, fa, fb, fy)

    def tile_step(tile, carry):
        rows = rows_of(tile)
        for f in range(g.F):
            halo = beyond.lanes_of(f, rows)
            packed = jnp.zeros((8, 128), f32)
            share = jnp.zeros((8, 128), f32)
            pushes = []
            for x in range(g.X):
                slope_x = rx[x]
                open_xy = open_y * (1.0 - slope_x)
                middle = inside[f, x, rows, :] + beyond.add(f, x, rows, halo)
                carried = at[f, x, rows, :] + middle
                share = share + slope_x * carried
                pushes.append(slope_y * carried)
                pulled = open_xy * middle
                q = dt[x, rows, :] * pulled
                p1[f, x, rows, :] = pulled
                q1[f, x, rows, :] = q
                packed = pack_lanes(x, 64, q, packed)
            my[f, rows, :] = packed_message(packed)
            dsn[f, rows, :] = lane_sums(pushes)
            dwe[f, rows, :] = open_y * share
        send_ends(g, 1, lambda f, x: q1[f, x, rows, :], rows, ma, mb)
        return carry

    lax.fori_loop(0, g.tiles, tile_step, 0)
    for f in range(g.F):
        my[f, g.K :, :] = jnp.zeros((g.X + 8, 128), f32)


def forward_first_kernel(
    g, relax, inside, dt, fa, fb, fy, sides, ma_in, mb_in, my_in, u1, ma, mb, my, rx
):
    width = relax[0]
    fill_ramp_x(g, width, rx)
    open_y = 1.0 - ramp_y(g, width)
    beyond = Beyond(g, 0, fa, fb, fy)
    lane = lanes()

    def tile_step(tile, carry):
        rows = rows_of(tile)
        for f in range(g.F):
            halo = beyond.lanes_of(f, rows)
            packed = jnp.zeros((8, 128), f32)
            for x in range(g.X):
                open_xy = open_y * (1.0 - rx[x])
                stepped = inside[f, x, rows, :] + dt[x, rows, :] * beyond.add(f, x, rows, halo)
                done = open_xy * stepped + sides[f, x, rows, :]
                u1[f, x, rows, :] = done
                packed = pack_lanes(x, 0, done, packed)
            my[f, rows, :] = jnp.where(lane < 64, packed_message(packed), my_in[f, rows, :])
        send_ends(g, 0, lambda f, x: u1[f, x, rows, :], rows, ma, mb)
        return carry

    lax.fori_loop(0, g.tiles, tile_step, 0)


def adjoint_last_kernel(g, inside, fa, fb, fy, gsn_own, out, gsn):
    out2 = out.reshape(g.F * g.K * g.X, g.Y)
    beyond = Beyond(g, 1, fa, fb, fy)

    def tile_step(tile, carry):
        rows = rows_of(tile)
        for f in range(g.F):
            halo = beyond.lanes_of(f, rows)
            for x in range(g.X):
                value = inside[f, x, rows, :] + beyond.add(f, x, rows, halo)
                strided(out2, g, f, tile, x)[...] = value
        return carry

    lax.fori_loop(0, g.tiles, tile_step, 0)
    if g.pair:
        here = lax.axis_index("gy")
        span = gsn.shape[3]
        for f in range(g.F):
            gsn[here, f] = gsn_own[f, :, :span]
            gsn[1 - here, f] = fy[f, g.K : g.K + g.X, :span]
    else:
        gsn[...] = jnp.zeros(gsn.shape, f32)


def forward_last_kernel(
    g, relax, mix, inside, dt, fa, fb, fy, sides, kept, swapped, out, mark, rx, lx
):
    width = relax[0]
    mark[...] = jnp.zeros((8, 128), f32)
    for x in range(-2, g.X + 2):
        rx[x + 2] = ramp_x(g, width, x)
    for x in range(g.X):
        lap_x = near * (rx[x + 1] + rx[x + 3]) + far * (rx[x] + rx[x + 4]) - 5.0 * rx[x + 2]
        lx[x] = lap_x
    open_y = 1.0 - ramp_y(g, width)
    masks = lap_masks()
    table = mix_table(mix, False)
    beyond = Beyond(g, 0, fa, fb, fy)
    out2 = out.reshape(g.F * g.K * g.X, g.Y)

    def tile_step(tile, carry):
        rows = rows_of(tile)
        bound = [
            open_y * (kept[f, rows, :] + swapped[f, rows, :]) for f in range(g.F)
        ]
        past = packed_message(kept[g.F, rows, :] + swapped[g.F, rows, :]) * beyond.valid
        for f in range(g.F):
            lap_y = unpack_lanes(f, 0, past, beyond.edge)
            for shift, mask in masks:
                lap_y = lap_y + mask * turn(bound[f], shift)
            mixed_bound = mixed(table, f, bound)
            halo = beyond.lanes_of(f, rows)
            for x in range(g.X):
                slope_x = rx[x + 2]
                open_xy = open_y * (1.0 - slope_x)
                lap = beyond.add(f, x, rows, halo) + slope_x * lap_y + lx[x] * bound[f]
                stepped = inside[f, x, rows, :] + slope_x * mixed_bound + dt[x, rows, :] * lap
                done = open_xy * stepped + slope_x * bound[f] + sides[f, x, rows, :]
                strided(out2, g, f, tile, x)[...] = done
        return carry

    lax.fori_loop(0, g.tiles, tile_step, 0)


def side_sums_kernel(g, dsn, tsn, my_in, gsn, my, wide):
    here = lax.axis_index("gy")
    shift = column_of(jnp.where(here == 0, tsn[0:1, :], tsn[1:2, :]))
    lane = lax.broadcasted_iota(jnp.int32, (g.X, 128), 1)
    batch = 128 // g.K
    for first in range(0, g.F, batch):
        some = range(first, min(first + batch, g.F))
        for f in some:
            wide[(f - first) * g.K : (f - first + 1) * g.K, :] = dsn[f]
        turned = wide[...].T[: g.X]
        for f in some:
            levels = jnp.where(lane < g.K, turn(turned, -(f - first) * g.K), 0.0)
            whole = shift_levels(levels, shift, 1)
            moved = turn(whole, 64)
            gsn[f] = jnp.where(here == 0, whole, moved)
            my[f, g.K : g.K + g.X, :] = jnp.where(here == 0, moved, whole)


def side_bounds_kernel(g, sn, fsn, tsn, bsn, wide):
    here = lax.axis_index("gy")
    shift = column_of(jnp.where(here == 0, tsn[0:1, :], tsn[1:2, :]))
    span = sn.shape[3]
    wide[...] = jnp.zeros(wide.shape, f32)
    for f in range(g.F):
        wide[f, : g.X, :span] = sn[here, f]
        mine = wide[f, : g.X, :]
        theirs = fsn[f, g.K : g.K + g.X, :]
        whole = jnp.where(here == 0, mine, theirs) + turn(
            jnp.where(here == 0, theirs, mine), 64
        )
        wide[f, : g.X, :] = shift_levels(whole, shift, -1)
        bsn[f] = wide[f].T[: g.K]


def side_spread_kernel(g, relax, bsn, out):
    slope_y = ramp_y(g, relax[0])

    def tile_step(tile, carry):
        rows = rows_of(tile)
        for f in range(g.F):
            bounds = bsn[f, rows, :]
            for x in range(g.X):
                out[f, x, rows, :] = slope_y * jnp.broadcast_to(bounds[:, x : x + 1], (8, 128))
        return carry

    lax.fori_loop(0, g.tiles, tile_step, 0)


def fold_rows(values, base, first, count):
    level = lax.broadcasted_iota(jnp.int32, (count, 128), 0) + base - first
    total = jnp.zeros((count, 128), f32)
    for j in range(values.shape[0]):
        row = jnp.broadcast_to(values[j : j + 1, :], (count, 128))
        total = jnp.where(level == j, row, total)
    return total


def fold_kernel(g, parent, terrain, fy, keep, send):
    here = lax.axis_index("gx")
    odd = here >= g.nx // 2
    span = parent.shape[2]
    first = here * span
    lane = lax.broadcasted_iota(jnp.int32, (span, 128), 1)
    top = g.K + g.X
    parts = []
    for e in range(2):
        part = [fold_rows(parent[e, f], terrain[e : e + 1, :], first, g.K) for f in range(g.F)]
        values = jnp.zeros((span, 128), f32)
        heights = jnp.zeros((span, 128), f32)
        for f in range(g.F):
            spots = (lane >= 4 * f) & (lane < 4 * f + 4)
            rows = fy[f, top : top + span, :]
            values = jnp.where(spots, turn(rows, 4 * f - 4 * e), values)
            heights = jnp.where(spots, turn(rows, 4 * f - 8 - 4 * e), heights)
        part.append(fold_rows(values, heights[0:1, :].astype(jnp.int32), first, g.K))
        parts.append(part)
    for i in range(g.F + 1):
        keep[i] = jnp.where(odd, parts[1][i], parts[0][i])
        send[i] = jnp.where(odd, parts[0][i], parts[1][i])


def join_kernel(g, sums, bounds, more_bounds, out):
    for f in range(g.F):
        out[f] = sums[f]
    for f in range(g.F + 1):
        out[g.F + f] = bounds[f] + more_bounds[f]


def split_kernel(g, state, moved, sums, bounds):
    for f in range(g.F):
        sums[f] = state[f] + moved[f]
    for f in range(g.F + 1):
        bounds[f] = state[g.F + f] + moved[g.F + f]


def add_kernel(g, first, second, out):
    out[...] = first[...] + second[...]


def spread_kernel(g, kept, swapped, terrain, out):
    here = lax.axis_index("gx")
    odd = here % 2
    span = out.shape[2]
    row = lax.broadcasted_iota(jnp.int32, (8, 128), 0)
    zero = jnp.zeros((8, 128), f32)
    for e in range(2):
        start = jnp.broadcast_to(here * span - terrain[e : e + 1, :], (8, 128)) + 8
        inside = (start > 0) & (start < g.K + 8)
        tile, rest = start >> 3, start & 7
        for f in range(g.F):
            chosen = jnp.where(odd == e, kept[f], swapped[f])
            tiles = [zero] + [chosen[8 * i : 8 * i + 8] for i in range(g.tiles)] + [zero]
            low, high = zero, zero
            for i in range(g.tiles + 1):
                low = jnp.where(tile == i, tiles[i], low)
                high = jnp.where(tile == i, tiles[i + 1], high)
            for step in (4, 2, 1):
                moves = (rest & step) != 0
                up_low = pltpu.roll(low, 8 - step, 0)
                up_high = pltpu.roll(high, 8 - step, 0)
                low = jnp.where(moves, jnp.where(row < 8 - step, up_low, up_high), low)
                high = jnp.where(moves, up_high, high)
            out[e, f] = jnp.where(inside, low, zero)[:span]


def call(kernel, outs, scratch, ins, time, aliases=None, after=()):
    count = len(ins)
    ins = ins + [("a", value) for value in after]

    def run(*refs):
        kernel(*refs[:count], *refs[len(ins) :])

    out_shape = [jax.ShapeDtypeStruct(s, f32) for s in outs]
    size = 4 * sum(functools.reduce(lambda a, b: a * b, s) for s in outs)
    return pl.pallas_call(
        run,
        out_shape=out_shape,
        in_specs=[places[where] for where, _ in ins],
        out_specs=[places["v"]] * len(outs),
        scratch_shapes=[pltpu.VMEM(s, f32) if isinstance(s, tuple) else s for s in scratch],
        input_output_aliases=aliases or {},
        compiler_params=pltpu.CompilerParams(vmem_limit_bytes=24 * 1024 * 1024),
        cost_estimate=pl.CostEstimate(flops=int(time * 1.1e9), bytes_accessed=2 * size, transcendentals=0),
    )(*[pltpu.with_memory_space_constraint(v, pltpu.HBM) if w == "h" else v for w, v in ins])


def body(
    child_state,
    cotangent,
    diffusivity,
    field_mix,
    parent_we,
    parent_sn,
    terrain_we,
    terrain_sn,
    relax_width,
):
    nx, ny = lax.axis_size("gx"), lax.axis_size("gy")
    g = Geometry(child_state.shape, nx, ny)
    F, K, X, Y = child_state.shape
    evens = [(i, i ^ 1) for i in range(nx)]
    odds = [(i, (((i + 1) ^ 1) - 1) % nx) for i in range(nx)]
    block = (F, X, K, 128)
    row_shape = (2, 2, F, K, 128)
    lane_shape = (F, g.tall, 128)
    edge_shape = (F, K, 128)
    ramps = (X, 8, 128)
    band = pltpu.VMEM((256, 128), jnp.bfloat16)
    laps = (F, X, 8, 128)

    def bind(kernel, *args):
        return functools.partial(kernel, g, *args)

    def swapped(values, distance):
        return lax.ppermute(values, "gx", [(i, i ^ distance) for i in range(nx)])

    def to_y(message):
        if g.pair:
            return lax.ppermute(message, "gy", [(0, 1), (1, 0)])
        up = lax.ppermute(message, "gy", [(i, i + 1) for i in range(ny - 1)])
        down = lax.ppermute(message, "gy", [(i + 1, i) for i in range(ny - 1)])
        low = (jnp.arange(128, dtype=jnp.int32) % 4 < 2)[None, None, :]
        rows = (jnp.arange(g.tall, dtype=jnp.int32) < K)[None, :, None]
        return jnp.where(low == rows, down, up)

    def add(first, second, after):
        (total,) = call(
            bind(add_kernel), [first.shape], [], [("v", first), ("v", second)], 0.1, after=after
        )
        return total

    sn_turned = jnp.swapaxes(parent_sn, 2, 3)
    ut, at, dt, qt, ma, mb, my = call(
        bind(pack_kernel),
        [block, block, (X, K, 128), block, row_shape, row_shape, lane_shape],
        [
            ramps,
            child_state.shape,
            child_state.shape,
            diffusivity.shape,
            sn_turned.shape,
            parent_we.shape,
            pltpu.VMEM(terrain_we.shape, jnp.int32),
            pltpu.SemaphoreType.DMA((3, g.tiles)),
            pltpu.SemaphoreType.DMA((3,)),
        ],
        [
            ("s", relax_width),
            ("h", child_state),
            ("h", cotangent),
            ("h", diffusivity),
            ("h", sn_turned),
            ("h", parent_we),
            ("h", terrain_we),
        ],
        3,
    )
    fy = to_y(my)
    fa = lax.ppermute(ma, "gx", evens)
    fb = lax.ppermute(mb, "gx", odds)

    (inside_a,) = call(
        bind(adjoint_inside_kernel, True),
        [block],
        [ramps, band, laps],
        [("s", relax_width), ("s", field_mix), ("v", at), ("v", qt)],
        2.5,
    )
    (inside_u,) = call(
        bind(forward_inside_kernel),
        [block],
        [band, laps],
        [("s", field_mix), ("v", ut), ("v", dt)],
        2.5,
        after=[inside_a],
    )
    keep, send = call(
        bind(fold_kernel),
        [(F + 1, K, 128)] * 2,
        [],
        [("v", parent_we), ("v", terrain_we), ("v", fy)],
        0.3,
    )
    first_bounds = swapped(send, nx // 2)
    if g.pair:
        (bsn,) = call(
            bind(side_bounds_kernel),
            [edge_shape],
            [(F, 128, 128)],
            [("v", sn_turned), ("v", fy), ("v", terrain_sn)],
            0.7,
        )
    else:
        bsn = bound_sn_general(g, parent_sn, terrain_sn)
    (sides,) = call(
        bind(side_spread_kernel), [block], [], [("s", relax_width), ("v", bsn)], 0.7
    )

    p1, q1, ma, mb, my, dwe, dsn = call(
        bind(adjoint_first_kernel),
        [block, block, row_shape, row_shape, lane_shape, edge_shape, edge_shape],
        [ramps],
        [
            ("s", relax_width),
            ("v", inside_a),
            ("v", at),
            ("v", dt),
            ("v", fa),
            ("v", fb),
            ("v", fy),
        ],
        3,
        after=[keep, sides],
    )
    (state,) = call(
        bind(join_kernel),
        [(2 * F + 1, K, 128)],
        [],
        [("v", dwe), ("v", keep), ("v", first_bounds)],
        0.1,
    )
    moved = swapped(state, 2)
    u1, ma, mb, my = call(
        bind(forward_first_kernel),
        [block, row_shape, row_shape, lane_shape],
        [ramps],
        [
            ("s", relax_width),
            ("v", inside_u),
            ("v", dt),
            ("v", fa),
            ("v", fb),
            ("v", fy),
            ("v", sides),
            ("v", ma),
            ("v", mb),
            ("v", my),
        ],
        2.5,
        {7: 1, 8: 2, 9: 3},
        after=[state],
    )
    if g.pair:
        gsn_own, my = call(
            bind(side_sums_kernel),
            [(F, X, 128), lane_shape],
            [(128, 128)],
            [("v", dsn), ("v", terrain_sn), ("v", my)],
            0.6,
            {2: 1},
        )
    else:
        gsn_own = dsn
    fy = to_y(my)
    fa = lax.ppermute(ma, "gx", evens)
    fb = lax.ppermute(mb, "gx", odds)

    state = add(state, moved, [gsn_own])
    distance = 4
    while distance < nx // 4:
        state = state + swapped(state, distance)
        distance *= 2
    moved = swapped(state, distance)
    (inside_a,) = call(
        bind(adjoint_inside_kernel, False),
        [block],
        [ramps, band, laps],
        [("s", relax_width), ("s", field_mix), ("v", p1), ("v", q1)],
        2.5,
        after=[state],
    )
    (inside_u,) = call(
        bind(forward_inside_kernel),
        [block],
        [band, laps],
        [("s", field_mix), ("v", u1), ("v", dt)],
        2.5,
        after=[inside_a],
    )
    sums, bounds = call(
        bind(split_kernel),
        [edge_shape, (F + 1, K, 128)],
        [],
        [("v", state), ("v", moved)],
        0.1,
        after=[inside_u],
    )
    other_bounds = swapped(bounds, 1)
    moved = swapped(sums, nx // 2)
    child_final, mark = call(
        bind(forward_last_kernel),
        [child_state.shape, (8, 128)],
        [(X + 4, 8, 128), ramps],
        [
            ("s", relax_width),
            ("s", field_mix),
            ("v", inside_u),
            ("v", dt),
            ("v", fa),
            ("v", fb),
            ("v", fy),
            ("v", sides),
            ("v", bounds),
            ("v", other_bounds),
        ],
        3,
    )
    sums = add(sums, moved, [mark])
    other_sums = swapped(sums, 1)
    grad_state, grad_sn = call(
        bind(adjoint_last_kernel),
        [child_state.shape, sn_turned.shape],
        [],
        [("v", inside_a), ("v", fa), ("v", fb), ("v", fy), ("v", gsn_own)],
        2.5,
        after=[sums],
    )
    (grad_we,) = call(
        bind(spread_kernel),
        [parent_we.shape],
        [],
        [("v", sums), ("v", other_sums), ("v", terrain_we)],
        0.7,
    )
    if g.pair:
        grad_sn = jnp.swapaxes(grad_sn, 2, 3)
    else:
        grad_sn = grad_sn_general(g, gsn_own, terrain_sn, parent_sn.shape[2])
    return (child_final, grad_state, grad_we, grad_sn)


def level_weights(g, terrain, span):
    first = lax.axis_index("gy") * span
    base = terrain[:, None, :] + jnp.arange(g.K, dtype=jnp.int32)[None, :, None]
    parent = first + jnp.arange(span, dtype=jnp.int32)
    return (parent[None, None, :, None] == base[:, :, None, :]).astype(f32)


def bound_sn_general(g, parent_sn, terrain_sn):
    weights = level_weights(g, terrain_sn, parent_sn.shape[2])
    bound = jnp.einsum("eflc,eklc->efkc", parent_sn, weights, precision=highest)
    bound = lax.psum(bound, "gy")
    mine = jnp.where(lax.axis_index("gy") < g.ny // 2, bound[0], bound[1])
    return jnp.pad(mine, ((0, 0), (0, 0), (0, 128 - g.X)))


def grad_sn_general(g, sums, terrain_sn, span):
    sums = sums[:, :, : g.X]
    south = lax.axis_index("gy") < g.ny // 2
    zero = jnp.zeros_like(sums)
    both = jnp.stack([jnp.where(south, sums, zero), jnp.where(south, zero, sums)])
    both = lax.psum(both, "gy")
    weights = level_weights(g, terrain_sn, span)
    return jnp.einsum("efkc,eklc->eflc", both, weights, precision=highest)


def solution(mesh):
    return jax.shard_map(
        body,
        mesh=mesh,
        in_specs=(
            P(None, None, "gx", "gy"),
            P(None, None, "gx", "gy"),
            P(None, "gx", "gy"),
            P(),
            P(None, None, "gx", "gy"),
            P(None, None, "gy", "gx"),
            P(None, "gy"),
            P(None, "gx"),
            P(),
        ),
        out_specs=(
            P(None, None, "gx", "gy"),
            P(None, None, "gx", "gy"),
            P(None, None, "gx", "gy"),
            P(None, None, "gy", "gx"),
        ),
        check_vma=False,
    )
```

```python
import functools

import jax
import jax.numpy as jnp
from jax import lax
from jax.experimental import pallas as pl
from jax.experimental.pallas import tpu as pltpu
from jax.sharding import PartitionSpec as P

near = 4.0 / 3.0
far = -1.0 / 12.0
coupling = 0.25
highest = lax.Precision.HIGHEST
f32 = jnp.float32
places = {
    "v": pl.BlockSpec(memory_space=pltpu.VMEM),
    "s": pl.BlockSpec(memory_space=pltpu.SMEM),
    "h": pl.BlockSpec(memory_space=pltpu.HBM),
    "a": pl.BlockSpec(memory_space=pl.ANY),
}
widest_zone = 15


class Geometry:
    def __init__(self, child, nx, ny):
        self.F, self.K, self.X, self.Y = child
        self.nx, self.ny = nx, ny
        self.tiles = self.K // 8
        assert self.K % 8 == 0 and self.Y == 128 and 4 * self.X <= 64
        assert self.X > widest_zone and self.Y > widest_zone
        assert self.X == 16
        assert nx >= 16 and nx & (nx - 1) == 0 and ny % 2 == 0
        assert 4 * self.F <= 128 and 128 % self.K == 0
        self.pair = ny == 2
        self.tall = self.K + self.X + 8


def lanes():
    return lax.broadcasted_iota(jnp.int32, (8, 128), 1)


def turn(values, shift):
    return pltpu.roll(values, shift % 128, values.ndim - 1)


def ramp(position, length, width):
    distance = jnp.minimum(position, length - 1 - position)
    inside = (position >= 0) & (position < length)
    top = jnp.where(inside, jnp.maximum(width - distance, 0), 0)
    bottom = jnp.full((8, 128), width + 1, jnp.int32)
    return jnp.broadcast_to(top, (8, 128)).astype(f32) / bottom.astype(f32)


def ramp_y(g, width):
    return ramp(lax.axis_index("gy") * g.Y + lanes(), g.ny * g.Y, width)


def ramp_x(g, width, x):
    return ramp(lax.axis_index("gx") * g.X + x, g.nx * g.X, width)


def fill_ramp_x(g, width, ref):
    for x in range(g.X):
        ref[x] = ramp_x(g, width, x)


def lap_masks():
    lane = lanes()
    zero = jnp.zeros((8, 128), f32)
    return (
        (1, jnp.where(lane > 0, near, zero)),
        (-1, jnp.where(lane < 127, near, zero)),
        (2, jnp.where(lane > 1, far, zero)),
        (-2, jnp.where(lane < 126, far, zero)),
    )


def fill_band(band):
    shape = (2 * 128, 128)
    row = lax.broadcasted_iota(jnp.int32, shape, 0) % 128
    gap = jnp.abs(row - lax.broadcasted_iota(jnp.int32, shape, 1))
    entry = jnp.where(gap == 0, -60.0, jnp.where(gap == 1, 16.0, jnp.where(gap == 2, -1.0, 0.0)))
    band[...] = entry.astype(jnp.bfloat16)


def along_lanes(values, band):
    high = values.astype(jnp.bfloat16)
    low = (values - high.astype(f32)).astype(jnp.bfloat16)
    return jnp.dot(
        jnp.concatenate([high, low], axis=1), band[...], preferred_element_type=f32
    )


def pack_lanes(x, base, values, packed):
    lane = lanes()
    start = base + 4 * x
    return jnp.where((lane >= start) & (lane < start + 4), turn(values, start + 2), packed)


def packed_message(packed):
    spot = lanes() % 4
    zero = jnp.zeros((8, 128), f32)
    low = far * turn(packed, -2) + jnp.where(spot == 1, near * turn(packed, -1), zero)
    high = far * turn(packed, 2) + jnp.where(spot == 2, near * turn(packed, 1), zero)
    return jnp.where(spot < 2, low, high)


def valid_lanes(g):
    at = lax.axis_index("gy")
    spot = lanes() % 4
    low = (at < g.ny - 1).astype(f32)
    high = (at > 0).astype(f32)
    return jnp.where(spot < 2, low, high)


def border():
    lane = lanes()
    return jnp.where((lane < 2) | (lane >= 126), 1.0, 0.0).astype(f32)


def unpack_lanes(x, base, packed, edge):
    return edge * turn(packed, -(base + 4 * x + 2))


def strided(ref, g, f, tile, x):
    start = (f * g.K + tile * 8) * g.X + x
    return ref.at[pl.ds(start, 8, stride=g.X), :]


def mix_table(mix, transposed):
    count = mix.shape[0]
    return [
        [
            (mix[h, f] if transposed else mix[f, h]) * coupling + (1.0 if f == h else 0.0)
            for h in range(count)
        ]
        for f in range(count)
    ]


def mixed(table, f, values):
    total = table[f][0] * values[0]
    for h in range(1, len(values)):
        total = total + table[f][h] * values[h]
    return total


def column_of(row):
    count = row.shape[1]
    wide = jnp.broadcast_to(row.astype(f32), (count, count))
    a = lax.broadcasted_iota(jnp.int32, (count, count), 0)
    b = lax.broadcasted_iota(jnp.int32, (count, count), 1)
    picked = jnp.sum(jnp.where(a == b, wide, 0.0), axis=1, keepdims=True)
    return jnp.broadcast_to(picked, (count, 128)).astype(jnp.int32)


def shift_levels(values, shift, sign):
    step = 1
    while step < 128:
        values = jnp.where((shift & step) != 0, turn(values, sign * step), values)
        step *= 2
    return values


def level_copies(g, pairs, sems, tile):
    levels = pl.ds(pl.multiple_of(tile * 8, 8), 8)
    copies = []
    for i, (source, target) in enumerate(pairs):
        at = (levels,) if len(source.shape) == 3 else (slice(None), levels)
        copies.append(pltpu.make_async_copy(source.at[at], target.at[at], sems.at[i, tile]))
    return copies


def rows_of(tile):
    return pl.ds(pl.multiple_of(tile * 8, 8), 8)


def odd_column():
    return lax.axis_index("gx") % 2 == 1


def send_ends(g, s, source, rows, ma, mb):
    odd = odd_column()
    for f in range(g.F):
        for j in range(2):
            low, high = source(f, j), source(f, g.X - 2 + j)
            ma[s, j, f, rows, :] = jnp.where(odd, low, high)
            mb[s, j, f, rows, :] = jnp.where(odd, high, low)


class Beyond:
    def __init__(self, g, s, fa, fb):
        self.g, self.s, self.fa, self.fb = g, s, fa, fb
        here = lax.axis_index("gx")
        self.odd = here % 2 == 1
        self.first, self.last = here == 0, here == g.nx - 1

    def left(self, j, f, rows):
        at = (self.s, j, f, rows, slice(None))
        value = jnp.where(self.odd, self.fa[at], self.fb[at])
        return jnp.where(self.first, jnp.zeros_like(value), value)

    def right(self, j, f, rows):
        at = (self.s, j, f, rows, slice(None))
        value = jnp.where(self.odd, self.fb[at], self.fa[at])
        return jnp.where(self.last, jnp.zeros_like(value), value)

    def columns(self, f, x, rows):
        last = self.g.X - 1
        if x == 0:
            return near * self.left(1, f, rows) + far * self.left(0, f, rows)
        if x == 1:
            return far * self.left(1, f, rows)
        if x == last - 1:
            return far * self.right(0, f, rows)
        if x == last:
            return near * self.right(0, f, rows) + far * self.right(1, f, rows)
        return None


class BeyondLanes:
    def __init__(self, g, s, fy):
        self.s, self.fy = s, fy
        self.edge = border()
        self.valid = valid_lanes(g)

    def tile(self, f, rows):
        return self.fy[f, rows, :] * self.valid

    def column(self, x, packed):
        return unpack_lanes(x, 64 * self.s, packed, self.edge)


def plus(value, more):
    return value if more is None else value + more


def lane_sums(vectors):
    lane = lanes()
    step = 1
    while len(vectors) > 1:
        low = (lane & step) == 0
        merged = []
        for a, b in zip(vectors[::2], vectors[1::2]):
            merged.append(jnp.where(low, a, b) + turn(jnp.where(low, b, a), step))
        vectors = merged
        step *= 2
    total = vectors[0]
    while step < 128:
        total = total + turn(total, step)
        step *= 2
    return total


def pack_kernel(
    g, relax, child_far, cot_far, diff_far, sn_far, parent_far, terrain_far,
    ut, at, dt, qt, ma, mb, my, rx, child, cot, diff, sn, parent, terrain, sems, side_sems,
):
    width = relax[0]
    pairs = ((diff_far, diff), (child_far, child), (cot_far, cot))
    for tile in range(g.tiles):
        for copy in level_copies(g, pairs, sems, tile):
            copy.start()
    side_copies = [
        pltpu.make_async_copy(source, target, side_sems.at[i])
        for i, (source, target) in enumerate(
            ((sn_far, sn), (parent_far, parent), (terrain_far, terrain))
        )
    ]
    for copy in side_copies:
        copy.start()
    fill_ramp_x(g, width, rx)
    open_y = 1.0 - ramp_y(g, width)
    child2 = child.reshape(g.F * g.K * g.X, g.Y)
    cot2 = cot.reshape(g.F * g.K * g.X, g.Y)
    diff2 = diff.reshape(g.K * g.X, g.Y)

    def tile_step(tile, carry):
        for copy in level_copies(g, pairs, sems, tile):
            copy.wait()
        rows = rows_of(tile)
        packed = [jnp.zeros((8, 128), f32) for _ in range(g.F)]
        for x in range(g.X):
            d = strided(diff2, g, 0, tile, x)[...]
            dt[x, rows, :] = d
            open_xy = open_y * (1.0 - rx[x])
            for f in range(g.F):
                u = strided(child2, g, f, tile, x)[...]
                a = strided(cot2, g, f, tile, x)[...]
                q = d * (open_xy * a)
                ut[f, x, rows, :] = u
                at[f, x, rows, :] = a
                qt[f, x, rows, :] = q
                packed[f] = pack_lanes(x, 0, u, packed[f])
                packed[f] = pack_lanes(x, 64, q, packed[f])
        for f in range(g.F):
            my[f, rows, :] = packed_message(packed[f])
        for s, source in enumerate((ut, qt)):
            send_ends(g, s, lambda f, x: source[f, x, rows, :], rows, ma, mb)
        return carry

    lax.fori_loop(0, g.tiles, tile_step, 0)
    for copy in side_copies:
        copy.wait()
    for f in range(g.F):
        my[f, g.K :, :] = jnp.zeros((g.X + 8, 128), f32)
    if g.pair:
        other = 1 - lax.axis_index("gy")
        for f in range(g.F):
            my[f, g.K : g.K + g.X, : sn.shape[3]] = sn[other, f]
    span = parent.shape[2]
    lane = lax.broadcasted_iota(jnp.int32, (span, 128), 1)
    for f in range(g.F):
        total = jnp.zeros((span, 128), f32)
        for e in range(2):
            heights = jnp.broadcast_to(terrain[e : e + 1, :].astype(f32), (span, 128))
            for spot, values in ((e, parent[e, f]), (2 + e, heights)):
                here = (lane >= 4 * spot) & (lane < 4 * spot + 4)
                total = jnp.where(here, turn(values, 4 * spot + 2), total)
        my[f, g.K + g.X : g.K + g.X + span, :] = total


def fill_laps(g, source, rows, band, laps):
    for f in range(g.F):
        cells = source[f, :, rows, :]
        parts = along_lanes(cells.reshape(8 * g.X, 128), band)
        for x in range(g.X):
            ones = [cells[x + i] for i in (-1, 1) if 0 <= x + i < g.X]
            twos = [cells[x + i] for i in (-2, 2) if 0 <= x + i < g.X]
            total = parts[8 * x : 8 * x + 8] + 16.0 * functools.reduce(jnp.add, ones)
            total = total - functools.reduce(jnp.add, twos)
            laps[f, x] = total * (1.0 / 12.0)


def adjoint_inside_kernel(g, scaled, relax, mix, ps, qs, fy, out, rx, band, laps):
    beyond = BeyondLanes(g, 1, fy)
    width = relax[0]
    table = mix_table(mix, True)
    fill_band(band)
    if scaled:
        fill_ramp_x(g, width, rx)
        open_y = 1.0 - ramp_y(g, width)

    def tile_step(tile, carry):
        rows = rows_of(tile)
        fill_laps(g, qs, rows, band, laps)
        halo = [beyond.tile(f, rows) for f in range(g.F)]
        for x in range(g.X):
            p = [ps[f, x, rows, :] for f in range(g.F)]
            if scaled:
                open_xy = open_y * (1.0 - rx[x])
                p = [open_xy * value for value in p]
            for f in range(g.F):
                out[f, x, rows, :] = mixed(table, f, p) + laps[f, x] + beyond.column(x, halo[f])
        return carry

    lax.fori_loop(0, g.tiles, tile_step, 0)


def forward_inside_kernel(g, mix, ut, dt, *rest):
    *fy, out, band, laps = rest
    table = mix_table(mix, False)
    fill_band(band)
    beyond = BeyondLanes(g, 0, fy[0]) if fy else None

    def tile_step(tile, carry):
        rows = rows_of(tile)
        fill_laps(g, ut, rows, band, laps)
        if fy:
            halo = [beyond.tile(f, rows) for f in range(g.F)]
        for x in range(g.X):
            u = [ut[f, x, rows, :] for f in range(g.F)]
            d = dt[x, rows, :]
            for f in range(g.F):
                lap = laps[f, x]
                if fy:
                    lap = lap + beyond.column(x, halo[f])
                out[f, x, rows, :] = mixed(table, f, u) + d * lap
        return carry

    lax.fori_loop(0, g.tiles, tile_step, 0)


def adjoint_first_kernel(
    g, relax, inside, at, dt, fa, fb, p1, q1, ma, mb, my, dwe, dsn, rx
):
    width = relax[0]
    fill_ramp_x(g, width, rx)
    slope_y = ramp_y(g, width)
    open_y = 1.0 - slope_y
    beyond = Beyond(g, 1, fa, fb)

    def tile_step(tile, carry):
        rows = rows_of(tile)
        for f in range(g.F):
            packed = jnp.zeros((8, 128), f32)
            share = jnp.zeros((8, 128), f32)
            pushes = []
            for x in range(g.X):
                slope_x = rx[x]
                open_xy = open_y * (1.0 - slope_x)
                middle = plus(inside[f, x, rows, :], beyond.columns(f, x, rows))
                carried = at[f, x, rows, :] + middle
                share = share + slope_x * carried
                pushes.append(slope_y * carried)
                pulled = open_xy * middle
                q = dt[x, rows, :] * pulled
                p1[f, x, rows, :] = pulled
                q1[f, x, rows, :] = q
                packed = pack_lanes(x, 64, q, packed)
            my[f, rows, :] = packed_message(packed)
            dsn[f, rows, :] = lane_sums(pushes)
            dwe[f, rows, :] = open_y * share
        send_ends(g, 1, lambda f, x: q1[f, x, rows, :], rows, ma, mb)
        return carry

    lax.fori_loop(0, g.tiles, tile_step, 0)
    for f in range(g.F):
        my[f, g.K :, :] = jnp.zeros((g.X + 8, 128), f32)


def forward_first_kernel(
    g, relax, inside, dt, fa, fb, fy, sides, ma_in, mb_in, my_in, u1, ma, mb, my, rx
):
    width = relax[0]
    fill_ramp_x(g, width, rx)
    open_y = 1.0 - ramp_y(g, width)
    beyond = Beyond(g, 0, fa, fb)
    beyond_lanes = BeyondLanes(g, 0, fy)
    lane = lanes()

    def tile_step(tile, carry):
        rows = rows_of(tile)
        for f in range(g.F):
            halo = beyond_lanes.tile(f, rows)
            packed = jnp.zeros((8, 128), f32)
            for x in range(g.X):
                open_xy = open_y * (1.0 - rx[x])
                lap = plus(beyond_lanes.column(x, halo), beyond.columns(f, x, rows))
                stepped = inside[f, x, rows, :] + dt[x, rows, :] * lap
                done = open_xy * stepped + sides[f, x, rows, :]
                u1[f, x, rows, :] = done
                packed = pack_lanes(x, 0, done, packed)
            my[f, rows, :] = jnp.where(lane < 64, packed_message(packed), my_in[f, rows, :])
        send_ends(g, 0, lambda f, x: u1[f, x, rows, :], rows, ma, mb)
        return carry

    lax.fori_loop(0, g.tiles, tile_step, 0)


def adjoint_last_kernel(g, inside, fa, fb, gsn_own, gsn_other, out, gsn, mark):
    mark[...] = jnp.zeros((8, 128), f32)
    out2 = out.reshape(g.F * g.K * g.X, g.Y)
    beyond = Beyond(g, 1, fa, fb)

    def tile_step(tile, carry):
        rows = rows_of(tile)
        for f in range(g.F):
            for x in range(g.X):
                value = plus(inside[f, x, rows, :], beyond.columns(f, x, rows))
                strided(out2, g, f, tile, x)[...] = value
        return carry

    lax.fori_loop(0, g.tiles, tile_step, 0)
    if g.pair:
        here = lax.axis_index("gy")
        span = gsn.shape[3]
        for f in range(g.F):
            gsn[here, f] = gsn_own[f, :, :span]
            gsn[1 - here, f] = gsn_other[f, :, :span]
    else:
        gsn[...] = jnp.zeros(gsn.shape, f32)


def forward_last_kernel(
    g, relax, mix, inside, dt, fa, fb, sides, kept, swapped, out, mark, rx, lx
):
    width = relax[0]
    mark[...] = jnp.zeros((8, 128), f32)
    for x in range(-2, g.X + 2):
        rx[x + 2] = ramp_x(g, width, x)
    for x in range(g.X):
        lap_x = near * (rx[x + 1] + rx[x + 3]) + far * (rx[x] + rx[x + 4]) - 5.0 * rx[x + 2]
        lx[x] = lap_x
    open_y = 1.0 - ramp_y(g, width)
    masks = lap_masks()
    table = mix_table(mix, False)
    beyond = Beyond(g, 0, fa, fb)
    edge, valid = border(), valid_lanes(g)
    out2 = out.reshape(g.F * g.K * g.X, g.Y)

    def tile_step(tile, carry):
        rows = rows_of(tile)
        bound = [
            open_y * (kept[f, rows, :] + swapped[f, rows, :]) for f in range(g.F)
        ]
        past = packed_message(kept[g.F, rows, :] + swapped[g.F, rows, :]) * valid
        for f in range(g.F):
            lap_y = unpack_lanes(f, 0, past, edge)
            for shift, mask in masks:
                lap_y = lap_y + mask * turn(bound[f], shift)
            mixed_bound = mixed(table, f, bound)
            for x in range(g.X):
                slope_x = rx[x + 2]
                open_xy = open_y * (1.0 - slope_x)
                lap = plus(slope_x * lap_y + lx[x] * bound[f], beyond.columns(f, x, rows))
                stepped = inside[f, x, rows, :] + slope_x * mixed_bound + dt[x, rows, :] * lap
                done = open_xy * stepped + slope_x * bound[f] + sides[f, x, rows, :]
                strided(out2, g, f, tile, x)[...] = done
        return carry

    lax.fori_loop(0, g.tiles, tile_step, 0)


def side_sums_kernel(g, dsn, tsn, gsn, sent, wide):
    here = lax.axis_index("gy")
    shift = column_of(jnp.where(here == 0, tsn[0:1, :], tsn[1:2, :]))
    lane = lax.broadcasted_iota(jnp.int32, (g.X, 128), 1)
    batch = 128 // g.K
    for first in range(0, g.F, batch):
        some = range(first, min(first + batch, g.F))
        for f in some:
            wide[(f - first) * g.K : (f - first + 1) * g.K, :] = dsn[f]
        turned = wide[...].T[: g.X]
        for f in some:
            levels = jnp.where(lane < g.K, turn(turned, -(f - first) * g.K), 0.0)
            whole = shift_levels(levels, shift, 1)
            moved = turn(whole, 64)
            gsn[f] = jnp.where(here == 0, whole, moved)
            sent[f] = jnp.where(here == 0, moved, whole)


def side_bounds_kernel(g, sn, fsn, tsn, bsn, wide):
    here = lax.axis_index("gy")
    shift = column_of(jnp.where(here == 0, tsn[0:1, :], tsn[1:2, :]))
    span = sn.shape[3]
    wide[...] = jnp.zeros(wide.shape, f32)
    for f in range(g.F):
        wide[f, : g.X, :span] = sn[here, f]
        mine = wide[f, : g.X, :]
        theirs = fsn[f, g.K : g.K + g.X, :]
        whole = jnp.where(here == 0, mine, theirs) + turn(
            jnp.where(here == 0, theirs, mine), 64
        )
        wide[f, : g.X, :] = shift_levels(whole, shift, -1)
        bsn[f] = wide[f].T[: g.K]


def side_spread_kernel(g, relax, bsn, out):
    slope_y = ramp_y(g, relax[0])

    def tile_step(tile, carry):
        rows = rows_of(tile)
        for f in range(g.F):
            bounds = bsn[f, rows, :]
            for x in range(g.X):
                out[f, x, rows, :] = slope_y * jnp.broadcast_to(bounds[:, x : x + 1], (8, 128))
        return carry

    lax.fori_loop(0, g.tiles, tile_step, 0)


def fold_rows(values, base, first, count):
    level = lax.broadcasted_iota(jnp.int32, (count, 128), 0) + base - first
    total = jnp.zeros((count, 128), f32)
    for j in range(values.shape[0]):
        row = jnp.broadcast_to(values[j : j + 1, :], (count, 128))
        total = jnp.where(level == j, row, total)
    return total


def fold_kernel(g, parent, terrain, fy, keep, send):
    here = lax.axis_index("gx")
    odd = here >= g.nx // 2
    span = parent.shape[2]
    first = here * span
    lane = lax.broadcasted_iota(jnp.int32, (span, 128), 1)
    top = g.K + g.X
    parts = []
    for e in range(2):
        part = [fold_rows(parent[e, f], terrain[e : e + 1, :], first, g.K) for f in range(g.F)]
        values = jnp.zeros((span, 128), f32)
        heights = jnp.zeros((span, 128), f32)
        for f in range(g.F):
            spots = (lane >= 4 * f) & (lane < 4 * f + 4)
            rows = fy[f, top : top + span, :]
            values = jnp.where(spots, turn(rows, 4 * f - 4 * e), values)
            heights = jnp.where(spots, turn(rows, 4 * f - 8 - 4 * e), heights)
        part.append(fold_rows(values, heights[0:1, :].astype(jnp.int32), first, g.K))
        parts.append(part)
    for i in range(g.F + 1):
        keep[i] = jnp.where(odd, parts[1][i], parts[0][i])
        send[i] = jnp.where(odd, parts[0][i], parts[1][i])


def join_kernel(g, sums, bounds, more_bounds, out):
    for f in range(g.F):
        out[f] = sums[f]
    for f in range(g.F + 1):
        out[g.F + f] = bounds[f] + more_bounds[f]


def split_kernel(g, state, moved, sums, bounds):
    for f in range(g.F):
        sums[f] = state[f] + moved[f]
    for f in range(g.F + 1):
        bounds[f] = state[g.F + f] + moved[g.F + f]


def add_kernel(g, first, second, out):
    out[...] = first[...] + second[...]


def spread_kernel(g, kept, swapped, terrain, out):
    here = lax.axis_index("gx")
    odd = here % 2
    span = out.shape[2]
    row = lax.broadcasted_iota(jnp.int32, (8, 128), 0)
    zero = jnp.zeros((8, 128), f32)
    for e in range(2):
        start = jnp.broadcast_to(here * span - terrain[e : e + 1, :], (8, 128)) + 8
        inside = (start > 0) & (start < g.K + 8)
        tile, rest = start >> 3, start & 7
        for f in range(g.F):
            chosen = jnp.where(odd == e, kept[f], swapped[f])
            tiles = [zero] + [chosen[8 * i : 8 * i + 8] for i in range(g.tiles)] + [zero]
            low, high = zero, zero
            for i in range(g.tiles + 1):
                low = jnp.where(tile == i, tiles[i], low)
                high = jnp.where(tile == i, tiles[i + 1], high)
            for step in (4, 2, 1):
                moves = (rest & step) != 0
                up_low = pltpu.roll(low, 8 - step, 0)
                up_high = pltpu.roll(high, 8 - step, 0)
                low = jnp.where(moves, jnp.where(row < 8 - step, up_low, up_high), low)
                high = jnp.where(moves, up_high, high)
            out[e, f] = jnp.where(inside, low, zero)[:span]


def call(kernel, outs, scratch, ins, time, aliases=None, after=()):
    count = len(ins)
    ins = ins + [("a", value) for value in after]

    def run(*refs):
        kernel(*refs[:count], *refs[len(ins) :])

    out_shape = [jax.ShapeDtypeStruct(s, f32) for s in outs]
    size = 4 * sum(functools.reduce(lambda a, b: a * b, s) for s in outs)
    return pl.pallas_call(
        run,
        out_shape=out_shape,
        in_specs=[places[where] for where, _ in ins],
        out_specs=[places["v"]] * len(outs),
        scratch_shapes=[pltpu.VMEM(s, f32) if isinstance(s, tuple) else s for s in scratch],
        input_output_aliases=aliases or {},
        compiler_params=pltpu.CompilerParams(vmem_limit_bytes=24 * 1024 * 1024),
        cost_estimate=pl.CostEstimate(flops=int(time * 1.1e9), bytes_accessed=2 * size, transcendentals=0),
    )(*[pltpu.with_memory_space_constraint(v, pltpu.HBM) if w == "h" else v for w, v in ins])


def body(
    child_state,
    cotangent,
    diffusivity,
    field_mix,
    parent_we,
    parent_sn,
    terrain_we,
    terrain_sn,
    relax_width,
):
    nx, ny = lax.axis_size("gx"), lax.axis_size("gy")
    g = Geometry(child_state.shape, nx, ny)
    F, K, X, Y = child_state.shape
    evens = [(i, i ^ 1) for i in range(nx)]
    odds = [(i, (((i + 1) ^ 1) - 1) % nx) for i in range(nx)]
    block = (F, X, K, 128)
    row_shape = (2, 2, F, K, 128)
    lane_shape = (F, g.tall, 128)
    edge_shape = (F, K, 128)
    ramps = (X, 8, 128)
    band = pltpu.VMEM((256, 128), jnp.bfloat16)
    laps = (F, X, 8, 128)

    def bind(kernel, *args):
        return functools.partial(kernel, g, *args)

    def swapped(values, distance):
        return lax.ppermute(values, "gx", [(i, i ^ distance) for i in range(nx)])

    def to_y(message):
        if g.pair:
            return lax.ppermute(message, "gy", [(0, 1), (1, 0)])
        up = lax.ppermute(message, "gy", [(i, i + 1) for i in range(ny - 1)])
        down = lax.ppermute(message, "gy", [(i + 1, i) for i in range(ny - 1)])
        low = (jnp.arange(128, dtype=jnp.int32) % 4 < 2)[None, None, :]
        rows = (jnp.arange(g.tall, dtype=jnp.int32) < K)[None, :, None]
        return jnp.where(low == rows, down, up)

    def add(first, second, after):
        (total,) = call(
            bind(add_kernel), [first.shape], [], [("v", first), ("v", second)], 0.1, after=after
        )
        return total

    sn_turned = jnp.swapaxes(parent_sn, 2, 3)
    ut, at, dt, qt, ma, mb, my = call(
        bind(pack_kernel),
        [block, block, (X, K, 128), block, row_shape, row_shape, lane_shape],
        [
            ramps,
            child_state.shape,
            child_state.shape,
            diffusivity.shape,
            sn_turned.shape,
            parent_we.shape,
            pltpu.VMEM(terrain_we.shape, jnp.int32),
            pltpu.SemaphoreType.DMA((3, g.tiles)),
            pltpu.SemaphoreType.DMA((3,)),
        ],
        [
            ("s", relax_width),
            ("h", child_state),
            ("h", cotangent),
            ("h", diffusivity),
            ("h", sn_turned),
            ("h", parent_we),
            ("h", terrain_we),
        ],
        3,
    )
    fy = to_y(my)
    fa = lax.ppermute(ma, "gx", evens)
    fb = lax.ppermute(mb, "gx", odds)

    (inside_u,) = call(
        bind(forward_inside_kernel),
        [block],
        [band, laps],
        [("s", field_mix), ("v", ut), ("v", dt)],
        2.5,
    )
    (inside_a,) = call(
        bind(adjoint_inside_kernel, True),
        [block],
        [ramps, band, laps],
        [("s", relax_width), ("s", field_mix), ("v", at), ("v", qt), ("v", fy)],
        2.5,
        after=[inside_u],
    )
    keep, send = call(
        bind(fold_kernel),
        [(F + 1, K, 128)] * 2,
        [],
        [("v", parent_we), ("v", terrain_we), ("v", fy)],
        0.3,
    )
    first_bounds = swapped(send, nx // 2)
    if g.pair:
        (bsn,) = call(
            bind(side_bounds_kernel),
            [edge_shape],
            [(F, 128, 128)],
            [("v", sn_turned), ("v", fy), ("v", terrain_sn)],
            0.7,
        )
    else:
        bsn = bound_sn_general(g, parent_sn, terrain_sn)
    (sides,) = call(
        bind(side_spread_kernel), [block], [], [("s", relax_width), ("v", bsn)], 0.7
    )

    p1, q1, ma, mb, my, dwe, dsn = call(
        bind(adjoint_first_kernel),
        [block, block, row_shape, row_shape, lane_shape, edge_shape, edge_shape],
        [ramps],
        [
            ("s", relax_width),
            ("v", inside_a),
            ("v", at),
            ("v", dt),
            ("v", fa),
            ("v", fb),
        ],
        3,
        after=[keep, sides],
    )
    (state,) = call(
        bind(join_kernel),
        [(2 * F + 1, K, 128)],
        [],
        [("v", dwe), ("v", keep), ("v", first_bounds)],
        0.1,
    )
    moved = swapped(state, 2)
    u1, ma, mb, my = call(
        bind(forward_first_kernel),
        [block, row_shape, row_shape, lane_shape],
        [ramps],
        [
            ("s", relax_width),
            ("v", inside_u),
            ("v", dt),
            ("v", fa),
            ("v", fb),
            ("v", fy),
            ("v", sides),
            ("v", ma),
            ("v", mb),
            ("v", my),
        ],
        2.5,
        {7: 1, 8: 2, 9: 3},
        after=[state],
    )
    fy = to_y(my)
    fa = lax.ppermute(ma, "gx", evens)
    fb = lax.ppermute(mb, "gx", odds)

    state = add(state, moved, [u1])
    gsn_own = gsn_other = dsn
    if g.pair:
        gsn_own, sent = call(
            bind(side_sums_kernel),
            [(F, X, 128)] * 2,
            [(128, 128)],
            [("v", dsn), ("v", terrain_sn)],
            0.6,
            after=[state],
        )
        gsn_other = lax.ppermute(sent, "gy", [(0, 1), (1, 0)])
    distance = 4
    while distance < nx // 4:
        state = state + swapped(state, distance)
        distance *= 2
    moved = swapped(state, distance)
    (inside_a,) = call(
        bind(adjoint_inside_kernel, False),
        [block],
        [ramps, band, laps],
        [("s", relax_width), ("s", field_mix), ("v", p1), ("v", q1), ("v", fy)],
        2.5,
        after=[state],
    )
    (inside_u,) = call(
        bind(forward_inside_kernel),
        [block],
        [band, laps],
        [("s", field_mix), ("v", u1), ("v", dt), ("v", fy)],
        2.5,
        after=[inside_a],
    )
    grad_state, grad_sn, early = call(
        bind(adjoint_last_kernel),
        [child_state.shape, sn_turned.shape, (8, 128)],
        [],
        [("v", inside_a), ("v", fa), ("v", fb), ("v", gsn_own), ("v", gsn_other)],
        2.5,
        after=[inside_u],
    )
    sums, bounds = call(
        bind(split_kernel),
        [edge_shape, (F + 1, K, 128)],
        [],
        [("v", state), ("v", moved)],
        0.1,
        after=[early],
    )
    other_bounds = swapped(bounds, 1)
    moved = swapped(sums, nx // 2)
    child_final, mark = call(
        bind(forward_last_kernel),
        [child_state.shape, (8, 128)],
        [(X + 4, 8, 128), ramps],
        [
            ("s", relax_width),
            ("s", field_mix),
            ("v", inside_u),
            ("v", dt),
            ("v", fa),
            ("v", fb),
            ("v", sides),
            ("v", bounds),
            ("v", other_bounds),
        ],
        3,
    )
    sums = add(sums, moved, [mark])
    other_sums = swapped(sums, 1)
    (grad_we,) = call(
        bind(spread_kernel),
        [parent_we.shape],
        [],
        [("v", sums), ("v", other_sums), ("v", terrain_we)],
        0.7,
    )
    if g.pair:
        grad_sn = jnp.swapaxes(grad_sn, 2, 3)
    else:
        grad_sn = grad_sn_general(g, gsn_own, terrain_sn, parent_sn.shape[2])
    return (child_final, grad_state, grad_we, grad_sn)


def level_weights(g, terrain, span):
    first = lax.axis_index("gy") * span
    base = terrain[:, None, :] + jnp.arange(g.K, dtype=jnp.int32)[None, :, None]
    parent = first + jnp.arange(span, dtype=jnp.int32)
    return (parent[None, None, :, None] == base[:, :, None, :]).astype(f32)


def bound_sn_general(g, parent_sn, terrain_sn):
    weights = level_weights(g, terrain_sn, parent_sn.shape[2])
    bound = jnp.einsum("eflc,eklc->efkc", parent_sn, weights, precision=highest)
    bound = lax.psum(bound, "gy")
    mine = jnp.where(lax.axis_index("gy") < g.ny // 2, bound[0], bound[1])
    return jnp.pad(mine, ((0, 0), (0, 0), (0, 128 - g.X)))


def grad_sn_general(g, sums, terrain_sn, span):
    sums = sums[:, :, : g.X]
    south = lax.axis_index("gy") < g.ny // 2
    zero = jnp.zeros_like(sums)
    both = jnp.stack([jnp.where(south, sums, zero), jnp.where(south, zero, sums)])
    both = lax.psum(both, "gy")
    weights = level_weights(g, terrain_sn, span)
    return jnp.einsum("efkc,eklc->eflc", both, weights, precision=highest)


def solution(mesh):
    return jax.shard_map(
        body,
        mesh=mesh,
        in_specs=(
            P(None, None, "gx", "gy"),
            P(None, None, "gx", "gy"),
            P(None, "gx", "gy"),
            P(),
            P(None, None, "gx", "gy"),
            P(None, None, "gy", "gx"),
            P(None, "gy"),
            P(None, "gx"),
            P(),
        ),
        out_specs=(
            P(None, None, "gx", "gy"),
            P(None, None, "gx", "gy"),
            P(None, None, "gx", "gy"),
            P(None, None, "gy", "gx"),
        ),
        check_vma=False,
    )
```

```python
import functools

import jax
import jax.numpy as jnp
from jax import lax
from jax.experimental import pallas as pl
from jax.experimental.pallas import tpu as pltpu
from jax.sharding import PartitionSpec as P

near = 4.0 / 3.0
far = -1.0 / 12.0
coupling = 0.25
highest = lax.Precision.HIGHEST
f32 = jnp.float32
places = {
    "v": pl.BlockSpec(memory_space=pltpu.VMEM),
    "s": pl.BlockSpec(memory_space=pltpu.SMEM),
    "h": pl.BlockSpec(memory_space=pltpu.HBM),
    "a": pl.BlockSpec(memory_space=pl.ANY),
}
widest_zone = 15


class Geometry:
    def __init__(self, child, nx, ny):
        self.F, self.K, self.X, self.Y = child
        self.nx, self.ny = nx, ny
        self.tiles = self.K // 8
        assert self.K % 8 == 0 and self.Y == 128 and 4 * self.X <= 64
        assert self.X > widest_zone and self.Y > widest_zone
        assert self.X == 16
        assert nx >= 16 and nx & (nx - 1) == 0 and ny % 2 == 0
        assert 4 * self.F <= 128 and 128 % self.K == 0
        self.pair = ny == 2
        self.tall = self.K + self.X + 8


def lanes():
    return lax.broadcasted_iota(jnp.int32, (8, 128), 1)


def turn(values, shift):
    return pltpu.roll(values, shift % 128, values.ndim - 1)


def ramp(position, length, width):
    distance = jnp.minimum(position, length - 1 - position)
    inside = (position >= 0) & (position < length)
    top = jnp.where(inside, jnp.maximum(width - distance, 0), 0)
    bottom = jnp.full((8, 128), width + 1, jnp.int32)
    return jnp.broadcast_to(top, (8, 128)).astype(f32) / bottom.astype(f32)


def ramp_y(g, width):
    return ramp(lax.axis_index("gy") * g.Y + lanes(), g.ny * g.Y, width)


def ramp_x(g, width, x):
    return ramp(lax.axis_index("gx") * g.X + x, g.nx * g.X, width)


def fill_ramp_x(g, width, ref):
    for x in range(g.X):
        ref[x] = ramp_x(g, width, x)


def lap_masks():
    lane = lanes()
    zero = jnp.zeros((8, 128), f32)
    return (
        (1, jnp.where(lane > 0, near, zero)),
        (-1, jnp.where(lane < 127, near, zero)),
        (2, jnp.where(lane > 1, far, zero)),
        (-2, jnp.where(lane < 126, far, zero)),
    )


def fill_band(band):
    shape = (2 * 128, 128)
    row = lax.broadcasted_iota(jnp.int32, shape, 0) % 128
    gap = jnp.abs(row - lax.broadcasted_iota(jnp.int32, shape, 1))
    entry = jnp.where(gap == 0, -60.0, jnp.where(gap == 1, 16.0, jnp.where(gap == 2, -1.0, 0.0)))
    band[...] = entry.astype(jnp.bfloat16)


def along_lanes(values, band):
    high = values.astype(jnp.bfloat16)
    low = (values - high.astype(f32)).astype(jnp.bfloat16)
    return jnp.dot(
        jnp.concatenate([high, low], axis=1), band[...], preferred_element_type=f32
    )


def pack_lanes(x, base, values, packed):
    lane = lanes()
    start = base + 4 * x
    return jnp.where((lane >= start) & (lane < start + 4), turn(values, start + 2), packed)


def packed_message(packed):
    spot = lanes() % 4
    zero = jnp.zeros((8, 128), f32)
    low = far * turn(packed, -2) + jnp.where(spot == 1, near * turn(packed, -1), zero)
    high = far * turn(packed, 2) + jnp.where(spot == 2, near * turn(packed, 1), zero)
    return jnp.where(spot < 2, low, high)


def valid_lanes(g):
    at = lax.axis_index("gy")
    spot = lanes() % 4
    low = (at < g.ny - 1).astype(f32)
    high = (at > 0).astype(f32)
    return jnp.where(spot < 2, low, high)


def border():
    lane = lanes()
    return jnp.where((lane < 2) | (lane >= 126), 1.0, 0.0).astype(f32)


def unpack_lanes(x, base, packed, edge):
    return edge * turn(packed, -(base + 4 * x + 2))


def strided(ref, g, f, tile, x):
    start = (f * g.K + tile * 8) * g.X + x
    return ref.at[pl.ds(start, 8, stride=g.X), :]


def mix_table(mix, transposed):
    count = mix.shape[0]
    return [
        [
            (mix[h, f] if transposed else mix[f, h]) * coupling + (1.0 if f == h else 0.0)
            for h in range(count)
        ]
        for f in range(count)
    ]


def mixed(table, f, values):
    total = table[f][0] * values[0]
    for h in range(1, len(values)):
        total = total + table[f][h] * values[h]
    return total


def column_of(row):
    count = row.shape[1]
    wide = jnp.broadcast_to(row.astype(f32), (count, count))
    a = lax.broadcasted_iota(jnp.int32, (count, count), 0)
    b = lax.broadcasted_iota(jnp.int32, (count, count), 1)
    picked = jnp.sum(jnp.where(a == b, wide, 0.0), axis=1, keepdims=True)
    return jnp.broadcast_to(picked, (count, 128)).astype(jnp.int32)


def shift_levels(values, shift, sign):
    step = 1
    while step < 128:
        values = jnp.where((shift & step) != 0, turn(values, sign * step), values)
        step *= 2
    return values


def level_copies(g, pairs, sems, tile):
    levels = pl.ds(pl.multiple_of(tile * 8, 8), 8)
    copies = []
    for i, (source, target) in enumerate(pairs):
        at = (levels,) if len(source.shape) == 3 else (slice(None), levels)
        copies.append(pltpu.make_async_copy(source.at[at], target.at[at], sems.at[i, tile]))
    return copies


def rows_of(tile):
    return pl.ds(pl.multiple_of(tile * 8, 8), 8)


def odd_column():
    return lax.axis_index("gx") % 2 == 1


def send_ends(g, s, source, rows, ma, mb):
    odd = odd_column()
    for f in range(g.F):
        for j in range(2):
            low, high = source(f, j), source(f, g.X - 2 + j)
            ma[s, j, f, rows, :] = jnp.where(odd, low, high)
            mb[s, j, f, rows, :] = jnp.where(odd, high, low)


class Beyond:
    def __init__(self, g, s, fa, fb):
        self.g, self.s, self.fa, self.fb = g, s, fa, fb
        here = lax.axis_index("gx")
        self.odd = here % 2 == 1
        self.first, self.last = here == 0, here == g.nx - 1

    def left(self, j, f, rows):
        at = (self.s, j, f, rows, slice(None))
        value = jnp.where(self.odd, self.fa[at], self.fb[at])
        return jnp.where(self.first, jnp.zeros_like(value), value)

    def right(self, j, f, rows):
        at = (self.s, j, f, rows, slice(None))
        value = jnp.where(self.odd, self.fb[at], self.fa[at])
        return jnp.where(self.last, jnp.zeros_like(value), value)

    def columns(self, f, x, rows):
        last = self.g.X - 1
        if x == 0:
            return near * self.left(1, f, rows) + far * self.left(0, f, rows)
        if x == 1:
            return far * self.left(1, f, rows)
        if x == last - 1:
            return far * self.right(0, f, rows)
        if x == last:
            return near * self.right(0, f, rows) + far * self.right(1, f, rows)
        return None


class BeyondLanes:
    def __init__(self, g, s, fy):
        self.s, self.fy = s, fy
        self.edge = border()
        self.valid = valid_lanes(g)

    def tile(self, f, rows):
        return self.fy[f, rows, :] * self.valid

    def column(self, x, packed):
        return unpack_lanes(x, 64 * self.s, packed, self.edge)


def plus(value, more):
    return value if more is None else value + more


def lane_sums(vectors):
    lane = lanes()
    step = 1
    while len(vectors) > 1:
        low = (lane & step) == 0
        merged = []
        for a, b in zip(vectors[::2], vectors[1::2]):
            merged.append(jnp.where(low, a, b) + turn(jnp.where(low, b, a), step))
        vectors = merged
        step *= 2
    total = vectors[0]
    while step < 128:
        total = total + turn(total, step)
        step *= 2
    return total


def pack_kernel(
    g, relax, child_far, cot_far, diff_far, sn_far, parent_far, terrain_far,
    ut, at, dt, qt, ma, mb, my, rx, child, cot, diff, sn, parent, terrain, sems, side_sems,
):
    width = relax[0]
    pairs = ((diff_far, diff), (child_far, child), (cot_far, cot))
    for tile in range(g.tiles):
        for copy in level_copies(g, pairs, sems, tile):
            copy.start()
    side_copies = [
        pltpu.make_async_copy(source, target, side_sems.at[i])
        for i, (source, target) in enumerate(
            ((sn_far, sn), (parent_far, parent), (terrain_far, terrain))
        )
    ]
    for copy in side_copies:
        copy.start()
    fill_ramp_x(g, width, rx)
    open_y = 1.0 - ramp_y(g, width)
    child2 = child.reshape(g.F * g.K * g.X, g.Y)
    cot2 = cot.reshape(g.F * g.K * g.X, g.Y)
    diff2 = diff.reshape(g.K * g.X, g.Y)

    def tile_step(tile, carry):
        for copy in level_copies(g, pairs, sems, tile):
            copy.wait()
        rows = rows_of(tile)
        packed = [jnp.zeros((8, 128), f32) for _ in range(g.F)]
        for x in range(g.X):
            d = strided(diff2, g, 0, tile, x)[...]
            dt[x, rows, :] = d
            open_xy = open_y * (1.0 - rx[x])
            for f in range(g.F):
                u = strided(child2, g, f, tile, x)[...]
                a = strided(cot2, g, f, tile, x)[...]
                q = d * (open_xy * a)
                ut[f, x, rows, :] = u
                at[f, x, rows, :] = a
                qt[f, x, rows, :] = q
                packed[f] = pack_lanes(x, 0, u, packed[f])
                packed[f] = pack_lanes(x, 64, q, packed[f])
        for f in range(g.F):
            my[f, rows, :] = packed_message(packed[f])
        for s, source in enumerate((ut, qt)):
            send_ends(g, s, lambda f, x: source[f, x, rows, :], rows, ma, mb)
        return carry

    lax.fori_loop(0, g.tiles, tile_step, 0)
    for copy in side_copies:
        copy.wait()
    for f in range(g.F):
        my[f, g.K :, :] = jnp.zeros((g.X + 8, 128), f32)
    if g.pair:
        other = 1 - lax.axis_index("gy")
        for f in range(g.F):
            my[f, g.K : g.K + g.X, : sn.shape[3]] = sn[other, f]
    span = parent.shape[2]
    lane = lax.broadcasted_iota(jnp.int32, (span, 128), 1)
    for f in range(g.F):
        total = jnp.zeros((span, 128), f32)
        for e in range(2):
            heights = jnp.broadcast_to(terrain[e : e + 1, :].astype(f32), (span, 128))
            for spot, values in ((e, parent[e, f]), (2 + e, heights)):
                here = (lane >= 4 * spot) & (lane < 4 * spot + 4)
                total = jnp.where(here, turn(values, 4 * spot + 2), total)
        my[f, g.K + g.X : g.K + g.X + span, :] = total


def fill_laps(g, source, rows, band, laps):
    for f in range(g.F):
        cells = source[f, :, rows, :]
        parts = along_lanes(cells.reshape(8 * g.X, 128), band)
        for x in range(g.X):
            ones = [cells[x + i] for i in (-1, 1) if 0 <= x + i < g.X]
            twos = [cells[x + i] for i in (-2, 2) if 0 <= x + i < g.X]
            total = parts[8 * x : 8 * x + 8] + 16.0 * functools.reduce(jnp.add, ones)
            total = total - functools.reduce(jnp.add, twos)
            laps[f, x] = total * (1.0 / 12.0)


def adjoint_inside_kernel(g, scaled, relax, mix, ps, qs, fy, out, rx, band, laps):
    beyond = BeyondLanes(g, 1, fy)
    width = relax[0]
    table = mix_table(mix, True)
    fill_band(band)
    if scaled:
        fill_ramp_x(g, width, rx)
        open_y = 1.0 - ramp_y(g, width)

    def tile_step(tile, carry):
        rows = rows_of(tile)
        fill_laps(g, qs, rows, band, laps)
        halo = [beyond.tile(f, rows) for f in range(g.F)]
        for x in range(g.X):
            p = [ps[f, x, rows, :] for f in range(g.F)]
            if scaled:
                open_xy = open_y * (1.0 - rx[x])
                p = [open_xy * value for value in p]
            for f in range(g.F):
                out[f, x, rows, :] = mixed(table, f, p) + laps[f, x] + beyond.column(x, halo[f])
        return carry

    lax.fori_loop(0, g.tiles, tile_step, 0)


def forward_inside_kernel(g, mix, ut, dt, *rest):
    *fy, out, band, laps = rest
    table = mix_table(mix, False)
    fill_band(band)
    beyond = BeyondLanes(g, 0, fy[0]) if fy else None

    def tile_step(tile, carry):
        rows = rows_of(tile)
        fill_laps(g, ut, rows, band, laps)
        if fy:
            halo = [beyond.tile(f, rows) for f in range(g.F)]
        for x in range(g.X):
            u = [ut[f, x, rows, :] for f in range(g.F)]
            d = dt[x, rows, :]
            for f in range(g.F):
                lap = laps[f, x]
                if fy:
                    lap = lap + beyond.column(x, halo[f])
                out[f, x, rows, :] = mixed(table, f, u) + d * lap
        return carry

    lax.fori_loop(0, g.tiles, tile_step, 0)


def adjoint_first_kernel(
    g, relax, inside, at, dt, fa, fb, p1, q1, ma, mb, my, dwe, dsn, rx
):
    width = relax[0]
    fill_ramp_x(g, width, rx)
    slope_y = ramp_y(g, width)
    open_y = 1.0 - slope_y
    beyond = Beyond(g, 1, fa, fb)

    def tile_step(tile, carry):
        rows = rows_of(tile)
        for f in range(g.F):
            packed = jnp.zeros((8, 128), f32)
            share = jnp.zeros((8, 128), f32)
            pushes = []
            for x in range(g.X):
                slope_x = rx[x]
                open_xy = open_y * (1.0 - slope_x)
                middle = plus(inside[f, x, rows, :], beyond.columns(f, x, rows))
                carried = at[f, x, rows, :] + middle
                share = share + slope_x * carried
                pushes.append(slope_y * carried)
                pulled = open_xy * middle
                q = dt[x, rows, :] * pulled
                p1[f, x, rows, :] = pulled
                q1[f, x, rows, :] = q
                packed = pack_lanes(x, 64, q, packed)
            my[f, rows, :] = packed_message(packed)
            dsn[f, rows, :] = lane_sums(pushes)
            dwe[f, rows, :] = open_y * share
        send_ends(g, 1, lambda f, x: q1[f, x, rows, :], rows, ma, mb)
        return carry

    lax.fori_loop(0, g.tiles, tile_step, 0)
    for f in range(g.F):
        my[f, g.K :, :] = jnp.zeros((g.X + 8, 128), f32)


def forward_first_kernel(
    g, relax, inside, dt, fa, fb, fy, sides, ma_in, mb_in, my_in, u1, ma, mb, my, rx
):
    width = relax[0]
    fill_ramp_x(g, width, rx)
    open_y = 1.0 - ramp_y(g, width)
    beyond = Beyond(g, 0, fa, fb)
    beyond_lanes = BeyondLanes(g, 0, fy)
    lane = lanes()

    def tile_step(tile, carry):
        rows = rows_of(tile)
        halo = [beyond_lanes.tile(f, rows) for f in range(g.F)]
        packed = [jnp.zeros((8, 128), f32) for _ in range(g.F)]
        for x in range(g.X):
            open_xy = open_y * (1.0 - rx[x])
            d = dt[x, rows, :]
            for f in range(g.F):
                lap = plus(beyond_lanes.column(x, halo[f]), beyond.columns(f, x, rows))
                stepped = inside[f, x, rows, :] + d * lap
                done = open_xy * stepped + sides[f, x, rows, :]
                u1[f, x, rows, :] = done
                packed[f] = pack_lanes(x, 0, done, packed[f])
        for f in range(g.F):
            my[f, rows, :] = jnp.where(lane < 64, packed_message(packed[f]), my_in[f, rows, :])
        send_ends(g, 0, lambda f, x: u1[f, x, rows, :], rows, ma, mb)
        return carry

    lax.fori_loop(0, g.tiles, tile_step, 0)


def adjoint_last_kernel(g, inside, fa, fb, gsn_own, gsn_other, out, gsn, mark):
    mark[...] = jnp.zeros((8, 128), f32)
    out2 = out.reshape(g.F * g.K * g.X, g.Y)
    beyond = Beyond(g, 1, fa, fb)

    def tile_step(tile, carry):
        rows = rows_of(tile)
        for f in range(g.F):
            for x in range(g.X):
                value = plus(inside[f, x, rows, :], beyond.columns(f, x, rows))
                strided(out2, g, f, tile, x)[...] = value
        return carry

    lax.fori_loop(0, g.tiles, tile_step, 0)
    if g.pair:
        here = lax.axis_index("gy")
        span = gsn.shape[3]
        for f in range(g.F):
            gsn[here, f] = gsn_own[f, :, :span]
            gsn[1 - here, f] = gsn_other[f, :, :span]
    else:
        gsn[...] = jnp.zeros(gsn.shape, f32)


def forward_last_kernel(
    g, relax, mix, inside, dt, fa, fb, sides, kept, swapped, out, mark, rx, lx
):
    width = relax[0]
    mark[...] = jnp.zeros((8, 128), f32)
    for x in range(-2, g.X + 2):
        rx[x + 2] = ramp_x(g, width, x)
    for x in range(g.X):
        lap_x = near * (rx[x + 1] + rx[x + 3]) + far * (rx[x] + rx[x + 4]) - 5.0 * rx[x + 2]
        lx[x] = lap_x
    open_y = 1.0 - ramp_y(g, width)
    masks = lap_masks()
    table = mix_table(mix, False)
    beyond = Beyond(g, 0, fa, fb)
    edge, valid = border(), valid_lanes(g)
    out2 = out.reshape(g.F * g.K * g.X, g.Y)

    def tile_step(tile, carry):
        rows = rows_of(tile)
        bound = [
            open_y * (kept[f, rows, :] + swapped[f, rows, :]) for f in range(g.F)
        ]
        past = packed_message(kept[g.F, rows, :] + swapped[g.F, rows, :]) * valid
        lap_y, mixed_bound = [], []
        for f in range(g.F):
            total = unpack_lanes(f, 0, past, edge)
            for shift, mask in masks:
                total = total + mask * turn(bound[f], shift)
            lap_y.append(total)
            mixed_bound.append(mixed(table, f, bound))
        for x in range(g.X):
            slope_x, lap_x = rx[x + 2], lx[x]
            open_xy = open_y * (1.0 - slope_x)
            d = dt[x, rows, :]
            along = slope_x * d
            across = lap_x * d
            for f in range(g.F):
                share = slope_x * mixed_bound[f] + along * lap_y[f] + across * bound[f]
                stepped = inside[f, x, rows, :] + share
                beside = beyond.columns(f, x, rows)
                if beside is not None:
                    stepped = stepped + d * beside
                done = open_xy * stepped + slope_x * bound[f] + sides[f, x, rows, :]
                strided(out2, g, f, tile, x)[...] = done
        return carry

    lax.fori_loop(0, g.tiles, tile_step, 0)


def side_sums_kernel(g, dsn, tsn, gsn, sent, wide):
    here = lax.axis_index("gy")
    shift = column_of(jnp.where(here == 0, tsn[0:1, :], tsn[1:2, :]))
    lane = lax.broadcasted_iota(jnp.int32, (g.X, 128), 1)
    batch = 128 // g.K
    for first in range(0, g.F, batch):
        some = range(first, min(first + batch, g.F))
        for f in some:
            wide[(f - first) * g.K : (f - first + 1) * g.K, :] = dsn[f]
        turned = wide[...].T[: g.X]
        for f in some:
            levels = jnp.where(lane < g.K, turn(turned, -(f - first) * g.K), 0.0)
            whole = shift_levels(levels, shift, 1)
            moved = turn(whole, 64)
            gsn[f] = jnp.where(here == 0, whole, moved)
            sent[f] = jnp.where(here == 0, moved, whole)


def side_bounds_kernel(g, sn, fsn, tsn, bsn, wide):
    here = lax.axis_index("gy")
    shift = column_of(jnp.where(here == 0, tsn[0:1, :], tsn[1:2, :]))
    span = sn.shape[3]
    wide[...] = jnp.zeros(wide.shape, f32)
    for f in range(g.F):
        wide[f, : g.X, :span] = sn[here, f]
        mine = wide[f, : g.X, :]
        theirs = fsn[f, g.K : g.K + g.X, :]
        whole = jnp.where(here == 0, mine, theirs) + turn(
            jnp.where(here == 0, theirs, mine), 64
        )
        wide[f, : g.X, :] = shift_levels(whole, shift, -1)
        bsn[f] = wide[f].T[: g.K]


def side_spread_kernel(g, relax, bsn, out):
    slope_y = ramp_y(g, relax[0])

    def tile_step(tile, carry):
        rows = rows_of(tile)
        for f in range(g.F):
            bounds = bsn[f, rows, :]
            for x in range(g.X):
                out[f, x, rows, :] = slope_y * jnp.broadcast_to(bounds[:, x : x + 1], (8, 128))
        return carry

    lax.fori_loop(0, g.tiles, tile_step, 0)


def fold_rows(values, base, first, count):
    level = lax.broadcasted_iota(jnp.int32, (count, 128), 0) + base - first
    total = jnp.zeros((count, 128), f32)
    for j in range(values.shape[0]):
        row = jnp.broadcast_to(values[j : j + 1, :], (count, 128))
        total = jnp.where(level == j, row, total)
    return total


def fold_kernel(g, parent, terrain, fy, keep, send):
    here = lax.axis_index("gx")
    odd = here >= g.nx // 2
    span = parent.shape[2]
    first = here * span
    lane = lax.broadcasted_iota(jnp.int32, (span, 128), 1)
    top = g.K + g.X
    parts = []
    for e in range(2):
        part = [fold_rows(parent[e, f], terrain[e : e + 1, :], first, g.K) for f in range(g.F)]
        values = jnp.zeros((span, 128), f32)
        heights = jnp.zeros((span, 128), f32)
        for f in range(g.F):
            spots = (lane >= 4 * f) & (lane < 4 * f + 4)
            rows = fy[f, top : top + span, :]
            values = jnp.where(spots, turn(rows, 4 * f - 4 * e), values)
            heights = jnp.where(spots, turn(rows, 4 * f - 8 - 4 * e), heights)
        part.append(fold_rows(values, heights[0:1, :].astype(jnp.int32), first, g.K))
        parts.append(part)
    for i in range(g.F + 1):
        keep[i] = jnp.where(odd, parts[1][i], parts[0][i])
        send[i] = jnp.where(odd, parts[0][i], parts[1][i])


def join_kernel(g, sums, bounds, more_bounds, out):
    for f in range(g.F):
        out[f] = sums[f]
    for f in range(g.F + 1):
        out[g.F + f] = bounds[f] + more_bounds[f]


def split_kernel(g, state, moved, sums, bounds):
    for f in range(g.F):
        sums[f] = state[f] + moved[f]
    for f in range(g.F + 1):
        bounds[f] = state[g.F + f] + moved[g.F + f]


def add_kernel(g, first, second, out):
    out[...] = first[...] + second[...]


def spread_kernel(g, kept, swapped, terrain, out):
    here = lax.axis_index("gx")
    odd = here % 2
    span = out.shape[2]
    row = lax.broadcasted_iota(jnp.int32, (8, 128), 0)
    zero = jnp.zeros((8, 128), f32)
    for e in range(2):
        start = jnp.broadcast_to(here * span - terrain[e : e + 1, :], (8, 128)) + 8
        inside = (start > 0) & (start < g.K + 8)
        tile, rest = start >> 3, start & 7
        for f in range(g.F):
            chosen = jnp.where(odd == e, kept[f], swapped[f])
            tiles = [zero] + [chosen[8 * i : 8 * i + 8] for i in range(g.tiles)] + [zero]
            low, high = zero, zero
            for i in range(g.tiles + 1):
                low = jnp.where(tile == i, tiles[i], low)
                high = jnp.where(tile == i, tiles[i + 1], high)
            for step in (4, 2, 1):
                moves = (rest & step) != 0
                up_low = pltpu.roll(low, 8 - step, 0)
                up_high = pltpu.roll(high, 8 - step, 0)
                low = jnp.where(moves, jnp.where(row < 8 - step, up_low, up_high), low)
                high = jnp.where(moves, up_high, high)
            out[e, f] = jnp.where(inside, low, zero)[:span]


def call(kernel, outs, scratch, ins, time, aliases=None, after=()):
    count = len(ins)
    ins = ins + [("a", value) for value in after]

    def run(*refs):
        kernel(*refs[:count], *refs[len(ins) :])

    out_shape = [jax.ShapeDtypeStruct(s, f32) for s in outs]
    size = 4 * sum(functools.reduce(lambda a, b: a * b, s) for s in outs)
    return pl.pallas_call(
        run,
        out_shape=out_shape,
        in_specs=[places[where] for where, _ in ins],
        out_specs=[places["v"]] * len(outs),
        scratch_shapes=[pltpu.VMEM(s, f32) if isinstance(s, tuple) else s for s in scratch],
        input_output_aliases=aliases or {},
        compiler_params=pltpu.CompilerParams(vmem_limit_bytes=24 * 1024 * 1024),
        cost_estimate=pl.CostEstimate(flops=int(time * 1.1e9), bytes_accessed=2 * size, transcendentals=0),
    )(*[pltpu.with_memory_space_constraint(v, pltpu.HBM) if w == "h" else v for w, v in ins])


def body(
    child_state,
    cotangent,
    diffusivity,
    field_mix,
    parent_we,
    parent_sn,
    terrain_we,
    terrain_sn,
    relax_width,
):
    nx, ny = lax.axis_size("gx"), lax.axis_size("gy")
    g = Geometry(child_state.shape, nx, ny)
    F, K, X, Y = child_state.shape
    evens = [(i, i ^ 1) for i in range(nx)]
    odds = [(i, (((i + 1) ^ 1) - 1) % nx) for i in range(nx)]
    block = (F, X, K, 128)
    row_shape = (2, 2, F, K, 128)
    lane_shape = (F, g.tall, 128)
    edge_shape = (F, K, 128)
    ramps = (X, 8, 128)
    band = pltpu.VMEM((256, 128), jnp.bfloat16)
    laps = (F, X, 8, 128)

    def bind(kernel, *args):
        return functools.partial(kernel, g, *args)

    def swapped(values, distance):
        return lax.ppermute(values, "gx", [(i, i ^ distance) for i in range(nx)])

    def to_y(message):
        if g.pair:
            return lax.ppermute(message, "gy", [(0, 1), (1, 0)])
        up = lax.ppermute(message, "gy", [(i, i + 1) for i in range(ny - 1)])
        down = lax.ppermute(message, "gy", [(i + 1, i) for i in range(ny - 1)])
        low = (jnp.arange(128, dtype=jnp.int32) % 4 < 2)[None, None, :]
        rows = (jnp.arange(g.tall, dtype=jnp.int32) < K)[None, :, None]
        return jnp.where(low == rows, down, up)

    def add(first, second, after):
        (total,) = call(
            bind(add_kernel), [first.shape], [], [("v", first), ("v", second)], 0.1, after=after
        )
        return total

    sn_turned = jnp.swapaxes(parent_sn, 2, 3)
    ut, at, dt, qt, ma, mb, my = call(
        bind(pack_kernel),
        [block, block, (X, K, 128), block, row_shape, row_shape, lane_shape],
        [
            ramps,
            child_state.shape,
            child_state.shape,
            diffusivity.shape,
            sn_turned.shape,
            parent_we.shape,
            pltpu.VMEM(terrain_we.shape, jnp.int32),
            pltpu.SemaphoreType.DMA((3, g.tiles)),
            pltpu.SemaphoreType.DMA((3,)),
        ],
        [
            ("s", relax_width),
            ("h", child_state),
            ("h", cotangent),
            ("h", diffusivity),
            ("h", sn_turned),
            ("h", parent_we),
            ("h", terrain_we),
        ],
        3,
    )
    fy = to_y(my)
    fa = lax.ppermute(ma, "gx", evens)
    fb = lax.ppermute(mb, "gx", odds)

    (inside_u,) = call(
        bind(forward_inside_kernel),
        [block],
        [band, laps],
        [("s", field_mix), ("v", ut), ("v", dt)],
        2.5,
    )
    (inside_a,) = call(
        bind(adjoint_inside_kernel, True),
        [block],
        [ramps, band, laps],
        [("s", relax_width), ("s", field_mix), ("v", at), ("v", qt), ("v", fy)],
        2.5,
        after=[inside_u],
    )
    keep, send = call(
        bind(fold_kernel),
        [(F + 1, K, 128)] * 2,
        [],
        [("v", parent_we), ("v", terrain_we), ("v", fy)],
        0.3,
    )
    first_bounds = swapped(send, nx // 2)
    if g.pair:
        (bsn,) = call(
            bind(side_bounds_kernel),
            [edge_shape],
            [(F, 128, 128)],
            [("v", sn_turned), ("v", fy), ("v", terrain_sn)],
            0.7,
        )
    else:
        bsn = bound_sn_general(g, parent_sn, terrain_sn)
    (sides,) = call(
        bind(side_spread_kernel), [block], [], [("s", relax_width), ("v", bsn)], 0.7
    )

    p1, q1, ma, mb, my, dwe, dsn = call(
        bind(adjoint_first_kernel),
        [block, block, row_shape, row_shape, lane_shape, edge_shape, edge_shape],
        [ramps],
        [
            ("s", relax_width),
            ("v", inside_a),
            ("v", at),
            ("v", dt),
            ("v", fa),
            ("v", fb),
        ],
        3,
        after=[keep, sides],
    )
    (state,) = call(
        bind(join_kernel),
        [(2 * F + 1, K, 128)],
        [],
        [("v", dwe), ("v", keep), ("v", first_bounds)],
        0.1,
    )
    moved = swapped(state, 2)
    u1, ma, mb, my = call(
        bind(forward_first_kernel),
        [block, row_shape, row_shape, lane_shape],
        [ramps],
        [
            ("s", relax_width),
            ("v", inside_u),
            ("v", dt),
            ("v", fa),
            ("v", fb),
            ("v", fy),
            ("v", sides),
            ("v", ma),
            ("v", mb),
            ("v", my),
        ],
        2.5,
        {7: 1, 8: 2, 9: 3},
        after=[state],
    )
    fy = to_y(my)
    fa = lax.ppermute(ma, "gx", evens)
    fb = lax.ppermute(mb, "gx", odds)

    state = add(state, moved, [u1])
    gsn_own = gsn_other = dsn
    if g.pair:
        gsn_own, sent = call(
            bind(side_sums_kernel),
            [(F, X, 128)] * 2,
            [(128, 128)],
            [("v", dsn), ("v", terrain_sn)],
            0.6,
            after=[state],
        )
        gsn_other = lax.ppermute(sent, "gy", [(0, 1), (1, 0)])
    distance = 4
    while distance < nx // 4:
        state = state + swapped(state, distance)
        distance *= 2
    moved = swapped(state, distance)
    (inside_a,) = call(
        bind(adjoint_inside_kernel, False),
        [block],
        [ramps, band, laps],
        [("s", relax_width), ("s", field_mix), ("v", p1), ("v", q1), ("v", fy)],
        2.5,
        after=[state],
    )
    (inside_u,) = call(
        bind(forward_inside_kernel),
        [block],
        [band, laps],
        [("s", field_mix), ("v", u1), ("v", dt), ("v", fy)],
        2.5,
        after=[inside_a],
    )
    grad_state, grad_sn, early = call(
        bind(adjoint_last_kernel),
        [child_state.shape, sn_turned.shape, (8, 128)],
        [],
        [("v", inside_a), ("v", fa), ("v", fb), ("v", gsn_own), ("v", gsn_other)],
        2.5,
        after=[inside_u],
    )
    sums, bounds = call(
        bind(split_kernel),
        [edge_shape, (F + 1, K, 128)],
        [],
        [("v", state), ("v", moved)],
        0.1,
        after=[early],
    )
    other_bounds = swapped(bounds, 1)
    west = [(i, i + nx // 2) for i in range(0, nx // 2, 2)]
    east = [(nx - 1 - i, nx - 1 - j) for i, j in west]
    moved = lax.ppermute(sums, "gx", west + east)
    child_final, mark = call(
        bind(forward_last_kernel),
        [child_state.shape, (8, 128)],
        [(X + 4, 8, 128), ramps],
        [
            ("s", relax_width),
            ("s", field_mix),
            ("v", inside_u),
            ("v", dt),
            ("v", fa),
            ("v", fb),
            ("v", sides),
            ("v", bounds),
            ("v", other_bounds),
        ],
        3,
    )
    sums = add(sums, moved, [mark])
    other_sums = swapped(sums, 1)
    (grad_we,) = call(
        bind(spread_kernel),
        [parent_we.shape],
        [],
        [("v", sums), ("v", other_sums), ("v", terrain_we)],
        0.7,
    )
    if g.pair:
        grad_sn = jnp.swapaxes(grad_sn, 2, 3)
    else:
        grad_sn = grad_sn_general(g, gsn_own, terrain_sn, parent_sn.shape[2])
    return (child_final, grad_state, grad_we, grad_sn)


def level_weights(g, terrain, span):
    first = lax.axis_index("gy") * span
    base = terrain[:, None, :] + jnp.arange(g.K, dtype=jnp.int32)[None, :, None]
    parent = first + jnp.arange(span, dtype=jnp.int32)
    return (parent[None, None, :, None] == base[:, :, None, :]).astype(f32)


def bound_sn_general(g, parent_sn, terrain_sn):
    weights = level_weights(g, terrain_sn, parent_sn.shape[2])
    bound = jnp.einsum("eflc,eklc->efkc", parent_sn, weights, precision=highest)
    bound = lax.psum(bound, "gy")
    mine = jnp.where(lax.axis_index("gy") < g.ny // 2, bound[0], bound[1])
    return jnp.pad(mine, ((0, 0), (0, 0), (0, 128 - g.X)))


def grad_sn_general(g, sums, terrain_sn, span):
    sums = sums[:, :, : g.X]
    south = lax.axis_index("gy") < g.ny // 2
    zero = jnp.zeros_like(sums)
    both = jnp.stack([jnp.where(south, sums, zero), jnp.where(south, zero, sums)])
    both = lax.psum(both, "gy")
    weights = level_weights(g, terrain_sn, span)
    return jnp.einsum("efkc,eklc->eflc", both, weights, precision=highest)


def solution(mesh):
    return jax.shard_map(
        body,
        mesh=mesh,
        in_specs=(
            P(None, None, "gx", "gy"),
            P(None, None, "gx", "gy"),
            P(None, "gx", "gy"),
            P(),
            P(None, None, "gx", "gy"),
            P(None, None, "gy", "gx"),
            P(None, "gy"),
            P(None, "gx"),
            P(),
        ),
        out_specs=(
            P(None, None, "gx", "gy"),
            P(None, None, "gx", "gy"),
            P(None, None, "gx", "gy"),
            P(None, None, "gy", "gx"),
        ),
        check_vma=False,
    )
```

```python
import functools

import jax
import jax.numpy as jnp
from jax import lax
from jax.experimental import pallas as pl
from jax.experimental.pallas import tpu as pltpu
from jax.sharding import PartitionSpec as P

near = 4.0 / 3.0
far = -1.0 / 12.0
coupling = 0.25
highest = lax.Precision.HIGHEST
f32 = jnp.float32
places = {
    "v": pl.BlockSpec(memory_space=pltpu.VMEM),
    "s": pl.BlockSpec(memory_space=pltpu.SMEM),
    "h": pl.BlockSpec(memory_space=pltpu.HBM),
    "a": pl.BlockSpec(memory_space=pl.ANY),
}
widest_zone = 15


class Geometry:
    def __init__(self, child, nx, ny):
        self.F, self.K, self.X, self.Y = child
        self.nx, self.ny = nx, ny
        self.tiles = self.K // 8
        assert self.K % 8 == 0 and self.Y == 128 and 4 * self.X <= 64
        assert self.X > widest_zone and self.Y > widest_zone
        assert self.X == 16
        assert nx >= 16 and nx & (nx - 1) == 0 and ny % 2 == 0
        assert 4 * self.F <= 128 and 128 % self.K == 0
        self.pair = ny == 2
        self.tall = self.K + self.X + 8


def lanes():
    return lax.broadcasted_iota(jnp.int32, (8, 128), 1)


def turn(values, shift):
    return pltpu.roll(values, shift % 128, values.ndim - 1)


def ramp(position, length, width):
    distance = jnp.minimum(position, length - 1 - position)
    inside = (position >= 0) & (position < length)
    top = jnp.where(inside, jnp.maximum(width - distance, 0), 0)
    bottom = jnp.full((8, 128), width + 1, jnp.int32)
    return jnp.broadcast_to(top, (8, 128)).astype(f32) / bottom.astype(f32)


def ramp_y(g, width):
    return ramp(lax.axis_index("gy") * g.Y + lanes(), g.ny * g.Y, width)


def ramp_x(g, width, x):
    return ramp(lax.axis_index("gx") * g.X + x, g.nx * g.X, width)


def fill_ramp_x(g, width, ref):
    for x in range(g.X):
        ref[x] = ramp_x(g, width, x)


def lap_masks():
    lane = lanes()
    zero = jnp.zeros((8, 128), f32)
    return (
        (1, jnp.where(lane > 0, near, zero)),
        (-1, jnp.where(lane < 127, near, zero)),
        (2, jnp.where(lane > 1, far, zero)),
        (-2, jnp.where(lane < 126, far, zero)),
    )


def fill_band(band):
    shape = (2 * 128, 128)
    row = lax.broadcasted_iota(jnp.int32, shape, 0) % 128
    gap = jnp.abs(row - lax.broadcasted_iota(jnp.int32, shape, 1))
    entry = jnp.where(gap == 0, -60.0, jnp.where(gap == 1, 16.0, jnp.where(gap == 2, -1.0, 0.0)))
    band[...] = entry.astype(jnp.bfloat16)


def along_lanes(values, band):
    high = values.astype(jnp.bfloat16)
    low = (values - high.astype(f32)).astype(jnp.bfloat16)
    return jnp.dot(
        jnp.concatenate([high, low], axis=1), band[...], preferred_element_type=f32
    )


def pack_lanes(x, base, values, packed):
    lane = lanes()
    start = base + 4 * x
    return jnp.where((lane >= start) & (lane < start + 4), turn(values, start + 2), packed)


def packed_message(packed):
    spot = lanes() % 4
    zero = jnp.zeros((8, 128), f32)
    low = far * turn(packed, -2) + jnp.where(spot == 1, near * turn(packed, -1), zero)
    high = far * turn(packed, 2) + jnp.where(spot == 2, near * turn(packed, 1), zero)
    return jnp.where(spot < 2, low, high)


def valid_lanes(g):
    at = lax.axis_index("gy")
    spot = lanes() % 4
    low = (at < g.ny - 1).astype(f32)
    high = (at > 0).astype(f32)
    return jnp.where(spot < 2, low, high)


def border():
    lane = lanes()
    return jnp.where((lane < 2) | (lane >= 126), 1.0, 0.0).astype(f32)


def unpack_lanes(x, base, packed, edge):
    return edge * turn(packed, -(base + 4 * x + 2))


def strided(ref, g, f, tile, x):
    start = (f * g.K + tile * 8) * g.X + x
    return ref.at[pl.ds(start, 8, stride=g.X), :]


def mix_table(mix, transposed):
    count = mix.shape[0]
    return [
        [
            (mix[h, f] if transposed else mix[f, h]) * coupling + (1.0 if f == h else 0.0)
            for h in range(count)
        ]
        for f in range(count)
    ]


def mixed(table, f, values):
    total = table[f][0] * values[0]
    for h in range(1, len(values)):
        total = total + table[f][h] * values[h]
    return total


def column_of(row):
    count = row.shape[1]
    wide = jnp.broadcast_to(row.astype(f32), (count, count))
    a = lax.broadcasted_iota(jnp.int32, (count, count), 0)
    b = lax.broadcasted_iota(jnp.int32, (count, count), 1)
    picked = jnp.sum(jnp.where(a == b, wide, 0.0), axis=1, keepdims=True)
    return jnp.broadcast_to(picked, (count, 128)).astype(jnp.int32)


def shift_levels(values, shift, sign):
    step = 1
    while step < 128:
        values = jnp.where((shift & step) != 0, turn(values, sign * step), values)
        step *= 2
    return values


def level_copies(g, pairs, sems, tile):
    levels = pl.ds(pl.multiple_of(tile * 8, 8), 8)
    copies = []
    for i, (source, target) in enumerate(pairs):
        at = (levels,) if len(source.shape) == 3 else (slice(None), levels)
        copies.append(pltpu.make_async_copy(source.at[at], target.at[at], sems.at[i, tile]))
    return copies


def rows_of(tile):
    return pl.ds(pl.multiple_of(tile * 8, 8), 8)


def odd_column():
    return lax.axis_index("gx") % 2 == 1


def send_ends(g, s, source, rows, ma, mb):
    odd = odd_column()
    for f in range(g.F):
        for j in range(2):
            low, high = source(f, j), source(f, g.X - 2 + j)
            ma[s, j, f, rows, :] = jnp.where(odd, low, high)
            mb[s, j, f, rows, :] = jnp.where(odd, high, low)


class Beyond:
    def __init__(self, g, s, fa, fb):
        self.g, self.s, self.fa, self.fb = g, s, fa, fb
        here = lax.axis_index("gx")
        self.odd = here % 2 == 1
        self.first, self.last = here == 0, here == g.nx - 1

    def left(self, j, f, rows):
        at = (self.s, j, f, rows, slice(None))
        value = jnp.where(self.odd, self.fa[at], self.fb[at])
        return jnp.where(self.first, jnp.zeros_like(value), value)

    def right(self, j, f, rows):
        at = (self.s, j, f, rows, slice(None))
        value = jnp.where(self.odd, self.fb[at], self.fa[at])
        return jnp.where(self.last, jnp.zeros_like(value), value)

    def columns(self, f, x, rows):
        last = self.g.X - 1
        if x == 0:
            return near * self.left(1, f, rows) + far * self.left(0, f, rows)
        if x == 1:
            return far * self.left(1, f, rows)
        if x == last - 1:
            return far * self.right(0, f, rows)
        if x == last:
            return near * self.right(0, f, rows) + far * self.right(1, f, rows)
        return None


class BeyondLanes:
    def __init__(self, g, s, fy):
        self.s, self.fy = s, fy
        self.edge = border()
        self.valid = valid_lanes(g)

    def tile(self, f, rows):
        return self.fy[f, rows, :] * self.valid

    def column(self, x, packed):
        return unpack_lanes(x, 64 * self.s, packed, self.edge)


def plus(value, more):
    return value if more is None else value + more


def lane_sums(vectors):
    lane = lanes()
    step = 1
    while len(vectors) > 1:
        low = (lane & step) == 0
        merged = []
        for a, b in zip(vectors[::2], vectors[1::2]):
            merged.append(jnp.where(low, a, b) + turn(jnp.where(low, b, a), step))
        vectors = merged
        step *= 2
    total = vectors[0]
    while step < 128:
        total = total + turn(total, step)
        step *= 2
    return total


def pack_kernel(
    g, relax, child_far, cot_far, diff_far, sn_far, parent_far, terrain_far,
    ut, at, dt, qt, ma, mb, my, rx, child, cot, diff, sn, parent, terrain, sems, side_sems,
):
    width = relax[0]
    pairs = ((diff_far, diff), (child_far, child), (cot_far, cot))
    for tile in range(g.tiles):
        for copy in level_copies(g, pairs, sems, tile):
            copy.start()
    side_copies = [
        pltpu.make_async_copy(source, target, side_sems.at[i])
        for i, (source, target) in enumerate(
            ((sn_far, sn), (parent_far, parent), (terrain_far, terrain))
        )
    ]
    for copy in side_copies:
        copy.start()
    fill_ramp_x(g, width, rx)
    open_y = 1.0 - ramp_y(g, width)
    child2 = child.reshape(g.F * g.K * g.X, g.Y)
    cot2 = cot.reshape(g.F * g.K * g.X, g.Y)
    diff2 = diff.reshape(g.K * g.X, g.Y)

    def tile_step(tile, carry):
        for copy in level_copies(g, pairs, sems, tile):
            copy.wait()
        rows = rows_of(tile)
        packed = [jnp.zeros((8, 128), f32) for _ in range(g.F)]
        for x in range(g.X):
            d = strided(diff2, g, 0, tile, x)[...]
            dt[x, rows, :] = d
            open_xy = open_y * (1.0 - rx[x])
            for f in range(g.F):
                u = strided(child2, g, f, tile, x)[...]
                a = strided(cot2, g, f, tile, x)[...]
                q = d * (open_xy * a)
                ut[f, x, rows, :] = u
                at[f, x, rows, :] = a
                qt[f, x, rows, :] = q
                packed[f] = pack_lanes(x, 0, u, packed[f])
                packed[f] = pack_lanes(x, 64, q, packed[f])
        for f in range(g.F):
            my[f, rows, :] = packed_message(packed[f])
        for s, source in enumerate((ut, qt)):
            send_ends(g, s, lambda f, x: source[f, x, rows, :], rows, ma, mb)
        return carry

    lax.fori_loop(0, g.tiles, tile_step, 0)
    for copy in side_copies:
        copy.wait()
    for f in range(g.F):
        my[f, g.K :, :] = jnp.zeros((g.X + 8, 128), f32)
    if g.pair:
        other = 1 - lax.axis_index("gy")
        for f in range(g.F):
            my[f, g.K : g.K + g.X, : sn.shape[3]] = sn[other, f]
    span = parent.shape[2]
    lane = lax.broadcasted_iota(jnp.int32, (span, 128), 1)
    for f in range(g.F):
        total = jnp.zeros((span, 128), f32)
        for e in range(2):
            heights = jnp.broadcast_to(terrain[e : e + 1, :].astype(f32), (span, 128))
            for spot, values in ((e, parent[e, f]), (2 + e, heights)):
                here = (lane >= 4 * spot) & (lane < 4 * spot + 4)
                total = jnp.where(here, turn(values, 4 * spot + 2), total)
        my[f, g.K + g.X : g.K + g.X + span, :] = total


def fill_laps(g, source, rows, band, laps):
    for f in range(g.F):
        cells = source[f, :, rows, :]
        parts = along_lanes(cells.reshape(8 * g.X, 128), band)
        for x in range(g.X):
            ones = [cells[x + i] for i in (-1, 1) if 0 <= x + i < g.X]
            twos = [cells[x + i] for i in (-2, 2) if 0 <= x + i < g.X]
            total = parts[8 * x : 8 * x + 8] + 16.0 * functools.reduce(jnp.add, ones)
            total = total - functools.reduce(jnp.add, twos)
            laps[f, x] = total * (1.0 / 12.0)


def adjoint_inside_kernel(g, scaled, relax, mix, ps, qs, fy, out, rx, band, laps):
    beyond = BeyondLanes(g, 1, fy)
    width = relax[0]
    table = mix_table(mix, True)
    fill_band(band)
    if scaled:
        fill_ramp_x(g, width, rx)
        open_y = 1.0 - ramp_y(g, width)

    def tile_step(tile, carry):
        rows = rows_of(tile)
        fill_laps(g, qs, rows, band, laps)
        halo = [beyond.tile(f, rows) for f in range(g.F)]
        for x in range(g.X):
            p = [ps[f, x, rows, :] for f in range(g.F)]
            if scaled:
                open_xy = open_y * (1.0 - rx[x])
                p = [open_xy * value for value in p]
            for f in range(g.F):
                out[f, x, rows, :] = mixed(table, f, p) + laps[f, x] + beyond.column(x, halo[f])
        return carry

    lax.fori_loop(0, g.tiles, tile_step, 0)


def forward_inside_kernel(g, mix, ut, dt, *rest):
    *fy, out, band, laps = rest
    table = mix_table(mix, False)
    fill_band(band)
    beyond = BeyondLanes(g, 0, fy[0]) if fy else None

    def tile_step(tile, carry):
        rows = rows_of(tile)
        fill_laps(g, ut, rows, band, laps)
        if fy:
            halo = [beyond.tile(f, rows) for f in range(g.F)]
        for x in range(g.X):
            u = [ut[f, x, rows, :] for f in range(g.F)]
            d = dt[x, rows, :]
            for f in range(g.F):
                lap = laps[f, x]
                if fy:
                    lap = lap + beyond.column(x, halo[f])
                out[f, x, rows, :] = mixed(table, f, u) + d * lap
        return carry

    lax.fori_loop(0, g.tiles, tile_step, 0)


def adjoint_first_kernel(
    g, relax, inside, at, dt, fa, fb, p1, q1, ma, mb, my, dwe, dsn, rx
):
    width = relax[0]
    fill_ramp_x(g, width, rx)
    slope_y = ramp_y(g, width)
    open_y = 1.0 - slope_y
    beyond = Beyond(g, 1, fa, fb)

    def tile_step(tile, carry):
        rows = rows_of(tile)
        for f in range(g.F):
            packed = jnp.zeros((8, 128), f32)
            share = jnp.zeros((8, 128), f32)
            pushes = []
            for x in range(g.X):
                slope_x = rx[x]
                open_xy = open_y * (1.0 - slope_x)
                middle = plus(inside[f, x, rows, :], beyond.columns(f, x, rows))
                carried = at[f, x, rows, :] + middle
                share = share + slope_x * carried
                pushes.append(slope_y * carried)
                pulled = open_xy * middle
                q = dt[x, rows, :] * pulled
                p1[f, x, rows, :] = pulled
                q1[f, x, rows, :] = q
                packed = pack_lanes(x, 64, q, packed)
            my[f, rows, :] = packed_message(packed)
            dsn[f, rows, :] = lane_sums(pushes)
            dwe[f, rows, :] = open_y * share
        send_ends(g, 1, lambda f, x: q1[f, x, rows, :], rows, ma, mb)
        return carry

    lax.fori_loop(0, g.tiles, tile_step, 0)
    for f in range(g.F):
        my[f, g.K :, :] = jnp.zeros((g.X + 8, 128), f32)


def forward_first_kernel(
    g, relax, inside, dt, fa, fb, fy, sides, ma_in, mb_in, my_in, u1, ma, mb, my, rx
):
    width = relax[0]
    fill_ramp_x(g, width, rx)
    open_y = 1.0 - ramp_y(g, width)
    beyond = Beyond(g, 0, fa, fb)
    beyond_lanes = BeyondLanes(g, 0, fy)
    lane = lanes()

    def tile_step(tile, carry):
        rows = rows_of(tile)
        halo = [beyond_lanes.tile(f, rows) for f in range(g.F)]
        packed = [jnp.zeros((8, 128), f32) for _ in range(g.F)]
        for x in range(g.X):
            open_xy = open_y * (1.0 - rx[x])
            d = dt[x, rows, :]
            for f in range(g.F):
                lap = plus(beyond_lanes.column(x, halo[f]), beyond.columns(f, x, rows))
                stepped = inside[f, x, rows, :] + d * lap
                done = open_xy * stepped + sides[f, x, rows, :]
                u1[f, x, rows, :] = done
                packed[f] = pack_lanes(x, 0, done, packed[f])
        for f in range(g.F):
            my[f, rows, :] = jnp.where(lane < 64, packed_message(packed[f]), my_in[f, rows, :])
        send_ends(g, 0, lambda f, x: u1[f, x, rows, :], rows, ma, mb)
        return carry

    lax.fori_loop(0, g.tiles, tile_step, 0)


def adjoint_last_kernel(g, inside, fa, fb, fy, gsn_own, out, gsn):
    out2 = out.reshape(g.F * g.K * g.X, g.Y)
    beyond = Beyond(g, 1, fa, fb)

    def tile_step(tile, carry):
        rows = rows_of(tile)
        for f in range(g.F):
            for x in range(g.X):
                value = plus(inside[f, x, rows, :], beyond.columns(f, x, rows))
                strided(out2, g, f, tile, x)[...] = value
        return carry

    lax.fori_loop(0, g.tiles, tile_step, 0)
    if g.pair:
        here = lax.axis_index("gy")
        span = gsn.shape[3]
        for f in range(g.F):
            gsn[here, f] = gsn_own[f, :, :span]
            gsn[1 - here, f] = fy[f, g.K : g.K + g.X, :span]
    else:
        gsn[...] = jnp.zeros(gsn.shape, f32)


def forward_last_kernel(
    g, relax, mix, inside, dt, fa, fb, sides, kept, swapped, out, mark, rx, lx
):
    width = relax[0]
    mark[...] = jnp.zeros((8, 128), f32)
    for x in range(-2, g.X + 2):
        rx[x + 2] = ramp_x(g, width, x)
    for x in range(g.X):
        lap_x = near * (rx[x + 1] + rx[x + 3]) + far * (rx[x] + rx[x + 4]) - 5.0 * rx[x + 2]
        lx[x] = lap_x
    open_y = 1.0 - ramp_y(g, width)
    masks = lap_masks()
    table = mix_table(mix, False)
    beyond = Beyond(g, 0, fa, fb)
    edge, valid = border(), valid_lanes(g)
    out2 = out.reshape(g.F * g.K * g.X, g.Y)

    def tile_step(tile, carry):
        rows = rows_of(tile)
        bound = [
            open_y * (kept[f, rows, :] + swapped[f, rows, :]) for f in range(g.F)
        ]
        past = packed_message(kept[g.F, rows, :] + swapped[g.F, rows, :]) * valid
        lap_y, mixed_bound = [], []
        for f in range(g.F):
            total = unpack_lanes(f, 0, past, edge)
            for shift, mask in masks:
                total = total + mask * turn(bound[f], shift)
            lap_y.append(total)
            mixed_bound.append(mixed(table, f, bound))
        for x in range(g.X):
            slope_x, lap_x = rx[x + 2], lx[x]
            open_xy = open_y * (1.0 - slope_x)
            d = dt[x, rows, :]
            along = slope_x * d
            across = lap_x * d
            for f in range(g.F):
                share = slope_x * mixed_bound[f] + along * lap_y[f] + across * bound[f]
                stepped = inside[f, x, rows, :] + share
                beside = beyond.columns(f, x, rows)
                if beside is not None:
                    stepped = stepped + d * beside
                done = open_xy * stepped + slope_x * bound[f] + sides[f, x, rows, :]
                strided(out2, g, f, tile, x)[...] = done
        return carry

    lax.fori_loop(0, g.tiles, tile_step, 0)


def side_sums_kernel(g, dsn, tsn, my_in, gsn, my, wide):
    here = lax.axis_index("gy")
    shift = column_of(jnp.where(here == 0, tsn[0:1, :], tsn[1:2, :]))
    lane = lax.broadcasted_iota(jnp.int32, (g.X, 128), 1)
    batch = 128 // g.K
    for first in range(0, g.F, batch):
        some = range(first, min(first + batch, g.F))
        for f in some:
            wide[(f - first) * g.K : (f - first + 1) * g.K, :] = dsn[f]
        turned = wide[...].T[: g.X]
        for f in some:
            levels = jnp.where(lane < g.K, turn(turned, -(f - first) * g.K), 0.0)
            whole = shift_levels(levels, shift, 1)
            moved = turn(whole, 64)
            gsn[f] = jnp.where(here == 0, whole, moved)
            my[f, g.K : g.K + g.X, :] = jnp.where(here == 0, moved, whole)


def side_bounds_kernel(g, sn, fsn, tsn, bsn, wide):
    here = lax.axis_index("gy")
    shift = column_of(jnp.where(here == 0, tsn[0:1, :], tsn[1:2, :]))
    span = sn.shape[3]
    wide[...] = jnp.zeros(wide.shape, f32)
    for f in range(g.F):
        wide[f, : g.X, :span] = sn[here, f]
        mine = wide[f, : g.X, :]
        theirs = fsn[f, g.K : g.K + g.X, :]
        whole = jnp.where(here == 0, mine, theirs) + turn(
            jnp.where(here == 0, theirs, mine), 64
        )
        wide[f, : g.X, :] = shift_levels(whole, shift, -1)
        bsn[f] = wide[f].T[: g.K]


def side_spread_kernel(g, relax, bsn, out):
    slope_y = ramp_y(g, relax[0])

    def tile_step(tile, carry):
        rows = rows_of(tile)
        for f in range(g.F):
            bounds = bsn[f, rows, :]
            for x in range(g.X):
                out[f, x, rows, :] = slope_y * jnp.broadcast_to(bounds[:, x : x + 1], (8, 128))
        return carry

    lax.fori_loop(0, g.tiles, tile_step, 0)


def fold_rows(values, base, first, count):
    level = lax.broadcasted_iota(jnp.int32, (count, 128), 0) + base - first
    total = jnp.zeros((count, 128), f32)
    for j in range(values.shape[0]):
        row = jnp.broadcast_to(values[j : j + 1, :], (count, 128))
        total = jnp.where(level == j, row, total)
    return total


def fold_kernel(g, parent, terrain, fy, keep, send):
    here = lax.axis_index("gx")
    odd = here >= g.nx // 2
    span = parent.shape[2]
    first = here * span
    lane = lax.broadcasted_iota(jnp.int32, (span, 128), 1)
    top = g.K + g.X
    parts = []
    for e in range(2):
        part = [fold_rows(parent[e, f], terrain[e : e + 1, :], first, g.K) for f in range(g.F)]
        values = jnp.zeros((span, 128), f32)
        heights = jnp.zeros((span, 128), f32)
        for f in range(g.F):
            spots = (lane >= 4 * f) & (lane < 4 * f + 4)
            rows = fy[f, top : top + span, :]
            values = jnp.where(spots, turn(rows, 4 * f - 4 * e), values)
            heights = jnp.where(spots, turn(rows, 4 * f - 8 - 4 * e), heights)
        part.append(fold_rows(values, heights[0:1, :].astype(jnp.int32), first, g.K))
        parts.append(part)
    for i in range(g.F + 1):
        keep[i] = jnp.where(odd, parts[1][i], parts[0][i])
        send[i] = jnp.where(odd, parts[0][i], parts[1][i])


def join_kernel(g, sums, bounds, more_bounds, out):
    for f in range(g.F):
        out[f] = sums[f]
    for f in range(g.F + 1):
        out[g.F + f] = bounds[f] + more_bounds[f]


def split_kernel(g, state, moved, sums, bounds):
    for f in range(g.F):
        sums[f] = state[f] + moved[f]
    for f in range(g.F + 1):
        bounds[f] = state[g.F + f] + moved[g.F + f]


def add_kernel(g, first, second, out):
    out[...] = first[...] + second[...]


def spread_kernel(g, flip, sums, terrain, out):
    here = lax.axis_index("gx")
    pair = (here ^ flip) // 2
    count = out.shape[1]
    row = lax.broadcasted_iota(jnp.int32, (8, 128), 0)
    zero = jnp.zeros((8, 128), f32)
    base = jnp.where(here % 2 == 1, terrain[1:2, :], terrain[0:1, :])
    for block in range(count // 8):
        start = jnp.broadcast_to(pair * count + 8 * block - base, (8, 128)) + 8
        inside = (start > 0) & (start < g.K + 8)
        tile, rest = start >> 3, start & 7
        for f in range(g.F):
            chosen = sums[f]
            tiles = [zero] + [chosen[8 * i : 8 * i + 8] for i in range(g.tiles)] + [zero]
            low, high = zero, zero
            for i in range(g.tiles + 1):
                low = jnp.where(tile == i, tiles[i], low)
                high = jnp.where(tile == i, tiles[i + 1], high)
            for step in (4, 2, 1):
                moves = (rest & step) != 0
                up_low = pltpu.roll(low, 8 - step, 0)
                up_high = pltpu.roll(high, 8 - step, 0)
                low = jnp.where(moves, jnp.where(row < 8 - step, up_low, up_high), low)
                high = jnp.where(moves, up_high, high)
            out[f, 8 * block : 8 * block + 8, :] = jnp.where(inside, low, zero)


def halves_kernel(g, own, moved, kept, sent):
    odd = odd_column()
    span = kept.shape[1]
    for f in range(g.F):
        both = own[f] + moved[f]
        low, high = both[:span], both[span:]
        kept[f] = jnp.where(odd, high, low)
        sent[f] = jnp.where(odd, low, high)


def assemble_kernel(g, kept, other, out):
    odd = lax.axis_index("gx") % 2
    for f in range(g.F):
        out[odd, f] = kept[f]
        out[1 - odd, f] = other[f]


def call(kernel, outs, scratch, ins, time, aliases=None, after=()):
    count = len(ins)
    ins = ins + [("a", value) for value in after]

    def run(*refs):
        kernel(*refs[:count], *refs[len(ins) :])

    out_shape = [jax.ShapeDtypeStruct(s, f32) for s in outs]
    size = 4 * sum(functools.reduce(lambda a, b: a * b, s) for s in outs)
    return pl.pallas_call(
        run,
        out_shape=out_shape,
        in_specs=[places[where] for where, _ in ins],
        out_specs=[places["v"]] * len(outs),
        scratch_shapes=[pltpu.VMEM(s, f32) if isinstance(s, tuple) else s for s in scratch],
        input_output_aliases=aliases or {},
        compiler_params=pltpu.CompilerParams(vmem_limit_bytes=24 * 1024 * 1024),
        cost_estimate=pl.CostEstimate(flops=int(time * 1.1e9), bytes_accessed=2 * size, transcendentals=0),
    )(*[pltpu.with_memory_space_constraint(v, pltpu.HBM) if w == "h" else v for w, v in ins])


def body(
    child_state,
    cotangent,
    diffusivity,
    field_mix,
    parent_we,
    parent_sn,
    terrain_we,
    terrain_sn,
    relax_width,
):
    nx, ny = lax.axis_size("gx"), lax.axis_size("gy")
    g = Geometry(child_state.shape, nx, ny)
    F, K, X, Y = child_state.shape
    evens = [(i, i ^ 1) for i in range(nx)]
    odds = [(i, (((i + 1) ^ 1) - 1) % nx) for i in range(nx)]
    block = (F, X, K, 128)
    row_shape = (2, 2, F, K, 128)
    lane_shape = (F, g.tall, 128)
    edge_shape = (F, K, 128)
    ramps = (X, 8, 128)
    band = pltpu.VMEM((256, 128), jnp.bfloat16)
    laps = (F, X, 8, 128)

    def bind(kernel, *args):
        return functools.partial(kernel, g, *args)

    def swapped(values, distance):
        return lax.ppermute(values, "gx", [(i, i ^ distance) for i in range(nx)])

    def to_y(message):
        if g.pair:
            return lax.ppermute(message, "gy", [(0, 1), (1, 0)])
        up = lax.ppermute(message, "gy", [(i, i + 1) for i in range(ny - 1)])
        down = lax.ppermute(message, "gy", [(i + 1, i) for i in range(ny - 1)])
        low = (jnp.arange(128, dtype=jnp.int32) % 4 < 2)[None, None, :]
        rows = (jnp.arange(g.tall, dtype=jnp.int32) < K)[None, :, None]
        return jnp.where(low == rows, down, up)

    def add(first, second, after):
        (total,) = call(
            bind(add_kernel), [first.shape], [], [("v", first), ("v", second)], 0.1, after=after
        )
        return total

    sn_turned = jnp.swapaxes(parent_sn, 2, 3)
    ut, at, dt, qt, ma, mb, my = call(
        bind(pack_kernel),
        [block, block, (X, K, 128), block, row_shape, row_shape, lane_shape],
        [
            ramps,
            child_state.shape,
            child_state.shape,
            diffusivity.shape,
            sn_turned.shape,
            parent_we.shape,
            pltpu.VMEM(terrain_we.shape, jnp.int32),
            pltpu.SemaphoreType.DMA((3, g.tiles)),
            pltpu.SemaphoreType.DMA((3,)),
        ],
        [
            ("s", relax_width),
            ("h", child_state),
            ("h", cotangent),
            ("h", diffusivity),
            ("h", sn_turned),
            ("h", parent_we),
            ("h", terrain_we),
        ],
        3,
    )
    fy = to_y(my)
    fa = lax.ppermute(ma, "gx", evens)
    fb = lax.ppermute(mb, "gx", odds)

    (inside_u,) = call(
        bind(forward_inside_kernel),
        [block],
        [band, laps],
        [("s", field_mix), ("v", ut), ("v", dt)],
        2.5,
    )
    (inside_a,) = call(
        bind(adjoint_inside_kernel, True),
        [block],
        [ramps, band, laps],
        [("s", relax_width), ("s", field_mix), ("v", at), ("v", qt), ("v", fy)],
        2.5,
        after=[inside_u],
    )
    keep, send = call(
        bind(fold_kernel),
        [(F + 1, K, 128)] * 2,
        [],
        [("v", parent_we), ("v", terrain_we), ("v", fy)],
        0.3,
    )
    first_bounds = swapped(send, nx // 2)
    if g.pair:
        (bsn,) = call(
            bind(side_bounds_kernel),
            [edge_shape],
            [(F, 128, 128)],
            [("v", sn_turned), ("v", fy), ("v", terrain_sn)],
            0.7,
        )
    else:
        bsn = bound_sn_general(g, parent_sn, terrain_sn)
    (sides,) = call(
        bind(side_spread_kernel), [block], [], [("s", relax_width), ("v", bsn)], 0.7
    )

    p1, q1, ma, mb, my, dwe, dsn = call(
        bind(adjoint_first_kernel),
        [block, block, row_shape, row_shape, lane_shape, edge_shape, edge_shape],
        [ramps],
        [
            ("s", relax_width),
            ("v", inside_a),
            ("v", at),
            ("v", dt),
            ("v", fa),
            ("v", fb),
        ],
        3,
        after=[keep, sides],
    )
    (state,) = call(
        bind(join_kernel),
        [(2 * F + 1, K, 128)],
        [],
        [("v", dwe), ("v", keep), ("v", first_bounds)],
        0.1,
    )
    moved = swapped(state, 2)
    u1, ma, mb, my = call(
        bind(forward_first_kernel),
        [block, row_shape, row_shape, lane_shape],
        [ramps],
        [
            ("s", relax_width),
            ("v", inside_u),
            ("v", dt),
            ("v", fa),
            ("v", fb),
            ("v", fy),
            ("v", sides),
            ("v", ma),
            ("v", mb),
            ("v", my),
        ],
        2.5,
        {7: 1, 8: 2, 9: 3},
        after=[state],
    )
    if g.pair:
        gsn_own, my = call(
            bind(side_sums_kernel),
            [(F, X, 128), lane_shape],
            [(128, 128)],
            [("v", dsn), ("v", terrain_sn), ("v", my)],
            0.6,
            {2: 1},
        )
    else:
        gsn_own = dsn
    fy = to_y(my)
    fa = lax.ppermute(ma, "gx", evens)
    fb = lax.ppermute(mb, "gx", odds)

    state = add(state, moved, [gsn_own])
    distance = 4
    while distance < nx // 4:
        state = state + swapped(state, distance)
        distance *= 2
    moved = swapped(state, distance)
    (inside_a,) = call(
        bind(adjoint_inside_kernel, False),
        [block],
        [ramps, band, laps],
        [("s", relax_width), ("s", field_mix), ("v", p1), ("v", q1), ("v", fy)],
        2.5,
        after=[state],
    )
    (inside_u,) = call(
        bind(forward_inside_kernel),
        [block],
        [band, laps],
        [("s", field_mix), ("v", u1), ("v", dt), ("v", fy)],
        2.5,
        after=[inside_a],
    )
    sums, bounds = call(
        bind(split_kernel),
        [edge_shape, (F + 1, K, 128)],
        [],
        [("v", state), ("v", moved)],
        0.1,
        after=[inside_u],
    )
    other_bounds = swapped(bounds, 1)
    span = parent_we.shape[2]
    pair_shape = (F, 2 * span, 128)
    (gone,) = call(
        bind(spread_kernel, nx // 2), [pair_shape], [], [("v", sums), ("v", terrain_we)], 0.7
    )
    moved = swapped(gone, nx // 2)
    child_final, mark = call(
        bind(forward_last_kernel),
        [child_state.shape, (8, 128)],
        [(X + 4, 8, 128), ramps],
        [
            ("s", relax_width),
            ("s", field_mix),
            ("v", inside_u),
            ("v", dt),
            ("v", fa),
            ("v", fb),
            ("v", sides),
            ("v", bounds),
            ("v", other_bounds),
        ],
        3,
    )
    (own,) = call(
        bind(spread_kernel, 0),
        [pair_shape],
        [],
        [("v", sums), ("v", terrain_we)],
        0.7,
        after=[mark],
    )
    kept, sent = call(
        bind(halves_kernel), [(F, span, 128)] * 2, [], [("v", own), ("v", moved)], 0.1
    )
    other_kept = swapped(sent, 1)
    grad_state, grad_sn = call(
        bind(adjoint_last_kernel),
        [child_state.shape, sn_turned.shape],
        [],
        [("v", inside_a), ("v", fa), ("v", fb), ("v", fy), ("v", gsn_own)],
        2.5,
        after=[kept],
    )
    (grad_we,) = call(
        bind(assemble_kernel),
        [parent_we.shape],
        [],
        [("v", kept), ("v", other_kept)],
        0.1,
    )
    if g.pair:
        grad_sn = jnp.swapaxes(grad_sn, 2, 3)
    else:
        grad_sn = grad_sn_general(g, gsn_own, terrain_sn, parent_sn.shape[2])
    return (child_final, grad_state, grad_we, grad_sn)


def level_weights(g, terrain, span):
    first = lax.axis_index("gy") * span
    base = terrain[:, None, :] + jnp.arange(g.K, dtype=jnp.int32)[None, :, None]
    parent = first + jnp.arange(span, dtype=jnp.int32)
    return (parent[None, None, :, None] == base[:, :, None, :]).astype(f32)


def bound_sn_general(g, parent_sn, terrain_sn):
    weights = level_weights(g, terrain_sn, parent_sn.shape[2])
    bound = jnp.einsum("eflc,eklc->efkc", parent_sn, weights, precision=highest)
    bound = lax.psum(bound, "gy")
    mine = jnp.where(lax.axis_index("gy") < g.ny // 2, bound[0], bound[1])
    return jnp.pad(mine, ((0, 0), (0, 0), (0, 128 - g.X)))


def grad_sn_general(g, sums, terrain_sn, span):
    sums = sums[:, :, : g.X]
    south = lax.axis_index("gy") < g.ny // 2
    zero = jnp.zeros_like(sums)
    both = jnp.stack([jnp.where(south, sums, zero), jnp.where(south, zero, sums)])
    both = lax.psum(both, "gy")
    weights = level_weights(g, terrain_sn, span)
    return jnp.einsum("efkc,eklc->eflc", both, weights, precision=highest)


def solution(mesh):
    return jax.shard_map(
        body,
        mesh=mesh,
        in_specs=(
            P(None, None, "gx", "gy"),
            P(None, None, "gx", "gy"),
            P(None, "gx", "gy"),
            P(),
            P(None, None, "gx", "gy"),
            P(None, None, "gy", "gx"),
            P(None, "gy"),
            P(None, "gx"),
            P(),
        ),
        out_specs=(
            P(None, None, "gx", "gy"),
            P(None, None, "gx", "gy"),
            P(None, None, "gx", "gy"),
            P(None, None, "gy", "gx"),
        ),
        check_vma=False,
    )
```

```python
import functools

import jax
import jax.numpy as jnp
from jax import lax
from jax.experimental import pallas as pl
from jax.experimental.pallas import tpu as pltpu
from jax.sharding import PartitionSpec as P

near = 4.0 / 3.0
far = -1.0 / 12.0
coupling = 0.25
highest = lax.Precision.HIGHEST
f32 = jnp.float32
places = {
    "v": pl.BlockSpec(memory_space=pltpu.VMEM),
    "s": pl.BlockSpec(memory_space=pltpu.SMEM),
    "h": pl.BlockSpec(memory_space=pltpu.HBM),
    "a": pl.BlockSpec(memory_space=pl.ANY),
}
widest_zone = 15


class Geometry:
    def __init__(self, child, nx, ny):
        self.F, self.K, self.X, self.Y = child
        self.nx, self.ny = nx, ny
        self.tiles = self.K // 8
        assert self.K % 8 == 0 and self.Y == 128 and 4 * self.X <= 64
        assert self.X > widest_zone and self.Y > widest_zone
        assert self.X == 16
        assert nx >= 16 and nx & (nx - 1) == 0 and ny % 2 == 0
        assert 4 * self.F <= 128 and 128 % self.K == 0
        self.pair = ny == 2
        self.tall = self.K + self.X + 8


def lanes():
    return lax.broadcasted_iota(jnp.int32, (8, 128), 1)


def turn(values, shift):
    return pltpu.roll(values, shift % 128, values.ndim - 1)


def ramp(position, length, width):
    distance = jnp.minimum(position, length - 1 - position)
    inside = (position >= 0) & (position < length)
    top = jnp.where(inside, jnp.maximum(width - distance, 0), 0)
    bottom = jnp.full((8, 128), width + 1, jnp.int32)
    return jnp.broadcast_to(top, (8, 128)).astype(f32) / bottom.astype(f32)


def ramp_y(g, width):
    return ramp(lax.axis_index("gy") * g.Y + lanes(), g.ny * g.Y, width)


def ramp_x(g, width, x):
    return ramp(lax.axis_index("gx") * g.X + x, g.nx * g.X, width)


def fill_ramp_x(g, width, ref):
    for x in range(g.X):
        ref[x] = ramp_x(g, width, x)


def lap_masks():
    lane = lanes()
    zero = jnp.zeros((8, 128), f32)
    return (
        (1, jnp.where(lane > 0, near, zero)),
        (-1, jnp.where(lane < 127, near, zero)),
        (2, jnp.where(lane > 1, far, zero)),
        (-2, jnp.where(lane < 126, far, zero)),
    )


def fill_band(band):
    shape = (2 * 128, 128)
    row = lax.broadcasted_iota(jnp.int32, shape, 0) % 128
    gap = jnp.abs(row - lax.broadcasted_iota(jnp.int32, shape, 1))
    entry = jnp.where(gap == 0, -60.0, jnp.where(gap == 1, 16.0, jnp.where(gap == 2, -1.0, 0.0)))
    band[...] = entry.astype(jnp.bfloat16)


def along_lanes(values, band):
    high = values.astype(jnp.bfloat16)
    low = (values - high.astype(f32)).astype(jnp.bfloat16)
    return jnp.dot(
        jnp.concatenate([high, low], axis=1), band[...], preferred_element_type=f32
    )


def pack_lanes(x, base, values, packed):
    lane = lanes()
    start = base + 4 * x
    return jnp.where((lane >= start) & (lane < start + 4), turn(values, start + 2), packed)


def packed_message(packed):
    spot = lanes() % 4
    zero = jnp.zeros((8, 128), f32)
    low = far * turn(packed, -2) + jnp.where(spot == 1, near * turn(packed, -1), zero)
    high = far * turn(packed, 2) + jnp.where(spot == 2, near * turn(packed, 1), zero)
    return jnp.where(spot < 2, low, high)


def valid_lanes(g):
    at = lax.axis_index("gy")
    spot = lanes() % 4
    low = (at < g.ny - 1).astype(f32)
    high = (at > 0).astype(f32)
    return jnp.where(spot < 2, low, high)


def border():
    lane = lanes()
    return jnp.where((lane < 2) | (lane >= 126), 1.0, 0.0).astype(f32)


def unpack_lanes(x, base, packed, edge):
    return edge * turn(packed, -(base + 4 * x + 2))


def strided(ref, g, f, tile, x):
    start = (f * g.K + tile * 8) * g.X + x
    return ref.at[pl.ds(start, 8, stride=g.X), :]


def mix_table(mix, transposed):
    count = mix.shape[0]
    return [
        [
            (mix[h, f] if transposed else mix[f, h]) * coupling + (1.0 if f == h else 0.0)
            for h in range(count)
        ]
        for f in range(count)
    ]


def mixed(table, f, values):
    total = table[f][0] * values[0]
    for h in range(1, len(values)):
        total = total + table[f][h] * values[h]
    return total


def column_of(row):
    count = row.shape[1]
    wide = jnp.broadcast_to(row.astype(f32), (count, count))
    a = lax.broadcasted_iota(jnp.int32, (count, count), 0)
    b = lax.broadcasted_iota(jnp.int32, (count, count), 1)
    picked = jnp.sum(jnp.where(a == b, wide, 0.0), axis=1, keepdims=True)
    return jnp.broadcast_to(picked, (count, 128)).astype(jnp.int32)


def shift_levels(values, shift, sign):
    step = 1
    while step < 128:
        values = jnp.where((shift & step) != 0, turn(values, sign * step), values)
        step *= 2
    return values


def level_copies(g, pairs, sems, tile):
    levels = pl.ds(pl.multiple_of(tile * 8, 8), 8)
    copies = []
    for i, (source, target) in enumerate(pairs):
        at = (levels,) if len(source.shape) == 3 else (slice(None), levels)
        copies.append(pltpu.make_async_copy(source.at[at], target.at[at], sems.at[i, tile]))
    return copies


def rows_of(tile):
    return pl.ds(pl.multiple_of(tile * 8, 8), 8)


def odd_column():
    return lax.axis_index("gx") % 2 == 1


def send_ends(g, s, source, rows, ma, mb):
    odd = odd_column()
    for f in range(g.F):
        for j in range(2):
            low, high = source(f, j), source(f, g.X - 2 + j)
            ma[s, j, f, rows, :] = jnp.where(odd, low, high)
            mb[s, j, f, rows, :] = jnp.where(odd, high, low)


class Beyond:
    def __init__(self, g, s, fa, fb):
        self.g, self.s, self.fa, self.fb = g, s, fa, fb
        here = lax.axis_index("gx")
        self.odd = here % 2 == 1
        self.first, self.last = here == 0, here == g.nx - 1

    def left(self, j, f, rows):
        at = (self.s, j, f, rows, slice(None))
        value = jnp.where(self.odd, self.fa[at], self.fb[at])
        return jnp.where(self.first, jnp.zeros_like(value), value)

    def right(self, j, f, rows):
        at = (self.s, j, f, rows, slice(None))
        value = jnp.where(self.odd, self.fb[at], self.fa[at])
        return jnp.where(self.last, jnp.zeros_like(value), value)

    def columns(self, f, x, rows):
        last = self.g.X - 1
        if x == 0:
            return near * self.left(1, f, rows) + far * self.left(0, f, rows)
        if x == 1:
            return far * self.left(1, f, rows)
        if x == last - 1:
            return far * self.right(0, f, rows)
        if x == last:
            return near * self.right(0, f, rows) + far * self.right(1, f, rows)
        return None


class BeyondLanes:
    def __init__(self, g, s, fy):
        self.s, self.fy = s, fy
        self.edge = border()
        self.valid = valid_lanes(g)

    def tile(self, f, rows):
        return self.fy[f, rows, :] * self.valid

    def column(self, x, packed):
        return unpack_lanes(x, 64 * self.s, packed, self.edge)


def plus(value, more):
    return value if more is None else value + more


def lane_sums(vectors):
    lane = lanes()
    step = 1
    while len(vectors) > 1:
        low = (lane & step) == 0
        merged = []
        for a, b in zip(vectors[::2], vectors[1::2]):
            merged.append(jnp.where(low, a, b) + turn(jnp.where(low, b, a), step))
        vectors = merged
        step *= 2
    total = vectors[0]
    while step < 128:
        total = total + turn(total, step)
        step *= 2
    return total


def pack_kernel(
    g, relax, child_far, cot_far, diff_far, sn_far, parent_far, terrain_far,
    ut, at, dt, qt, ma, mb, my, rx, child, cot, diff, sn, parent, terrain, sems, side_sems,
):
    width = relax[0]
    pairs = ((diff_far, diff), (child_far, child), (cot_far, cot))
    for tile in range(g.tiles):
        for copy in level_copies(g, pairs, sems, tile):
            copy.start()
    side_copies = [
        pltpu.make_async_copy(source, target, side_sems.at[i])
        for i, (source, target) in enumerate(
            ((sn_far, sn), (parent_far, parent), (terrain_far, terrain))
        )
    ]
    for copy in side_copies:
        copy.start()
    fill_ramp_x(g, width, rx)
    open_y = 1.0 - ramp_y(g, width)
    child2 = child.reshape(g.F * g.K * g.X, g.Y)
    cot2 = cot.reshape(g.F * g.K * g.X, g.Y)
    diff2 = diff.reshape(g.K * g.X, g.Y)

    def tile_step(tile, carry):
        for copy in level_copies(g, pairs, sems, tile):
            copy.wait()
        rows = rows_of(tile)
        packed = [jnp.zeros((8, 128), f32) for _ in range(g.F)]
        for x in range(g.X):
            d = strided(diff2, g, 0, tile, x)[...]
            dt[x, rows, :] = d
            open_xy = open_y * (1.0 - rx[x])
            for f in range(g.F):
                u = strided(child2, g, f, tile, x)[...]
                a = strided(cot2, g, f, tile, x)[...]
                q = d * (open_xy * a)
                ut[f, x, rows, :] = u
                at[f, x, rows, :] = a
                qt[f, x, rows, :] = q
                packed[f] = pack_lanes(x, 0, u, packed[f])
                packed[f] = pack_lanes(x, 64, q, packed[f])
        for f in range(g.F):
            my[f, rows, :] = packed_message(packed[f])
        for s, source in enumerate((ut, qt)):
            send_ends(g, s, lambda f, x: source[f, x, rows, :], rows, ma, mb)
        return carry

    lax.fori_loop(0, g.tiles, tile_step, 0)
    for copy in side_copies:
        copy.wait()
    for f in range(g.F):
        my[f, g.K :, :] = jnp.zeros((g.X + 8, 128), f32)
    if g.pair:
        other = 1 - lax.axis_index("gy")
        for f in range(g.F):
            my[f, g.K : g.K + g.X, : sn.shape[3]] = sn[other, f]
    span = parent.shape[2]
    lane = lax.broadcasted_iota(jnp.int32, (span, 128), 1)
    for f in range(g.F):
        total = jnp.zeros((span, 128), f32)
        for e in range(2):
            heights = jnp.broadcast_to(terrain[e : e + 1, :].astype(f32), (span, 128))
            for spot, values in ((e, parent[e, f]), (2 + e, heights)):
                here = (lane >= 4 * spot) & (lane < 4 * spot + 4)
                total = jnp.where(here, turn(values, 4 * spot + 2), total)
        my[f, g.K + g.X : g.K + g.X + span, :] = total


def fill_laps(g, source, rows, band, laps):
    for f in range(g.F):
        cells = source[f, :, rows, :]
        parts = along_lanes(cells.reshape(8 * g.X, 128), band)
        for x in range(g.X):
            ones = [cells[x + i] for i in (-1, 1) if 0 <= x + i < g.X]
            twos = [cells[x + i] for i in (-2, 2) if 0 <= x + i < g.X]
            total = parts[8 * x : 8 * x + 8] + 16.0 * functools.reduce(jnp.add, ones)
            total = total - functools.reduce(jnp.add, twos)
            laps[f, x] = total * (1.0 / 12.0)


def adjoint_inside_kernel(g, scaled, relax, mix, ps, qs, fy, out, rx, band, laps):
    beyond = BeyondLanes(g, 1, fy)
    width = relax[0]
    table = mix_table(mix, True)
    fill_band(band)
    if scaled:
        fill_ramp_x(g, width, rx)
        open_y = 1.0 - ramp_y(g, width)

    def tile_step(tile, carry):
        rows = rows_of(tile)
        fill_laps(g, qs, rows, band, laps)
        halo = [beyond.tile(f, rows) for f in range(g.F)]
        for x in range(g.X):
            p = [ps[f, x, rows, :] for f in range(g.F)]
            if scaled:
                open_xy = open_y * (1.0 - rx[x])
                p = [open_xy * value for value in p]
            for f in range(g.F):
                out[f, x, rows, :] = mixed(table, f, p) + laps[f, x] + beyond.column(x, halo[f])
        return carry

    lax.fori_loop(0, g.tiles, tile_step, 0)


def forward_inside_kernel(g, mix, ut, dt, *rest):
    *fy, out, band, laps = rest
    table = mix_table(mix, False)
    fill_band(band)
    beyond = BeyondLanes(g, 0, fy[0]) if fy else None

    def tile_step(tile, carry):
        rows = rows_of(tile)
        fill_laps(g, ut, rows, band, laps)
        if fy:
            halo = [beyond.tile(f, rows) for f in range(g.F)]
        for x in range(g.X):
            u = [ut[f, x, rows, :] for f in range(g.F)]
            d = dt[x, rows, :]
            for f in range(g.F):
                lap = laps[f, x]
                if fy:
                    lap = lap + beyond.column(x, halo[f])
                out[f, x, rows, :] = mixed(table, f, u) + d * lap
        return carry

    lax.fori_loop(0, g.tiles, tile_step, 0)


def adjoint_first_kernel(
    g, relax, inside, at, dt, fa, fb, p1, q1, ma, mb, my, dwe, dsn, rx
):
    width = relax[0]
    fill_ramp_x(g, width, rx)
    slope_y = ramp_y(g, width)
    open_y = 1.0 - slope_y
    beyond = Beyond(g, 1, fa, fb)

    def tile_step(tile, carry):
        rows = rows_of(tile)
        for f in range(g.F):
            packed = jnp.zeros((8, 128), f32)
            share = jnp.zeros((8, 128), f32)
            pushes = []
            for x in range(g.X):
                slope_x = rx[x]
                open_xy = open_y * (1.0 - slope_x)
                middle = plus(inside[f, x, rows, :], beyond.columns(f, x, rows))
                carried = at[f, x, rows, :] + middle
                share = share + slope_x * carried
                pushes.append(slope_y * carried)
                pulled = open_xy * middle
                q = dt[x, rows, :] * pulled
                p1[f, x, rows, :] = pulled
                q1[f, x, rows, :] = q
                packed = pack_lanes(x, 64, q, packed)
            my[f, rows, :] = packed_message(packed)
            dsn[f, rows, :] = lane_sums(pushes)
            dwe[f, rows, :] = open_y * share
        send_ends(g, 1, lambda f, x: q1[f, x, rows, :], rows, ma, mb)
        return carry

    lax.fori_loop(0, g.tiles, tile_step, 0)
    for f in range(g.F):
        my[f, g.K :, :] = jnp.zeros((g.X + 8, 128), f32)


def forward_first_kernel(
    g, relax, inside, dt, fa, fb, fy, sides, ma_in, mb_in, my_in, u1, ma, mb, my, rx
):
    width = relax[0]
    fill_ramp_x(g, width, rx)
    open_y = 1.0 - ramp_y(g, width)
    beyond = Beyond(g, 0, fa, fb)
    beyond_lanes = BeyondLanes(g, 0, fy)
    lane = lanes()

    def tile_step(tile, carry):
        rows = rows_of(tile)
        halo = [beyond_lanes.tile(f, rows) for f in range(g.F)]
        packed = [jnp.zeros((8, 128), f32) for _ in range(g.F)]
        for x in range(g.X):
            open_xy = open_y * (1.0 - rx[x])
            d = dt[x, rows, :]
            for f in range(g.F):
                lap = plus(beyond_lanes.column(x, halo[f]), beyond.columns(f, x, rows))
                stepped = inside[f, x, rows, :] + d * lap
                done = open_xy * stepped + sides[f, x, rows, :]
                u1[f, x, rows, :] = done
                packed[f] = pack_lanes(x, 0, done, packed[f])
        for f in range(g.F):
            my[f, rows, :] = jnp.where(lane < 64, packed_message(packed[f]), my_in[f, rows, :])
        send_ends(g, 0, lambda f, x: u1[f, x, rows, :], rows, ma, mb)
        return carry

    lax.fori_loop(0, g.tiles, tile_step, 0)


def adjoint_last_kernel(g, inside, fa, fb, fy, gsn_own, out_far, gsn, out, sems):
    pairs = ((out, out_far),)
    out2 = out.reshape(g.F * g.K * g.X, g.Y)
    beyond = Beyond(g, 1, fa, fb)

    def tile_step(tile, carry):
        rows = rows_of(tile)
        for f in range(g.F):
            for x in range(g.X):
                value = plus(inside[f, x, rows, :], beyond.columns(f, x, rows))
                strided(out2, g, f, tile, x)[...] = value
        for copy in level_copies(g, pairs, sems, tile):
            copy.start()
        return carry

    lax.fori_loop(0, g.tiles, tile_step, 0)
    if g.pair:
        here = lax.axis_index("gy")
        span = gsn.shape[3]
        for f in range(g.F):
            gsn[here, f] = gsn_own[f, :, :span]
            gsn[1 - here, f] = fy[f, g.K : g.K + g.X, :span]
    else:
        gsn[...] = jnp.zeros(gsn.shape, f32)
    for tile in range(g.tiles):
        for copy in level_copies(g, pairs, sems, tile):
            copy.wait()


def forward_last_kernel(
    g, relax, mix, inside, dt, fa, fb, sides, kept, swapped, out_far, mark, rx, lx, out, sems
):
    width = relax[0]
    mark[...] = jnp.zeros((8, 128), f32)
    for x in range(-2, g.X + 2):
        rx[x + 2] = ramp_x(g, width, x)
    for x in range(g.X):
        lap_x = near * (rx[x + 1] + rx[x + 3]) + far * (rx[x] + rx[x + 4]) - 5.0 * rx[x + 2]
        lx[x] = lap_x
    open_y = 1.0 - ramp_y(g, width)
    masks = lap_masks()
    table = mix_table(mix, False)
    beyond = Beyond(g, 0, fa, fb)
    edge, valid = border(), valid_lanes(g)
    pairs = ((out, out_far),)
    out2 = out.reshape(g.F * g.K * g.X, g.Y)

    def tile_step(tile, carry):
        rows = rows_of(tile)
        bound = [
            open_y * (kept[f, rows, :] + swapped[f, rows, :]) for f in range(g.F)
        ]
        past = packed_message(kept[g.F, rows, :] + swapped[g.F, rows, :]) * valid
        lap_y, mixed_bound = [], []
        for f in range(g.F):
            total = unpack_lanes(f, 0, past, edge)
            for shift, mask in masks:
                total = total + mask * turn(bound[f], shift)
            lap_y.append(total)
            mixed_bound.append(mixed(table, f, bound))
        for x in range(g.X):
            slope_x, lap_x = rx[x + 2], lx[x]
            open_xy = open_y * (1.0 - slope_x)
            d = dt[x, rows, :]
            along = slope_x * d
            across = lap_x * d
            for f in range(g.F):
                share = slope_x * mixed_bound[f] + along * lap_y[f] + across * bound[f]
                stepped = inside[f, x, rows, :] + share
                beside = beyond.columns(f, x, rows)
                if beside is not None:
                    stepped = stepped + d * beside
                done = open_xy * stepped + slope_x * bound[f] + sides[f, x, rows, :]
                strided(out2, g, f, tile, x)[...] = done
        for copy in level_copies(g, pairs, sems, tile):
            copy.start()
        return carry

    lax.fori_loop(0, g.tiles, tile_step, 0)
    for tile in range(g.tiles):
        for copy in level_copies(g, pairs, sems, tile):
            copy.wait()


def side_sums_kernel(g, dsn, tsn, my_in, gsn, my, wide):
    here = lax.axis_index("gy")
    shift = column_of(jnp.where(here == 0, tsn[0:1, :], tsn[1:2, :]))
    lane = lax.broadcasted_iota(jnp.int32, (g.X, 128), 1)
    batch = 128 // g.K
    for first in range(0, g.F, batch):
        some = range(first, min(first + batch, g.F))
        for f in some:
            wide[(f - first) * g.K : (f - first + 1) * g.K, :] = dsn[f]
        turned = wide[...].T[: g.X]
        for f in some:
            levels = jnp.where(lane < g.K, turn(turned, -(f - first) * g.K), 0.0)
            whole = shift_levels(levels, shift, 1)
            moved = turn(whole, 64)
            gsn[f] = jnp.where(here == 0, whole, moved)
            my[f, g.K : g.K + g.X, :] = jnp.where(here == 0, moved, whole)


def side_bounds_kernel(g, sn, fsn, tsn, bsn, wide):
    here = lax.axis_index("gy")
    shift = column_of(jnp.where(here == 0, tsn[0:1, :], tsn[1:2, :]))
    span = sn.shape[3]
    wide[...] = jnp.zeros(wide.shape, f32)
    for f in range(g.F):
        wide[f, : g.X, :span] = sn[here, f]
        mine = wide[f, : g.X, :]
        theirs = fsn[f, g.K : g.K + g.X, :]
        whole = jnp.where(here == 0, mine, theirs) + turn(
            jnp.where(here == 0, theirs, mine), 64
        )
        wide[f, : g.X, :] = shift_levels(whole, shift, -1)
        bsn[f] = wide[f].T[: g.K]


def side_spread_kernel(g, relax, bsn, out):
    slope_y = ramp_y(g, relax[0])

    def tile_step(tile, carry):
        rows = rows_of(tile)
        for f in range(g.F):
            bounds = bsn[f, rows, :]
            for x in range(g.X):
                out[f, x, rows, :] = slope_y * jnp.broadcast_to(bounds[:, x : x + 1], (8, 128))
        return carry

    lax.fori_loop(0, g.tiles, tile_step, 0)


def fold_rows(values, base, first, count):
    level = lax.broadcasted_iota(jnp.int32, (count, 128), 0) + base - first
    total = jnp.zeros((count, 128), f32)
    for j in range(values.shape[0]):
        row = jnp.broadcast_to(values[j : j + 1, :], (count, 128))
        total = jnp.where(level == j, row, total)
    return total


def fold_kernel(g, parent, terrain, fy, keep, send):
    here = lax.axis_index("gx")
    odd = here >= g.nx // 2
    span = parent.shape[2]
    first = here * span
    lane = lax.broadcasted_iota(jnp.int32, (span, 128), 1)
    top = g.K + g.X
    parts = []
    for e in range(2):
        part = [fold_rows(parent[e, f], terrain[e : e + 1, :], first, g.K) for f in range(g.F)]
        values = jnp.zeros((span, 128), f32)
        heights = jnp.zeros((span, 128), f32)
        for f in range(g.F):
            spots = (lane >= 4 * f) & (lane < 4 * f + 4)
            rows = fy[f, top : top + span, :]
            values = jnp.where(spots, turn(rows, 4 * f - 4 * e), values)
            heights = jnp.where(spots, turn(rows, 4 * f - 8 - 4 * e), heights)
        part.append(fold_rows(values, heights[0:1, :].astype(jnp.int32), first, g.K))
        parts.append(part)
    for i in range(g.F + 1):
        keep[i] = jnp.where(odd, parts[1][i], parts[0][i])
        send[i] = jnp.where(odd, parts[0][i], parts[1][i])


def join_kernel(g, sums, bounds, more_bounds, out):
    for f in range(g.F):
        out[f] = sums[f]
    for f in range(g.F + 1):
        out[g.F + f] = bounds[f] + more_bounds[f]


def split_kernel(g, state, moved, sums, bounds):
    for f in range(g.F):
        sums[f] = state[f] + moved[f]
    for f in range(g.F + 1):
        bounds[f] = state[g.F + f] + moved[g.F + f]


def add_kernel(g, first, second, out):
    out[...] = first[...] + second[...]


def spread_kernel(g, flip, sums, terrain, out):
    here = lax.axis_index("gx")
    pair = (here ^ flip) // 2
    count = out.shape[1]
    row = lax.broadcasted_iota(jnp.int32, (8, 128), 0)
    zero = jnp.zeros((8, 128), f32)
    base = jnp.where(here % 2 == 1, terrain[1:2, :], terrain[0:1, :])
    for block in range(count // 8):
        start = jnp.broadcast_to(pair * count + 8 * block - base, (8, 128)) + 8
        inside = (start > 0) & (start < g.K + 8)
        tile, rest = start >> 3, start & 7
        for f in range(g.F):
            chosen = sums[f]
            tiles = [zero] + [chosen[8 * i : 8 * i + 8] for i in range(g.tiles)] + [zero]
            low, high = zero, zero
            for i in range(g.tiles + 1):
                low = jnp.where(tile == i, tiles[i], low)
                high = jnp.where(tile == i, tiles[i + 1], high)
            for step in (4, 2, 1):
                moves = (rest & step) != 0
                up_low = pltpu.roll(low, 8 - step, 0)
                up_high = pltpu.roll(high, 8 - step, 0)
                low = jnp.where(moves, jnp.where(row < 8 - step, up_low, up_high), low)
                high = jnp.where(moves, up_high, high)
            out[f, 8 * block : 8 * block + 8, :] = jnp.where(inside, low, zero)


def halves_kernel(g, own, moved, kept, sent):
    odd = odd_column()
    span = kept.shape[1]
    for f in range(g.F):
        both = own[f] + moved[f]
        low, high = both[:span], both[span:]
        kept[f] = jnp.where(odd, high, low)
        sent[f] = jnp.where(odd, low, high)


def assemble_kernel(g, kept, other, out):
    odd = lax.axis_index("gx") % 2
    for f in range(g.F):
        out[odd, f] = kept[f]
        out[1 - odd, f] = other[f]


def call(kernel, outs, scratch, ins, time, aliases=None, after=(), far=False):
    count = len(ins)
    ins = ins + [("a", value) for value in after]

    def run(*refs):
        kernel(*refs[:count], *refs[len(ins) :])

    out_shape = [jax.ShapeDtypeStruct(s, f32) for s in outs]
    size = 4 * sum(functools.reduce(lambda a, b: a * b, s) for s in outs)
    return pl.pallas_call(
        run,
        out_shape=out_shape,
        in_specs=[places[where] for where, _ in ins],
        out_specs=[places["h" if far and i == 0 else "v"] for i in range(len(outs))],
        scratch_shapes=[pltpu.VMEM(s, f32) if isinstance(s, tuple) else s for s in scratch],
        input_output_aliases=aliases or {},
        compiler_params=pltpu.CompilerParams(vmem_limit_bytes=24 * 1024 * 1024),
        cost_estimate=pl.CostEstimate(flops=int(time * 1.1e9), bytes_accessed=2 * size, transcendentals=0),
    )(*[pltpu.with_memory_space_constraint(v, pltpu.HBM) if w == "h" else v for w, v in ins])


def body(
    child_state,
    cotangent,
    diffusivity,
    field_mix,
    parent_we,
    parent_sn,
    terrain_we,
    terrain_sn,
    relax_width,
):
    nx, ny = lax.axis_size("gx"), lax.axis_size("gy")
    g = Geometry(child_state.shape, nx, ny)
    F, K, X, Y = child_state.shape
    evens = [(i, i ^ 1) for i in range(nx)]
    odds = [(i, (((i + 1) ^ 1) - 1) % nx) for i in range(nx)]
    block = (F, X, K, 128)
    row_shape = (2, 2, F, K, 128)
    lane_shape = (F, g.tall, 128)
    edge_shape = (F, K, 128)
    ramps = (X, 8, 128)
    out_sems = pltpu.SemaphoreType.DMA((1, g.tiles))
    band = pltpu.VMEM((256, 128), jnp.bfloat16)
    laps = (F, X, 8, 128)

    def bind(kernel, *args):
        return functools.partial(kernel, g, *args)

    def swapped(values, distance):
        return lax.ppermute(values, "gx", [(i, i ^ distance) for i in range(nx)])

    def to_y(message):
        if g.pair:
            return lax.ppermute(message, "gy", [(0, 1), (1, 0)])
        up = lax.ppermute(message, "gy", [(i, i + 1) for i in range(ny - 1)])
        down = lax.ppermute(message, "gy", [(i + 1, i) for i in range(ny - 1)])
        low = (jnp.arange(128, dtype=jnp.int32) % 4 < 2)[None, None, :]
        rows = (jnp.arange(g.tall, dtype=jnp.int32) < K)[None, :, None]
        return jnp.where(low == rows, down, up)

    def add(first, second, after):
        (total,) = call(
            bind(add_kernel), [first.shape], [], [("v", first), ("v", second)], 0.1, after=after
        )
        return total

    sn_turned = jnp.swapaxes(parent_sn, 2, 3)
    ut, at, dt, qt, ma, mb, my = call(
        bind(pack_kernel),
        [block, block, (X, K, 128), block, row_shape, row_shape, lane_shape],
        [
            ramps,
            child_state.shape,
            child_state.shape,
            diffusivity.shape,
            sn_turned.shape,
            parent_we.shape,
            pltpu.VMEM(terrain_we.shape, jnp.int32),
            pltpu.SemaphoreType.DMA((3, g.tiles)),
            pltpu.SemaphoreType.DMA((3,)),
        ],
        [
            ("s", relax_width),
            ("h", child_state),
            ("h", cotangent),
            ("h", diffusivity),
            ("h", sn_turned),
            ("h", parent_we),
            ("h", terrain_we),
        ],
        3,
    )
    fy = to_y(my)
    fa = lax.ppermute(ma, "gx", evens)
    fb = lax.ppermute(mb, "gx", odds)

    (inside_u,) = call(
        bind(forward_inside_kernel),
        [block],
        [band, laps],
        [("s", field_mix), ("v", ut), ("v", dt)],
        2.5,
    )
    (inside_a,) = call(
        bind(adjoint_inside_kernel, True),
        [block],
        [ramps, band, laps],
        [("s", relax_width), ("s", field_mix), ("v", at), ("v", qt), ("v", fy)],
        2.5,
        after=[inside_u],
    )
    keep, send = call(
        bind(fold_kernel),
        [(F + 1, K, 128)] * 2,
        [],
        [("v", parent_we), ("v", terrain_we), ("v", fy)],
        0.3,
    )
    first_bounds = swapped(send, nx // 2)
    if g.pair:
        (bsn,) = call(
            bind(side_bounds_kernel),
            [edge_shape],
            [(F, 128, 128)],
            [("v", sn_turned), ("v", fy), ("v", terrain_sn)],
            0.7,
        )
    else:
        bsn = bound_sn_general(g, parent_sn, terrain_sn)
    (sides,) = call(
        bind(side_spread_kernel), [block], [], [("s", relax_width), ("v", bsn)], 0.7
    )

    p1, q1, ma, mb, my, dwe, dsn = call(
        bind(adjoint_first_kernel),
        [block, block, row_shape, row_shape, lane_shape, edge_shape, edge_shape],
        [ramps],
        [
            ("s", relax_width),
            ("v", inside_a),
            ("v", at),
            ("v", dt),
            ("v", fa),
            ("v", fb),
        ],
        3,
        after=[keep, sides],
    )
    (state,) = call(
        bind(join_kernel),
        [(2 * F + 1, K, 128)],
        [],
        [("v", dwe), ("v", keep), ("v", first_bounds)],
        0.1,
    )
    moved = swapped(state, 2)
    u1, ma, mb, my = call(
        bind(forward_first_kernel),
        [block, row_shape, row_shape, lane_shape],
        [ramps],
        [
            ("s", relax_width),
            ("v", inside_u),
            ("v", dt),
            ("v", fa),
            ("v", fb),
            ("v", fy),
            ("v", sides),
            ("v", ma),
            ("v", mb),
            ("v", my),
        ],
        2.5,
        {7: 1, 8: 2, 9: 3},
        after=[state],
    )
    if g.pair:
        gsn_own, my = call(
            bind(side_sums_kernel),
            [(F, X, 128), lane_shape],
            [(128, 128)],
            [("v", dsn), ("v", terrain_sn), ("v", my)],
            0.6,
            {2: 1},
        )
    else:
        gsn_own = dsn
    fy = to_y(my)
    fa = lax.ppermute(ma, "gx", evens)
    fb = lax.ppermute(mb, "gx", odds)

    state = add(state, moved, [gsn_own])
    distance = 4
    while distance < nx // 4:
        state = state + swapped(state, distance)
        distance *= 2
    moved = swapped(state, distance)
    (inside_a,) = call(
        bind(adjoint_inside_kernel, False),
        [block],
        [ramps, band, laps],
        [("s", relax_width), ("s", field_mix), ("v", p1), ("v", q1), ("v", fy)],
        2.5,
        after=[state],
    )
    (inside_u,) = call(
        bind(forward_inside_kernel),
        [block],
        [band, laps],
        [("s", field_mix), ("v", u1), ("v", dt), ("v", fy)],
        2.5,
        after=[inside_a],
    )
    sums, bounds = call(
        bind(split_kernel),
        [edge_shape, (F + 1, K, 128)],
        [],
        [("v", state), ("v", moved)],
        0.1,
        after=[inside_u],
    )
    other_bounds = swapped(bounds, 1)
    span = parent_we.shape[2]
    pair_shape = (F, 2 * span, 128)
    (gone,) = call(
        bind(spread_kernel, nx // 2), [pair_shape], [], [("v", sums), ("v", terrain_we)], 0.7
    )
    moved = swapped(gone, nx // 2)
    child_final, mark = call(
        bind(forward_last_kernel),
        [child_state.shape, (8, 128)],
        [(X + 4, 8, 128), ramps, child_state.shape, out_sems],
        [
            ("s", relax_width),
            ("s", field_mix),
            ("v", inside_u),
            ("v", dt),
            ("v", fa),
            ("v", fb),
            ("v", sides),
            ("v", bounds),
            ("v", other_bounds),
        ],
        3,
        far=True,
    )
    (own,) = call(
        bind(spread_kernel, 0),
        [pair_shape],
        [],
        [("v", sums), ("v", terrain_we)],
        0.7,
        after=[mark],
    )
    kept, sent = call(
        bind(halves_kernel), [(F, span, 128)] * 2, [], [("v", own), ("v", moved)], 0.1
    )
    other_kept = swapped(sent, 1)
    grad_state, grad_sn = call(
        bind(adjoint_last_kernel),
        [child_state.shape, sn_turned.shape],
        [child_state.shape, out_sems],
        [("v", inside_a), ("v", fa), ("v", fb), ("v", fy), ("v", gsn_own)],
        2.5,
        after=[kept],
        far=True,
    )
    (grad_we,) = call(
        bind(assemble_kernel),
        [parent_we.shape],
        [],
        [("v", kept), ("v", other_kept)],
        0.1,
    )
    if g.pair:
        grad_sn = jnp.swapaxes(grad_sn, 2, 3)
    else:
        grad_sn = grad_sn_general(g, gsn_own, terrain_sn, parent_sn.shape[2])
    return (child_final, grad_state, grad_we, grad_sn)


def level_weights(g, terrain, span):
    first = lax.axis_index("gy") * span
    base = terrain[:, None, :] + jnp.arange(g.K, dtype=jnp.int32)[None, :, None]
    parent = first + jnp.arange(span, dtype=jnp.int32)
    return (parent[None, None, :, None] == base[:, :, None, :]).astype(f32)


def bound_sn_general(g, parent_sn, terrain_sn):
    weights = level_weights(g, terrain_sn, parent_sn.shape[2])
    bound = jnp.einsum("eflc,eklc->efkc", parent_sn, weights, precision=highest)
    bound = lax.psum(bound, "gy")
    mine = jnp.where(lax.axis_index("gy") < g.ny // 2, bound[0], bound[1])
    return jnp.pad(mine, ((0, 0), (0, 0), (0, 128 - g.X)))


def grad_sn_general(g, sums, terrain_sn, span):
    sums = sums[:, :, : g.X]
    south = lax.axis_index("gy") < g.ny // 2
    zero = jnp.zeros_like(sums)
    both = jnp.stack([jnp.where(south, sums, zero), jnp.where(south, zero, sums)])
    both = lax.psum(both, "gy")
    weights = level_weights(g, terrain_sn, span)
    return jnp.einsum("efkc,eklc->eflc", both, weights, precision=highest)


def solution(mesh):
    return jax.shard_map(
        body,
        mesh=mesh,
        in_specs=(
            P(None, None, "gx", "gy"),
            P(None, None, "gx", "gy"),
            P(None, "gx", "gy"),
            P(),
            P(None, None, "gx", "gy"),
            P(None, None, "gy", "gx"),
            P(None, "gy"),
            P(None, "gx"),
            P(),
        ),
        out_specs=(
            P(None, None, "gx", "gy"),
            P(None, None, "gx", "gy"),
            P(None, None, "gx", "gy"),
            P(None, None, "gy", "gx"),
        ),
        check_vma=False,
    )
```
